32 devices in a mesh: dp: 4 (over x, core), seq: 8 (over z, y).
Axes of the slice: x: 2, y: 2, z: 4, core: 2. Of those that a mesh axis runs over, the one named last changes fastest.
Arguments:
- tokens: bfloat16 [4096, 512], P(('dp', 'seq')), may hold values from -6 to 6
- seg_start: int32 [4096], P(('dp', 'seq')), may hold values from 0 to 4032, as said below
- norm_one: float32 [512], replicated, may hold values from 0.5 to 1.5
- w_in: bfloat16 [512, 2048], replicated, may hold values from -0.25 to 0.25
- conv_w: float32 [4, 1024], replicated, may hold values from -3 to 3
- conv_b: float32 [1024], replicated, may hold values from -2.5 to 2.5
- w_xproj: bfloat16 [1024, 64], replicated, may hold values from -0.1875 to 0.1875
- w_dt: bfloat16 [32, 1024], replicated, may hold values from -2 to 2
- dt_bias: float32 [1024], replicated, may hold values from -13 to -3
- a_log: float32 [1024, 16], replicated, may hold values from 0 to 2
- d_skip: float32 [1024], replicated, may hold values from 0.5 to 1.5
- w_out: bfloat16 [1024, 512], replicated, may hold values from -0.75 to 0.75
- norm_two: float32 [512], replicated, may hold values from 0.5 to 1.5
- w_qkv: bfloat16 [512, 1536], replicated, may hold values from -0.25 to 0.25
- w_proj: bfloat16 [512, 512], replicated, may hold values from -1.5 to 1.5
- cotangent: bfloat16 [4096, 512], P(('dp', 'seq')), may hold values from -6 to 6
Outputs:
- out: bfloat16 [4096, 512], P(('dp', 'seq'))
- grad_tokens: float32 [4096, 512], P(('dp', 'seq'))
- grad_norm_one: float32 [512], replicated
- grad_w_in: float32 [512, 2048], replicated
- grad_conv_w: float32 [4, 1024], replicated
- grad_conv_b: float32 [1024], replicated
- grad_w_xproj: float32 [1024, 64], replicated
- grad_w_dt: float32 [32, 1024], replicated
- grad_dt_bias: float32 [1024], replicated
- grad_a_log: float32 [1024, 16], replicated
- grad_d_skip: float32 [1024], replicated
- grad_w_out: float32 [1024, 512], replicated
- grad_norm_two: float32 [512], replicated
- grad_w_qkv: float32 [512, 1536], replicated
- grad_w_proj: float32 [512, 512], replicated
The draws below stay inside these ranges and needn't reach their ends.
Inputs may be any that keep to these rules, and one draw needn't show every extreme that they name: seg_start[t] is the index of the first token of token t's sequence: never falling, at most t, equal to t at every start, and every batch group of 1024 tokens begins a sequence. Each group holds one to three sequences: a head of at most 64 tokens (possibly none), a main sequence that starts within the group's first 64 tokens and ends within its last 64 tokens, and a tail of at most 64 tokens (possibly none). The first group is one sequence of 1024 tokens; the last group's last sequence has exactly 64 tokens.
All inputs are finite; a program needn't handle non-finite values.
Results may differ from the reference program's by a relative error of at most 0.014.
The reference program's roundings to bfloat16 on the way count: a program that leaves them out, or rounds other values in their place, can miss the bound.
Values may be sent and summed in bfloat16 or wider, within the bound.
No kernel may reach another device: no remote copies, remote signals or barrier semaphores. Data moves between devices by JAX's collectives and lax.ppermute only.
A program may use at most 256 MiB of HBM per device.

```python
import jax
import jax.numpy as jnp
from jax import lax

D = 512
E = 1024
N = 16
R = 32
K = 4
H = 8
HD = 64
TOK_DEV = 128
GROUP = 1024
TOKENS = 4096
N_DP = 4


def draw_seg_start(key, part):
    key = jax.random.fold_in(key, 11)
    key_first, key_last = jax.random.split(key)
    groups = TOKENS // GROUP
    first_length = jax.random.randint(key_first, (groups, 1), 0, TOK_DEV // 2 + 1)
    last_length = jax.random.randint(key_last, (groups, 1), 0, TOK_DEV // 2 + 1)
    group_index = jnp.arange(groups, dtype=jnp.int32)[:, None]
    first_length = jnp.where(group_index == 0, 0, first_length)
    last_length = jnp.where(group_index == 0, 0, last_length)
    last_length = jnp.where(group_index == groups - 1, TOK_DEV // 2, last_length)
    inside = jnp.arange(GROUP, dtype=jnp.int32)[None, :]
    long_end = GROUP - last_length
    local_start = jnp.where(inside < first_length, 0, jnp.where(inside < long_end, first_length, long_end))
    offsets = (jnp.arange(groups, dtype=jnp.int32) * GROUP)[:, None]
    return (local_start + offsets).reshape(TOKENS).astype(jnp.int32)


def shard_levels(key, dims, pieces, smallest, top_value):
    level = 1.0
    for dim, blocks in pieces:
        draws = jax.random.uniform(jax.random.fold_in(jax.random.fold_in(key, 6), dim), (blocks,), jnp.float32, smallest / len(pieces), top_value / len(pieces))
        level = level * jnp.repeat(jnp.exp(draws), dims[dim] // blocks).reshape((-1,) + (1,) * (len(dims) - 1 - dim))
    return level


def bell_draw(key, shape, spread, most, pieces=(), kind=jnp.bfloat16):
    drawn = spread * jax.random.normal(key, shape, jnp.float32)
    if pieces:
        drawn = drawn * shard_levels(key, shape, pieces, -0.22, 0.18)
    return jnp.clip(drawn, -most, most).astype(kind)


def setup_inputs(seed: int = 0) -> dict:
    arg_keys = jax.random.split(jax.random.key(seed), 17)
    tokens = bell_draw(arg_keys[0], (TOKENS, D), 1.0, 6.0, ((0, 32),))
    seg_start = draw_seg_start(jax.random.fold_in(arg_keys[16], 71), 0)
    norm_one = jnp.clip(1.0 + 0.1 * jax.random.normal(arg_keys[2], (D,), jnp.float32), 0.5, 1.5)
    w_in = bell_draw(arg_keys[3], (D, 2 * E), D ** -0.5, 0.25)
    conv_w = bell_draw(arg_keys[4], (K, E), 0.5, 3.0, (), jnp.float32)
    conv_b = bell_draw(arg_keys[5], (E,), 0.3, 2.5, (), jnp.float32)
    w_xproj = bell_draw(arg_keys[6], (E, R + 2 * N), E ** -0.5, 0.1875)
    w_dt = bell_draw(arg_keys[7], (R, E), (R // 4) ** -0.5, 2.0)
    dt_bias = jnp.clip(jax.random.uniform(arg_keys[8], (E,), jnp.float32, -13.0, -3.0), -13.0, -3.0)
    a_log = jnp.clip(jax.random.uniform(arg_keys[9], (E, N), jnp.float32, 0.0, 2.0), 0.0, 2.0)
    d_skip = jnp.clip(jax.random.uniform(arg_keys[10], (E,), jnp.float32, 0.5, 1.5), 0.5, 1.5)
    w_out = bell_draw(arg_keys[11], (E, D), (E // 16) ** -0.5, 0.75)
    norm_two = jnp.clip(1.0 + 0.1 * jax.random.normal(arg_keys[12], (D,), jnp.float32), 0.5, 1.5)
    w_qkv = bell_draw(arg_keys[13], (D, 3 * D), D ** -0.5, 0.25)
    w_proj = bell_draw(arg_keys[14], (D, D), (D // 32) ** -0.5, 1.5)
    cotangent = bell_draw(arg_keys[15], (TOKENS, D), 1.0, 6.0, ((0, 32),))
    return {"tokens": tokens, "seg_start": seg_start, "norm_one": norm_one, "w_in": w_in, "conv_w": conv_w, "conv_b": conv_b, "w_xproj": w_xproj, "w_dt": w_dt, "dt_bias": dt_bias, "a_log": a_log, "d_skip": d_skip, "w_out": w_out, "norm_two": norm_two, "w_qkv": w_qkv, "w_proj": w_proj, "cotangent": cotangent}


@jax.custom_vjp
def low(v):
    return lax.optimization_barrier(v.astype(jnp.bfloat16)).astype(jnp.float32)

@jax.custom_vjp
def low_back(v):
    return v

def low_keep(v):
    return (low(v), None)

def low_pass(kept, grad):
    return (grad,)

def back_keep(v):
    return (v, None)

def back_low(kept, grad):
    return (low(grad),)
low.defvjp(low_keep, low_pass)
low_back.defvjp(back_keep, back_low)
epsilon = 1e-05
highest = lax.Precision.HIGHEST

def product(left, right):
    return jnp.dot(left, right, precision=highest, preferred_element_type=jnp.float32)

def rms_scale(values, gain):
    return values * lax.rsqrt(lax.optimization_barrier(jnp.mean(values * values, axis=-1, keepdims=True)) + epsilon) * gain

def combine_linear(earlier, later):
    return (earlier[0] * later[0], later[0] * earlier[1] + later[1])

def causal_conv(padded, starts, places, conv_weight, conv_bias):
    row_total = starts.shape[0]
    taps = conv_weight.shape[0]
    result = conv_bias + jnp.zeros((row_total, padded.shape[1]), padded.dtype)
    for offset in range(taps):
        source = places - (taps - 1) + offset
        usable = (source >= starts).astype(padded.dtype)[:, None]
        result = result + conv_weight[offset] * padded[offset:offset + row_total] * usable
    return result

def layer_group(hidden, starts, places, parameters):
    norm_one, w_in, conv_w, conv_b, w_xproj, w_dt, dt_bias, a_log, d_skip, w_out, norm_two, w_qkv, w_proj = parameters
    blocks = GROUP // TOK_DEV

    def blocked(values):
        return values.reshape((blocks, TOK_DEV) + values.shape[1:])
    normed = low(rms_scale(hidden, norm_one))
    projected = low(low_back(product(normed, w_in)))
    inner_rows = projected[:, :E]
    gate_rows = projected[:, E:]
    padded = jnp.concatenate([jnp.zeros((K - 1, E), jnp.float32), inner_rows], axis=0)
    mixed = low(jax.nn.silu(causal_conv(padded, starts, places, conv_w, conv_b)))
    selector = low_back(product(mixed, w_xproj))
    step_low = low(selector[:, :R])
    input_proj = selector[:, R:R + N]
    output_proj = selector[:, R + N:]
    step_size = jax.nn.softplus(low_back(product(step_low, w_dt)) + dt_bias)
    keep_state = (places != starts).astype(jnp.float32)
    a_hat = -jnp.exp(a_log)

    def scan_block(carried, block):
        step_blk, mixed_blk, in_blk, out_blk, keep_blk = block
        decays = jnp.exp(step_blk[:, :, None] * a_hat[None]) * keep_blk[:, None, None]
        driven = (step_blk * mixed_blk)[:, :, None] * in_blk[:, None, :]
        cum_decay, local_states = lax.associative_scan(combine_linear, (decays, driven))
        states = local_states + cum_decay * carried[None]
        return (states[-1], lax.optimization_barrier(jnp.sum(states * out_blk[:, None, :], axis=2)))
    initial = jnp.zeros((E, N), jnp.float32)
    final_state, read_out = lax.scan(jax.checkpoint(scan_block), initial, (blocked(step_size), blocked(mixed), blocked(input_proj), blocked(output_proj), blocked(keep_state)))
    ssm_out = read_out.reshape(GROUP, E) + d_skip * mixed
    gated = low(ssm_out * jax.nn.silu(gate_rows))
    after_mamba = hidden + low_back(product(gated, w_out))
    normed_two = low(rms_scale(after_mamba, norm_two))
    qkv_rows = low(low_back(product(normed_two, w_qkv)))
    queries = qkv_rows[:, :D].reshape(GROUP, H, HD)
    keys_all = qkv_rows[:, D:2 * D].reshape(GROUP, H, HD)
    values_all = qkv_rows[:, 2 * D:].reshape(GROUP, H, HD)

    def attend(block):
        query_blk, place_blk, start_blk = block
        scores = low_back(HD ** (-0.5) * jnp.einsum('qhd,khd->hqk', query_blk, keys_all, precision=highest))
        visible = (places[None, :] <= place_blk[:, None]) & (places[None, :] >= start_blk[:, None])
        scores = jnp.where(visible[None], scores, -1e+30)
        largest = lax.optimization_barrier(jnp.max(scores, axis=2, keepdims=True))
        exponent = jnp.exp(scores - largest)
        attention_probs = exponent / lax.optimization_barrier(jnp.sum(exponent, axis=2, keepdims=True))
        return jnp.einsum('hqk,khd->qhd', low(attention_probs), values_all, precision=highest).reshape(TOK_DEV, D)
    attended = lax.map(jax.checkpoint(attend), (blocked(queries), blocked(places), blocked(starts)))
    attended = low(low_back(attended.reshape(GROUP, D)))
    return after_mamba + low_back(product(attended, w_proj))

def reference(tokens, seg_start, norm_one, w_in, conv_w, conv_b, w_xproj, w_dt, dt_bias, a_log, d_skip, w_out, norm_two, w_qkv, w_proj, cotangent):
    places = jnp.arange(TOKENS, dtype=jnp.int32).reshape(N_DP, GROUP)
    starts = seg_start.astype(jnp.int32).reshape(N_DP, GROUP)
    parameters = tuple((element.astype(jnp.float32) for element in (norm_one, w_in, conv_w, conv_b, w_xproj, w_dt, dt_bias, a_log, d_skip, w_out, norm_two, w_qkv, w_proj)))

    def forward(hidden, *weights):

        def one_group(element):
            return layer_group(element[0], element[1], element[2], weights)
        return lax.map(jax.checkpoint(one_group), (hidden.reshape(N_DP, GROUP, D), starts, places)).reshape(TOKENS, D)
    result, pullback = jax.vjp(forward, tokens.astype(jnp.float32), *parameters)
    grads = pullback(cotangent.astype(jnp.float32))
    return (result.astype(jnp.bfloat16), grads[0], grads[1], grads[2], grads[3], grads[4], grads[5], grads[6], grads[7], grads[8], grads[9], grads[10], grads[11], grads[12], grads[13])
```

```python
import functools

import jax
import jax.numpy as jnp
from jax import lax
from jax.experimental import pallas as pl
from jax.experimental.pallas import tpu as pltpu
from jax.sharding import PartitionSpec as P

H = 8
HD = 64
LANES = 128
HALO = 16
SMALL = 128
RESET = 1e30
EPSILON = 1e-05
LOG2E = 1.4426950408889634
LN2 = 0.6931471805599453
BF = jnp.bfloat16
F32 = jnp.float32
VMEM_LIMIT = 48 * 1024 * 1024


def dot(a, b):
    return jnp.dot(a, b, preferred_element_type=F32)


def dot_nt(a, b):
    return lax.dot_general(a, b, (((1,), (1,)), ((), ())), preferred_element_type=F32)


def dot_tn(a, b):
    return lax.dot_general(a, b, (((0,), (0,)), ((), ())), preferred_element_type=F32)


def tile(j):
    return slice(j * LANES, (j + 1) * LANES)


def softplus(x):
    u = jnp.exp(-jnp.abs(x))
    series = u * (1.0 - u * (0.5 - u * (1.0 / 3.0 - u * 0.25)))
    return jnp.maximum(x, 0.0) + jnp.where(u < 0.015, series, jnp.log(1.0 + u))


def rms_parts(x):
    return lax.rsqrt(jnp.mean(x * x, axis=-1, keepdims=True) + EPSILON)


def rms_back(x, gain, grad):
    r = rms_parts(x)
    scaled = grad * gain
    inner = jnp.mean(x * scaled, axis=-1, keepdims=True)
    return r * scaled - x * (r * r * r * inner), grad * x * r


def to_rows(ref, j, value):
    ref[pl.ds(j, value.shape[0], stride=8), :] = value


def from_rows(ref, j, count):
    return ref[pl.ds(j, count, stride=8), :]


def block(ref, t):
    return ref[pl.ds(pl.multiple_of(t * 8, 8), 8), :]


def offsets_in_sequence(seg_ref, seq_size):
    count = seg_ref.shape[1]
    base = (lax.axis_index("dp") * seq_size + lax.axis_index("seq")) * count
    places = base + lax.broadcasted_iota(jnp.int32, (1, count), 1)
    row = (places - seg_ref[...]).astype(F32)
    return jnp.transpose(jnp.broadcast_to(row, (LANES, count)))


def conv_tile(ext_ref, w_ref, b_ref, offset, j, count):
    taps = w_ref.shape[0]
    pre = jnp.broadcast_to(b_ref[:, tile(j)], (count, LANES))
    for k in range(taps):
        rows = ext_ref[pl.ds(HALO - taps + 1 + k, count), tile(j)]
        pre = pre + jnp.where(offset >= taps - 1 - k, w_ref[k : k + 1, tile(j)] * rows, 0.0)
    return pre


def forward_kernel(
    seq_size, tok, halo, cot, n1, w_in, conv_w, conv_b, w_xp, w_dt, dtb, a_log, seg,
    o_msg, o_nc, o_inner, o_gate, o_mixed, o_bc, o_low, o_pre, o_s, o_dx, o_a,
    ext, smem, sem,
):
    count, width = tok.shape
    states = a_log.shape[0]
    inner_width = conv_w.shape[1]
    tiles = inner_width // LANES
    rank = w_dt.shape[0]
    x = jnp.concatenate([halo[...], tok[...]], axis=0).astype(F32)
    normed = (x * rms_parts(x) * n1[...]).astype(BF)
    o_nc[:, :width] = normed[HALO:]
    o_nc[:, width:] = cot[...]
    inner = dot(normed, w_in[:, :inner_width]).astype(BF)
    o_inner[...] = inner
    ext[...] = inner.astype(F32)
    o_gate[...] = dot(normed[HALO:], w_in[:, inner_width:]).astype(BF)
    offset = offsets_in_sequence(seg, seq_size)
    for j in range(tiles):
        pre = conv_tile(ext, conv_w, conv_b, offset, j, count)
        o_mixed[:, tile(j)] = (pre * jax.nn.sigmoid(pre)).astype(BF)
    selector = dot(o_mixed[...], w_xp[...])
    low = selector[:, :rank].astype(BF)
    o_low[...] = low
    o_bc[...] = selector[:, rank:]
    copy = pltpu.make_async_copy(o_bc, smem, sem)
    copy.start()
    o_pre[...] = dot(low, w_dt[...]) + dtb[...]
    for j in range(tiles):
        step = softplus(o_pre[:, tile(j)])
        to_rows(o_s, j, jnp.where(offset == 0.0, RESET, step))
        to_rows(o_dx, j, step * o_mixed[:, tile(j)].astype(F32))
        to_rows(o_a, j, -LOG2E * jnp.exp(a_log[:, tile(j)]))
    copy.wait()

    def one(t, carry):
        total, state = carry
        s, dx = block(o_s, t), block(o_dx, t)
        return total + s, tuple(
            jnp.exp2(s * block(o_a, n)) * state[n] + dx * smem[t, n] for n in range(states)
        )

    zero = jnp.zeros((8, LANES), F32)
    total, state = lax.fori_loop(0, count, one, (zero, (zero,) * states), unroll=4)
    high = total.astype(BF).astype(F32)
    seg_local = (seg[...] - lax.axis_index("dp") * (seq_size * count)).astype(F32)
    seg_high = jnp.floor(seg_local * (1.0 / 64.0))
    last = jnp.concatenate([seg_high, seg_local - 64.0 * seg_high, jnp.zeros((14, LANES), F32)], axis=0)
    blocks = [jnp.concatenate([state[n], state[n + 1]], axis=0) for n in range(0, states, 2)]
    blocks += [jnp.concatenate([high, total - high], axis=0), last]
    for i, value in enumerate(blocks):
        value = value.astype(BF)
        for d in range(seq_size):
            o_msg[d, 16 * i : 16 * i + 16, :] = value


def total_step(msg, d, states):
    rows = msg[d, states * 8 : states * 8 + 16, :].astype(F32)
    return rows[:8] + rows[8:]


def state_rows(msg, d, n):
    rows = msg[d, 16 * (n // 2) : 16 * (n // 2) + 16, :].astype(F32)
    return rows[:8] if n % 2 == 0 else rows[8:]


def middle_kernel(
    msg, s_ref, dx_ref, bc, a_ref, mixed, gate, d_skip, tok, w_out, n2, w_qkv, cot, w_proj,
    o_qkvg, o_start, o_ssm, o_gn, o_after,
    y_ref, smem, sem,
):
    count, inner_width = mixed.shape
    width = tok.shape[1]
    tiles = inner_width // LANES
    states = a_ref.shape[0] // 8
    copy = pltpu.make_async_copy(bc, smem, sem)
    copy.start()
    zero = jnp.zeros((8, LANES), F32)

    def join(d, carry):
        total = total_step(msg, d, states)
        return tuple(
            jnp.exp2(block(a_ref, n) * total) * carry[n] + state_rows(msg, d, n)
            for n in range(states)
        )

    start = lax.fori_loop(0, lax.axis_index("seq"), join, (zero,) * states)
    for n in range(states):
        o_start[8 * n : 8 * n + 8, :] = start[n]
    copy.wait()

    def one(t, state):
        s, dx = block(s_ref, t), block(dx_ref, t)
        state = tuple(
            jnp.exp2(s * block(a_ref, n)) * state[n] + dx * smem[t, n] for n in range(states)
        )
        parts = [state[n] * smem[t, states + n] for n in range(states)]
        while len(parts) > 1:
            parts = [a + b for a, b in zip(parts[::2], parts[1::2])]
        y_ref[pl.ds(pl.multiple_of(t * 8, 8), 8), :] = parts[0]
        return state

    lax.fori_loop(0, count, one, start, unroll=4)
    for j in range(tiles):
        ssm = from_rows(y_ref, j, count) + d_skip[:, tile(j)] * mixed[:, tile(j)].astype(F32)
        o_ssm[:, tile(j)] = ssm
        v = gate[:, tile(j)].astype(F32)
        o_gn[:, tile(j)] = (ssm * (v * jax.nn.sigmoid(v))).astype(BF)
    after = tok[...].astype(F32) + dot(o_gn[:, :inner_width], w_out[...])
    o_after[...] = after
    normed = (after * rms_parts(after) * n2[...]).astype(BF)
    o_gn[:, inner_width:] = normed
    qkv = dot(normed, w_qkv[...])
    gatt = dot_nt(cot[...], w_proj[...])
    copies = o_qkvg.shape[0] // H
    left = lax.broadcasted_iota(jnp.int32, (count, LANES), 1) < HD
    for p in range(H // 2):
        q, k, v = (qkv[:, i * width + p * LANES : i * width + (p + 1) * LANES] for i in range(3))
        g = gatt[:, tile(p)]
        first = (jnp.where(left, q, pltpu.roll(k, HD, 1)), jnp.where(left, v, pltpu.roll(g, HD, 1)))
        second = (jnp.where(left, pltpu.roll(q, HD, 1), k), jnp.where(left, pltpu.roll(v, HD, 1), g))
        for h, pair in ((2 * p, first), (2 * p + 1, second)):
            for i, value in enumerate(pair):
                value = value.astype(BF)
                for r in range(copies):
                    o_qkvg[h * copies + r, :, tile(i)] = value


def attention_kernel(qkvg, msg, o_back, qz, kr, gz, vr, dk, dv):
    seq_size, count = qkvg.shape[0], qkvg.shape[1]
    rows = seq_size * count
    starts_at = msg.shape[1] - 16
    left = lax.broadcasted_iota(jnp.int32, (count, LANES), 1) < HD
    for d in range(seq_size):
        at = slice(d * count, (d + 1) * count)
        a, b = qkvg[d, :, :LANES].astype(F32), qkvg[d, :, LANES:].astype(F32)
        qz[at, :] = jnp.where(left, a, 0.0).astype(BF)
        kr[at, :] = pltpu.roll(a, HD, 1).astype(BF)
        gz[at, :] = jnp.where(left, 0.0, b).astype(BF)
        vr[at, :] = pltpu.roll(b, HD, 1).astype(BF)
    dk[...] = jnp.zeros_like(dk)
    dv[...] = jnp.zeros_like(dv)
    scale = HD**-0.5

    def queries(b, length):
        at = pl.ds(b * count if isinstance(b, int) else pl.multiple_of(b * count, count), count)
        tail = msg[b, starts_at : starts_at + 16, :].astype(F32)
        starts = jnp.broadcast_to(tail[0:1] * 64.0 + tail[1:2], (LANES, LANES))
        first = jnp.transpose(starts)[:, :1].astype(jnp.int32)
        column = lax.broadcasted_iota(jnp.int32, (count, length), 1)
        row = b * count + lax.broadcasted_iota(jnp.int32, (count, 1), 0)
        visible = (column <= row) & (column >= first)
        scores = jnp.where(visible, dot_nt(qz[at, :], kr[:length, :]) * scale, -1e30)
        weight = jnp.exp(scores - jnp.max(scores, axis=1, keepdims=True))
        probs = weight * (1.0 / jnp.sum(weight, axis=1, keepdims=True))
        low = probs.astype(BF)
        grad_probs = dot_nt(gz[at, :], vr[:length, :])
        delta = jnp.sum(probs * grad_probs, axis=1, keepdims=True)
        grad_scores = (probs * (grad_probs - delta)).astype(BF)
        dk[:length, :] += dot_tn(grad_scores, kr[at, :])
        dv[:length, :] += dot_tn(low, vr[at, :])
        dq = dot(grad_scores, kr[:length, :])
        attended = dot(low, vr[:length, :])
        o_back[b, :, :LANES] = (dq * scale).astype(BF)
        o_back[b, :, LANES:] = attended.astype(BF)

    if seq_size <= 8:
        for b in range(seq_size):
            queries(b, (b + 1) * count)
    else:
        lax.fori_loop(0, seq_size, lambda b, _: (queries(b, rows), 0)[1], 0)
    for d in range(seq_size):
        at = slice(d * count, (d + 1) * count)
        o_back[d, :, :LANES] = jnp.where(left, o_back[d, :, :LANES].astype(F32), dk[at, :] * scale).astype(BF)
        o_back[d, :, LANES:] = jnp.where(left, dv[at, :], o_back[d, :, LANES:].astype(F32)).astype(BF)


def backward_kernel(
    back, after, cot, w_proj, w_qkv, n2, w_out, gate, ssm, s_ref, bc, a_ref,
    o_out, o_after, o_n2, o_gate, o_g, o_msg,
    turned, smem, sem,
):
    seq_size, count = back.shape[0], back.shape[1]
    width = after.shape[1]
    inner_width = gate.shape[1]
    tiles = inner_width // LANES
    states = a_ref.shape[0] // 8
    copies = seq_size // H
    copy = pltpu.make_async_copy(bc, smem, sem)
    copy.start()
    left = lax.broadcasted_iota(jnp.int32, (count, LANES), 1) < HD
    dq, dk, dv, att = [], [], [], []
    for p in range(H // 2):
        a0, b0 = (back[2 * p * copies, :, tile(i)].astype(F32) for i in range(2))
        a1, b1 = (back[(2 * p + 1) * copies, :, tile(i)].astype(F32) for i in range(2))
        dq.append(jnp.where(left, a0, pltpu.roll(a1, HD, 1)))
        dk.append(jnp.where(left, pltpu.roll(a0, HD, 1), a1))
        dv.append(jnp.where(left, b0, pltpu.roll(b1, HD, 1)))
        att.append(jnp.where(left, pltpu.roll(b0, HD, 1), b1))
    attended = jnp.concatenate(att, axis=1).astype(BF)
    o_out[...] = (after[...] + dot(attended, w_proj[...])).astype(BF)
    grad_qkv = jnp.concatenate(dq + dk + dv, axis=1).astype(BF)
    grad_x, grad_gain = rms_back(after[...], n2[...], dot_nt(grad_qkv, w_qkv[...]))
    o_n2[...] = jnp.sum(grad_gain, axis=0, keepdims=True)
    grad_after = cot[...].astype(F32) + grad_x
    o_after[...] = grad_after
    branch = grad_after.astype(BF)
    grad_gated = dot_nt(branch, w_out[...])
    gate_rows = inner_width // seq_size
    branch_rows = width // seq_size
    for j in range(tiles):
        v = gate[:, tile(j)].astype(F32)
        sig = jax.nn.sigmoid(v)
        grad = grad_gated[:, tile(j)]
        to_rows(o_g, j, grad * (v * sig))
        grad_gate = grad * ssm[:, tile(j)] * (sig * (1.0 + v * (1.0 - sig)))
        o_gate[:, tile(j)] = grad_gate.astype(BF)
        turned[tile(j), :] = jnp.transpose(grad_gate).astype(BF)
    for d in range(seq_size):
        o_msg[d, states * 8 : states * 8 + gate_rows, :] = turned[d * gate_rows : (d + 1) * gate_rows, :]
    for j in range(width // LANES):
        turned[tile(j), :] = jnp.transpose(grad_after[:, tile(j)]).astype(BF)
    for d in range(seq_size):
        o_msg[d, states * 8 + gate_rows :, :] = turned[d * branch_rows : (d + 1) * branch_rows, :]
    copy.wait()

    def one(i, later):
        t = count - 1 - i
        s, g = block(s_ref, t), block(o_g, t)
        return tuple(
            jnp.exp2(s * block(a_ref, n)) * (g * smem[t, states + n] + later[n])
            for n in range(states)
        )

    leaving = lax.fori_loop(0, count, one, (jnp.zeros((8, LANES), F32),) * states, unroll=4)
    for n in range(0, states, 2):
        value = jnp.concatenate([leaving[n], leaving[n + 1]], axis=0).astype(BF)
        for d in range(seq_size):
            o_msg[d, 8 * n : 8 * n + 16, :] = value


def fold8(values, sub):
    low4, low2, low1 = sub < 4, (sub & 2) == 0, (sub & 1) == 0
    four = []
    for k in range(4):
        a, b = values[k], values[k + 4]
        four.append(jnp.where(low4, a, b) + pltpu.roll(jnp.where(low4, b, a), 4, 0))
    two = []
    for k in range(2):
        a, b = four[k], four[k + 2]
        two.append(jnp.where(low2, a + pltpu.roll(a, 6, 0), b + pltpu.roll(b, 2, 0)))
    a, b = two
    return jnp.where(low1, a + pltpu.roll(a, 7, 0), b + pltpu.roll(b, 1, 0))


def adjoint_kernel(
    seq_size, back, msg, start, s_ref, dx_ref, g_ref, bc, a_ref, mixed, low, step_pre, inner, conv_w, conv_b, seg,
    w_dt, w_xp, d_skip, grad_gate, w_in, tok, halo, n1, grad_after, grad_n2,
    o_msg, o_tok, o_halo,
    held, gs_ref, ai_ref, sums, small, ext, gext, smem, sem,
):
    count, inner_width = mixed.shape
    width = tok.shape[1]
    tiles = inner_width // LANES
    states = a_ref.shape[0] // 8
    rank = w_dt.shape[0]
    taps = conv_w.shape[0]
    copy = pltpu.make_async_copy(bc, smem, sem)
    copy.start()
    zero = jnp.zeros((8, LANES), F32)
    for n in range(states):
        held[8 * n : 8 * n + 8, :] = start[8 * n : 8 * n + 8, :]
    copy.wait()

    def again(t, state):
        s, dx = block(s_ref, t), block(dx_ref, t)
        state = tuple(
            jnp.exp2(s * block(a_ref, n)) * state[n] + dx * smem[t, n] for n in range(states)
        )
        for n in range(states):
            held[pl.ds(pl.multiple_of(((t + 1) * states + n) * 8, 8), 8), :] = state[n]
        return state

    lax.fori_loop(0, count, again, tuple(start[8 * n : 8 * n + 8, :] for n in range(states)), unroll=2)

    def join(i, carry):
        d = seq_size - 1 - i
        total = total_step(msg, d, states)
        return tuple(
            jnp.exp2(block(a_ref, n) * total) * carry[n] + state_rows(back, d, n)
            for n in range(states)
        )

    leaving = lax.fori_loop(0, seq_size - 1 - lax.axis_index("seq"), join, (zero,) * states)
    sub = lax.broadcasted_iota(jnp.int32, (8, LANES), 0)

    def one(i, carry):
        later, grad_a = carry
        t = count - 1 - i
        s, dx, g = block(s_ref, t), block(dx_ref, t), block(g_ref, t)
        new_later, new_grad_a, with_b, with_c = [], [], [], []
        grad_step, adjoint_in = zero, zero
        for n in range(states):
            a = block(a_ref, n)
            adjoint = g * smem[t, states + n] + later[n]
            passed = jnp.exp2(s * a) * adjoint
            before = held[pl.ds(pl.multiple_of((t * states + n) * 8, 8), 8), :]
            now = held[pl.ds(pl.multiple_of(((t + 1) * states + n) * 8, 8), 8), :]
            grad_decay = passed * before
            grad_step = grad_step + grad_decay * a
            adjoint_in = adjoint_in + adjoint * smem[t, n]
            new_later.append(passed)
            new_grad_a.append(grad_a[n] + grad_decay * s)
            with_b.append(adjoint * dx)
            with_c.append(g * now)
        here = pl.ds(pl.multiple_of(t * 8, 8), 8)
        gs_ref[here, :] = grad_step
        ai_ref[here, :] = adjoint_in
        for i, part in enumerate((with_b[:8], with_b[8:], with_c[:8], with_c[8:])):
            sums[pl.ds(pl.multiple_of(t * 32 + 8 * i, 8), 8), :] = fold8(part, sub)
        return tuple(new_later), tuple(new_grad_a)

    _, grad_a = lax.fori_loop(0, count, one, (leaving, (zero,) * states))
    small[...] = jnp.zeros_like(small)
    for n in range(states):
        small[(104 + n) * 8 : (105 + n) * 8, :] = grad_a[n] * (LN2 * block(a_ref, n))
    lane = lax.broadcasted_iota(jnp.int32, (count, rank + 2 * states), 1)
    grad_bc = jnp.zeros((count, rank + 2 * states), F32)
    for q in range(2 * states):
        total = jnp.sum(sums[pl.ds(q, count, stride=2 * states), :], axis=1, keepdims=True)
        grad_bc = jnp.where(lane == rank + q, total, grad_bc)
    offset = offsets_in_sequence(seg, seq_size)
    halves = []
    for j in range(tiles):
        mix = mixed[:, tile(j)].astype(F32)
        pre = step_pre[:, tile(j)]
        grad_step = LN2 * from_rows(gs_ref, j, count) + mix * from_rows(ai_ref, j, count)
        grad_pre = grad_step * jax.nn.sigmoid(pre)
        small[101 * 8 + j : 101 * 8 + j + 1, :] = jnp.sum(grad_pre, axis=0, keepdims=True)
        grad_ssm = from_rows(g_ref, j, count)
        small[102 * 8 + j : 102 * 8 + j + 1, :] = jnp.sum(grad_ssm * mix, axis=0, keepdims=True)
        halves.append(grad_pre.astype(BF))
    half = jnp.concatenate(halves, axis=1)
    grad_w_dt = dot_tn(low[...], half)
    padded_dt = jnp.concatenate([w_dt[...], jnp.zeros((2 * states, inner_width), BF)], axis=0)
    grad_selector = (dot_nt(half, padded_dt) + grad_bc).astype(BF)
    grad_w_xp = dot_tn(grad_selector, mixed[...])
    from_selector = dot_nt(grad_selector, w_xp[...])
    ext[...] = inner[...].astype(F32)
    gext[...] = jnp.zeros_like(gext)
    for j in range(tiles):
        to_rows(small.at[pl.ds(0, 64 * 8)], j, grad_w_xp[:, tile(j)])
        to_rows(small.at[pl.ds(64 * 8, 32 * 8)], j, grad_w_dt[:, tile(j)])
        pre = conv_tile(ext, conv_w, conv_b, offset, j, count)
        sig = jax.nn.sigmoid(pre)
        grad_mixed = (
            softplus(step_pre[:, tile(j)]) * from_rows(ai_ref, j, count)
            + from_rows(g_ref, j, count) * d_skip[:, tile(j)]
            + from_selector[:, tile(j)]
        )
        grad_pre = grad_mixed * (sig * (1.0 + pre * (1.0 - sig)))
        small[100 * 8 + j : 100 * 8 + j + 1, :] = jnp.sum(grad_pre, axis=0, keepdims=True)
        for k in range(taps):
            shifted = pl.ds(HALO - taps + 1 + k, count)
            usable = jnp.where(offset >= taps - 1 - k, grad_pre, 0.0)
            row = (96 + k) * 8 + j
            small[row : row + 1, :] = jnp.sum(usable * ext[shifted, tile(j)], axis=0, keepdims=True)
            gext[shifted, tile(j)] += conv_w[k : k + 1, tile(j)] * usable
    piece = inner_width // seq_size
    per = small.shape[0] // seq_size
    grad_inner = gext[...].astype(BF)
    for j in range(tiles):
        value = jnp.transpose(gext[HALO:, tile(j)]).astype(BF)
        for i in range(LANES // piece):
            o_msg[j * (LANES // piece) + i, :piece, :] = value[i * piece : (i + 1) * piece]
    for d in range(seq_size):
        rows = gext[:HALO, d * piece : (d + 1) * piece]
        if piece < LANES:
            rows = jnp.concatenate([rows, jnp.zeros((HALO, LANES - piece), F32)], axis=1)
        o_msg[d, piece : piece + HALO, :] = rows.astype(BF)
    grad_normed = dot_nt(grad_inner, w_in[:, :inner_width])
    own = dot_nt(grad_gate[...], w_in[:, inner_width:])
    grad_normed = jnp.concatenate([grad_normed[:HALO], grad_normed[HALO:] + own], axis=0)
    x = jnp.concatenate([halo[...], tok[...]], axis=0).astype(F32)
    grad_x, grad_gain = rms_back(x, n1[...], grad_normed)
    o_tok[...] = grad_after[...] + grad_x[HALO:]
    o_halo[...] = grad_x[HALO - 8 : HALO]
    grad_gain = jnp.sum(grad_gain, axis=0, keepdims=True)
    for j in range(width // LANES):
        small[103 * 8 + j : 103 * 8 + j + 1, :] = grad_gain[:, tile(j)]
        small[103 * 8 + 4 + j : 103 * 8 + 5 + j, :] = grad_n2[:, tile(j)]
    for d in range(seq_size):
        o_msg[d, piece + HALO :, :] = small[d * per : (d + 1) * per, :].astype(BF)


def early_products_kernel(width, back, nc, gn, adj, o_head, o_gate, o_out):
    seq_size, count = back.shape[0], back.shape[1]
    rows = seq_size * count
    inner_width = gn.shape[1] - width
    gate_rows, branch_rows = o_gate.shape[0], o_out.shape[0]
    at = adj.shape[1] - gate_rows - branch_rows
    both = back[...].reshape(rows, 2 * LANES)
    first = dot_tn(both[:, :LANES], gn[:, inner_width:])
    second = dot_tn(both[:, LANES:], gn[:, inner_width:])
    third = dot_tn(both[:, LANES:], nc[:, width:])
    o_head[:HD, :] = third[HD:].astype(BF)
    o_head[HD : 3 * HD, :] = first.astype(BF)
    o_head[3 * HD :, :] = second[:HD].astype(BF)
    gate = jnp.zeros((gate_rows, width), F32)
    out = jnp.zeros((branch_rows, inner_width), F32)
    for d in range(seq_size):
        src = slice(d * count, (d + 1) * count)
        gate = gate + dot(adj[d, at : at + gate_rows, :], nc[src, :width])
        out = out + dot(adj[d, at + gate_rows :, :], gn[src, :inner_width])
    o_gate[...] = gate.astype(BF)
    o_out[...] = out.astype(BF)


def late_products_kernel(width, tail, nc, o_in, o_small):
    seq_size = tail.shape[0]
    count = nc.shape[0] // seq_size
    piece = o_in.shape[0]
    grad = jnp.zeros((piece, width), F32)
    small = jnp.zeros(o_small.shape, F32)
    for d in range(seq_size):
        grad = grad + dot(tail[d, :piece, :], nc[d * count : (d + 1) * count, :width])
        small = small + tail[d, piece + HALO :, :].astype(F32)
        if d:
            borrowed = dot_tn(tail[d, piece : piece + HALO, :], nc[d * count - HALO : d * count, :width])
            grad = grad + borrowed[:piece]
    o_in[...] = grad.astype(BF)
    o_small[...] = small.astype(BF)


def call(kernel, outs, scratch, *args, name=None):
    return pl.pallas_call(
        kernel,
        out_shape=[jax.ShapeDtypeStruct(s, d) for s, d in outs],
        scratch_shapes=scratch,
        compiler_params=pltpu.CompilerParams(vmem_limit_bytes=VMEM_LIMIT),
        name=name,
    )(*args)


def exchange(value, axes):
    return lax.all_to_all(value, axes, 0, 0, tiled=True)


def everywhere(value):
    axes = ("dp", "seq")
    count = lax.axis_size(axes)
    return exchange(jnp.broadcast_to(value[None], (count,) + value.shape), axes)


def body(
    tokens, seg_start, norm_one, w_in, conv_w, conv_b, w_xproj, w_dt, dt_bias, a_log, d_skip,
    w_out, norm_two, w_qkv, w_proj, cotangent,
):
    count, width = tokens.shape
    inner_width = w_in.shape[1] // 2
    states = a_log.shape[1]
    rank = w_dt.shape[0]
    groups, seq_size = lax.axis_size("dp"), lax.axis_size("seq")
    rows = count * seq_size
    ext_rows = HALO + count
    piece = inner_width // seq_size
    branch = width // seq_size
    copies = seq_size // H
    line = lambda v: v.reshape(1, -1)
    seg = line(seg_start)
    n1, n2, cb, dtb, skip = (line(v) for v in (norm_one, norm_two, conv_b, dt_bias, d_skip))
    vmem, smem = pltpu.VMEM, pltpu.SMEM((count, 2 * states), F32)
    sem = pltpu.SemaphoreType.DMA
    blocks = ((count * 8, LANES), F32)
    onward = [(i, i + 1) for i in range(seq_size - 1)]
    halo = lax.ppermute(tokens[count - HALO :], "seq", onward)
    msg, nc, inner, gate, mixed, bc, low, step_pre, s, dx, a = call(
        functools.partial(forward_kernel, seq_size),
        [
            ((seq_size, states * 8 + 32, LANES), BF), ((count, 2 * width), BF), ((ext_rows, inner_width), BF),
            ((count, inner_width), BF), ((count, inner_width), BF), ((count, 2 * states), F32), ((count, rank), BF),
            ((count, inner_width), F32), blocks, blocks, ((states * 8, LANES), F32),
        ],
        [vmem((ext_rows, inner_width), F32), smem, sem],
        tokens, halo, cotangent, n1, w_in, conv_w, cb, w_xproj, w_dt, dtb, a_log.T, seg,
        name="forward",
    )
    nc_all = lax.all_gather(nc, "seq", axis=0, tiled=True)
    msg = exchange(msg, "seq")
    qkvg, start, ssm, gn, after = call(
        middle_kernel,
        [
            ((seq_size, count, 2 * LANES), BF), ((states * 8, LANES), F32), ((count, inner_width), F32),
            ((count, inner_width + width), BF), ((count, width), F32),
        ],
        [vmem(*blocks), smem, sem],
        msg, s, dx, bc, a, mixed, gate, skip, tokens, w_out, n2, w_qkv, cotangent, w_proj,
        name="middle",
    )
    gn_all = lax.all_gather(gn, "seq", axis=0, tiled=True)
    qkvg = exchange(qkvg, "seq")
    (back,) = call(
        attention_kernel,
        [((seq_size, count, 2 * LANES), BF)],
        [vmem((rows, LANES), BF)] * 4 + [vmem((rows, LANES), F32)] * 2,
        qkvg, msg, name="attention",
    )
    back_own = exchange(back, "seq")
    out, grad_after, grad_n2, grad_gate, g, adj = call(
        backward_kernel,
        [
            ((count, width), BF), ((count, width), F32), ((1, width), F32), ((count, inner_width), BF), blocks,
            ((seq_size, states * 8 + piece + branch, LANES), BF),
        ],
        [vmem((inner_width, LANES), BF), smem, sem],
        back_own, after, cotangent, w_proj, w_qkv, n2, w_out, gate, ssm, s, bc, a,
        name="backward",
    )
    adj = exchange(adj, "seq")
    head, gate_part, out_part = call(
        functools.partial(early_products_kernel, width),
        [((4 * HD, width), BF), ((piece, width), BF), ((branch, inner_width), BF)],
        [],
        back, nc_all, gn_all, adj, name="early_products",
    )
    if copies > 1:
        own = 4 * HD // copies
        head = lax.dynamic_slice_in_dim(head, lax.axis_index("seq") % copies * own, own, 0)
    early = jnp.concatenate([v.reshape(groups, -1, LANES) for v in (head, gate_part, out_part)], axis=1)
    early = jnp.sum(exchange(early, "dp").astype(F32), axis=0).astype(BF)
    early = lax.all_gather(early, ("dp", "seq"))
    tail, grad_tokens, grad_halo = call(
        functools.partial(adjoint_kernel, seq_size),
        [
            ((seq_size, piece + HALO + SMALL * 8 // seq_size, LANES), BF), ((count, width), F32), ((8, width), F32),
        ],
        [
            vmem(((count + 1) * states * 8, LANES), F32), vmem(*blocks), vmem(*blocks),
            vmem((count * 2 * states, LANES), F32), vmem((SMALL * 8, LANES), F32),
            vmem((ext_rows, inner_width), F32), vmem((ext_rows, inner_width), F32), smem, sem,
        ],
        adj, msg, start, s, dx, g, bc, a, mixed, low, step_pre, inner, conv_w, cb, seg,
        w_dt, w_xproj, skip, grad_gate, w_in, tokens, halo, n1, grad_after, grad_n2,
        name="adjoint",
    )
    tail = exchange(tail, "seq")
    returned = lax.ppermute(grad_halo, "seq", [(i + 1, i) for i in range(seq_size - 1)])
    grad_tokens = grad_tokens.at[count - 8 :].add(returned)
    in_part, small = call(
        functools.partial(late_products_kernel, width),
        [((piece, width), BF), ((SMALL * 8 // seq_size, LANES), BF)],
        [],
        tail, nc_all, name="late_products",
    )
    late = jnp.concatenate([v.reshape(groups, -1, LANES) for v in (in_part, small)], axis=1)
    late = jnp.sum(exchange(late, "dp").astype(F32), axis=0).astype(BF)
    late = everywhere(late)

    def whole(gathered, first, last):
        part = gathered.reshape(groups, seq_size, -1, LANES)[:, :, first:last]
        return part.swapaxes(0, 1).reshape(seq_size, -1)

    def cut(sizes):
        ends, total = [], 0
        for n in sizes:
            ends.append((total, total + n // LANES // groups))
            total = ends[-1][1]
        return ends

    at_head, at_gate, at_out = cut((4 * HD * width // copies, piece * width, branch * inner_width))
    at_in, at_small = cut((piece * width, SMALL * 8 // seq_size * LANES))
    heads = whole(early, *at_head).reshape(H, 4, HD, width)
    grad_w_proj = heads[:, 0].reshape(H * HD, width).astype(F32)
    grad_w_qkv = heads[:, 1:].transpose(3, 1, 0, 2).reshape(width, 3 * width).astype(F32)
    grad_w_out = whole(early, *at_out).reshape(width, inner_width).T.astype(F32)
    grad_w_in = jnp.concatenate(
        [whole(late, *at_in).reshape(inner_width, width), whole(early, *at_gate).reshape(inner_width, width)], axis=0
    ).T.astype(F32)
    small = whole(late, *at_small).reshape(SMALL, inner_width).astype(F32)
    return (
        out,
        grad_tokens,
        small[103, :width],
        grad_w_in,
        small[96:100],
        small[100],
        small[:64].T,
        small[64:96],
        small[101],
        small[104:120].T,
        small[102],
        grad_w_out,
        small[103, width:],
        grad_w_qkv,
        grad_w_proj,
    )


def solution(mesh):
    split, copied = P(("dp", "seq"), None), P()
    return jax.shard_map(
        body,
        mesh=mesh,
        in_specs=(split, P(("dp", "seq"))) + (copied,) * 13 + (split,),
        out_specs=(split, split) + (copied,) * 13,
        check_vma=False,
    )
```

```python
import functools

import jax
import jax.numpy as jnp
import numpy as np
from jax import lax
from jax.experimental import pallas as pl
from jax.experimental.pallas import tpu as pltpu
from jax.sharding import PartitionSpec as P

H = 8
HD = 64
LANES = 128
HALO = 16
SMALL = 128
RESET = 1e30
EPSILON = 1e-05
LOG2E = 1.4426950408889634
LN2 = 0.6931471805599453
BF = jnp.bfloat16
F32 = jnp.float32


def dot(a, b):
    return jnp.dot(a, b, preferred_element_type=F32)


def dot_nt(a, b):
    return lax.dot_general(a, b, (((1,), (1,)), ((), ())), preferred_element_type=F32)


def dot_tn(a, b):
    return lax.dot_general(a, b, (((0,), (0,)), ((), ())), preferred_element_type=F32)


def tile(j):
    return slice(j * LANES, (j + 1) * LANES)


def softplus(x):
    u = jnp.exp(-jnp.abs(x))
    series = u * (1.0 - u * (0.5 - u * (1.0 / 3.0 - u * 0.25)))
    return jnp.maximum(x, 0.0) + jnp.where(u < 0.015, series, jnp.log(1.0 + u))


def rms_parts(x):
    return lax.rsqrt(jnp.mean(x * x, axis=-1, keepdims=True) + EPSILON)


def rms_back(x, gain, grad):
    r = rms_parts(x)
    scaled = grad * gain
    inner = jnp.mean(x * scaled, axis=-1, keepdims=True)
    return r * scaled - x * (r * r * r * inner), grad * x * r


def to_rows(ref, j, value):
    ref[pl.ds(j, value.shape[0], stride=8), :] = value


def from_rows(ref, j, count):
    return ref[pl.ds(j, count, stride=8), :]


def block(ref, t):
    return ref[pl.ds(pl.multiple_of(t * 8, 8), 8), :]


def offsets_in_sequence(seg_ref, seq_size):
    count = seg_ref.shape[1]
    base = (lax.axis_index("dp") * seq_size + lax.axis_index("seq")) * count
    places = base + lax.broadcasted_iota(jnp.int32, (1, count), 1)
    row = (places - seg_ref[...]).astype(F32)
    return jnp.transpose(jnp.broadcast_to(row, (LANES, count)))


def conv_tile(ext_ref, w_ref, b_ref, offset, j, count):
    taps = w_ref.shape[0]
    pre = jnp.broadcast_to(b_ref[:, tile(j)], (count, LANES))
    for k in range(taps):
        rows = ext_ref[pl.ds(HALO - taps + 1 + k, count), tile(j)]
        pre = pre + jnp.where(offset >= taps - 1 - k, w_ref[k : k + 1, tile(j)] * rows, 0.0)
    return pre


def forward_kernel(
    seq_size, tok, halo, n1, w_in, conv_w, conv_b, w_xp, w_dt, dtb, a_log, seg,
    o_msg, o_normed, o_inner, o_gate, o_mixed, o_bc, o_low, o_pre, o_s, o_dx, o_a,
    ext, smem, sem,
):
    tok, halo, n1, seg = ready(tok, halo, n1, seg)
    count = tok.shape[0]
    states = a_log.shape[0]
    inner_width = conv_w.shape[1]
    tiles = inner_width // LANES
    rank = w_dt.shape[0]
    x = jnp.concatenate([halo[...], tok[...]], axis=0).astype(F32)
    normed = (x * rms_parts(x) * n1[...]).astype(BF)
    o_normed[...] = normed[HALO:]
    sent(o_normed)
    w_in = ready(w_in)
    inner = dot(normed, w_in[:, :inner_width]).astype(BF)
    o_inner[...] = inner
    sent(o_inner)
    ext[...] = inner.astype(F32)
    o_gate[...] = dot(normed[HALO:], w_in[:, inner_width:]).astype(BF)
    sent(o_gate)
    conv_w, conv_b, w_xp, w_dt, dtb, a_log = ready(conv_w, conv_b, w_xp, w_dt, dtb, a_log)
    offset = offsets_in_sequence(seg, seq_size)
    for j in range(tiles):
        pre = conv_tile(ext, conv_w, conv_b, offset, j, count)
        o_mixed[:, tile(j)] = (pre * jax.nn.sigmoid(pre)).astype(BF)
    sent(o_mixed)
    selector = dot_nt(o_mixed[...], w_xp[...])
    low = selector[:, :rank].astype(BF)
    o_low[...] = low
    o_bc[...] = selector[:, rank:]
    sent(o_low, o_bc)
    copy = pltpu.make_async_copy(o_bc.ref, smem, sem)
    copy.start()
    o_pre[...] = dot(low, w_dt[...]) + dtb[...]
    sent(o_pre)
    for j in range(tiles):
        step = softplus(o_pre[:, tile(j)])
        to_rows(o_s, j, jnp.where(offset == 0.0, RESET, step))
        to_rows(o_dx, j, step * o_mixed[:, tile(j)].astype(F32))
        to_rows(o_a, j, -LOG2E * jnp.exp(a_log[:, tile(j)]))
    sent(o_s, o_dx, o_a)
    copy.wait()

    def one(t, carry):
        total, state = carry
        s, dx = block(o_s, t), block(o_dx, t)
        return total + s, tuple(
            jnp.exp2(s * block(o_a, n)) * state[n] + dx * smem[t, n] for n in range(states)
        )

    zero = jnp.zeros((8, LANES), F32)
    total, state = lax.fori_loop(0, count, one, (zero, (zero,) * states), unroll=4)
    high = total.astype(BF).astype(F32)
    seg_local = (seg[...] - lax.axis_index("dp") * (seq_size * count)).astype(F32)
    seg_high = jnp.floor(seg_local * (1.0 / 64.0))
    last = jnp.concatenate([seg_high, seg_local - 64.0 * seg_high, jnp.zeros((14, LANES), F32)], axis=0)
    blocks = [jnp.concatenate([state[n], state[n + 1]], axis=0) for n in range(0, states, 2)]
    blocks += [jnp.concatenate([high, total - high], axis=0), last]
    for i, value in enumerate(blocks):
        value = value.astype(BF)
        for d in range(seq_size):
            o_msg[d, 16 * i : 16 * i + 16, :] = value


def total_step(msg, d, states):
    rows = msg[d, states * 8 : states * 8 + 16, :].astype(F32)
    return rows[:8] + rows[8:]


def state_rows(msg, d, n):
    rows = msg[d, 16 * (n // 2) : 16 * (n // 2) + 16, :].astype(F32)
    return rows[:8] if n % 2 == 0 else rows[8:]


def middle_kernel(
    msg, a_ref, bc, s_ref, dx_ref, mixed, gate, d_skip, tok, w_out, n2, w_qkv, cot, w_proj, normed_one,
    o_qkvg, o_start, o_ssm, o_normed, o_after,
    gated, y_ref,
):
    msg, a_ref = ready(msg, a_ref)
    states = a_ref.shape[0] // 8
    zero = jnp.zeros((8, LANES), F32)

    def join(d, carry):
        total = total_step(msg, d, states)
        return tuple(
            jnp.exp2(block(a_ref, n) * total) * carry[n] + state_rows(msg, d, n)
            for n in range(states)
        )

    start = lax.fori_loop(0, lax.axis_index("seq"), join, (zero,) * states)
    for n in range(states):
        o_start[8 * n : 8 * n + 8, :] = start[n]
    sent(o_start)
    s_ref, dx_ref, smem = ready(s_ref, dx_ref, bc)
    count = smem.shape[0]

    def one(t, state):
        s, dx = block(s_ref, t), block(dx_ref, t)
        state = tuple(
            jnp.exp2(s * block(a_ref, n)) * state[n] + dx * smem[t, n] for n in range(states)
        )
        parts = [state[n] * smem[t, states + n] for n in range(states)]
        while len(parts) > 1:
            parts = [a + b for a, b in zip(parts[::2], parts[1::2])]
        y_ref[pl.ds(pl.multiple_of(t * 8, 8), 8), :] = parts[0]
        return state

    lax.fori_loop(0, count, one, start, unroll=4)
    mixed, gate, d_skip, tok, w_out, n2 = ready(mixed, gate, d_skip, tok, w_out, n2)
    inner_width, width = mixed.shape[1], tok.shape[1]
    tiles = inner_width // LANES
    for j in range(tiles):
        ssm = from_rows(y_ref, j, count) + d_skip[:, tile(j)] * mixed[:, tile(j)].astype(F32)
        o_ssm[:, tile(j)] = ssm
        v = gate[:, tile(j)].astype(F32)
        gated[:, tile(j)] = (ssm * (v * jax.nn.sigmoid(v))).astype(BF)
    sent(o_ssm)
    piece = inner_width // o_qkvg.shape[0]
    for d in range(o_qkvg.shape[0]):
        o_qkvg[d, :, 2 * LANES : 2 * LANES + piece] = gated[:, d * piece : (d + 1) * piece]
    after = tok[...].astype(F32) + dot(gated[...], w_out[...])
    o_after[...] = after
    sent(o_after)
    normed = (after * rms_parts(after) * n2[...]).astype(BF)
    normed_one, w_qkv, cot, w_proj = ready(normed_one, w_qkv, cot, w_proj)
    o_normed[:, :width] = normed_one[...]
    o_normed[:, width:] = normed
    sent(o_normed)
    qkv = dot(normed, w_qkv[...])
    gatt = dot_nt(cot[...], w_proj[...])
    copies = o_qkvg.shape[0] // H
    left = lax.broadcasted_iota(jnp.int32, (count, LANES), 1) < HD
    for p in range(H // 2):
        q, k, v = (qkv[:, i * width + p * LANES : i * width + (p + 1) * LANES] for i in range(3))
        g = gatt[:, tile(p)]
        first = (jnp.where(left, q, pltpu.roll(k, HD, 1)), jnp.where(left, v, pltpu.roll(g, HD, 1)))
        second = (jnp.where(left, pltpu.roll(q, HD, 1), k), jnp.where(left, pltpu.roll(v, HD, 1), g))
        for h, pair in ((2 * p, first), (2 * p + 1, second)):
            for i, value in enumerate(pair):
                value = value.astype(BF)
                for r in range(copies):
                    o_qkvg[h * copies + r, :, tile(i)] = value


def attention_kernel(qkvg, ends, o_back, qz, kr, gz, vr, dk, dv):
    qkvg, ends = ready(qkvg, ends)
    seq_size, count = qkvg.shape[0], qkvg.shape[1]
    rows = seq_size * count
    left = lax.broadcasted_iota(jnp.int32, (count, LANES), 1) < HD
    for d in range(seq_size):
        at = slice(d * count, (d + 1) * count)
        a, b = qkvg[d, :, :LANES].astype(F32), qkvg[d, :, LANES : 2 * LANES].astype(F32)
        qz[at, :] = jnp.where(left, a, 0.0).astype(BF)
        kr[at, :] = pltpu.roll(a, HD, 1).astype(BF)
        gz[at, :] = jnp.where(left, 0.0, b).astype(BF)
        vr[at, :] = pltpu.roll(b, HD, 1).astype(BF)
    dk[...] = jnp.zeros_like(dk)
    dv[...] = jnp.zeros_like(dv)
    scale = HD**-0.5

    def queries(b, length):
        at = pl.ds(b * count if isinstance(b, int) else pl.multiple_of(b * count, count), count)
        tail = ends[b].astype(F32)
        starts = jnp.broadcast_to(tail[0:1] * 64.0 + tail[1:2], (LANES, LANES))
        first = jnp.transpose(starts)[:, :1].astype(jnp.int32)
        column = lax.broadcasted_iota(jnp.int32, (count, length), 1)
        row = b * count + lax.broadcasted_iota(jnp.int32, (count, 1), 0)
        visible = (column <= row) & (column >= first)
        scores = jnp.where(visible, dot_nt(qz[at, :], kr[:length, :]) * scale, -1e30)
        weight = jnp.exp(scores - jnp.max(scores, axis=1, keepdims=True))
        probs = weight * (1.0 / jnp.sum(weight, axis=1, keepdims=True))
        low = probs.astype(BF)
        grad_probs = dot_nt(gz[at, :], vr[:length, :])
        delta = jnp.sum(probs * grad_probs, axis=1, keepdims=True)
        grad_scores = (probs * (grad_probs - delta)).astype(BF)
        dk[:length, :] += dot_tn(grad_scores, kr[at, :])
        dv[:length, :] += dot_tn(low, vr[at, :])
        dq = dot(grad_scores, kr[:length, :])
        attended = dot(low, vr[:length, :])
        o_back[b, :, :LANES] = (dq * scale).astype(BF)
        o_back[b, :, LANES:] = attended.astype(BF)

    if seq_size <= 8:
        for b in range(seq_size):
            queries(b, (b + 1) * count)
    else:
        lax.fori_loop(0, seq_size, lambda b, _: (queries(b, rows), 0)[1], 0)
    for d in range(seq_size):
        at = slice(d * count, (d + 1) * count)
        o_back[d, :, :LANES] = jnp.where(left, o_back[d, :, :LANES].astype(F32), dk[at, :] * scale).astype(BF)
        o_back[d, :, LANES:] = jnp.where(left, dv[at, :], o_back[d, :, LANES:].astype(F32)).astype(BF)


def backward_kernel(
    back, after, w_proj, w_qkv, n2, cot, w_out, gate, ssm, s_ref, a_ref, bc,
    o_out, o_after, o_branch, o_n2, o_gate, o_g, o_msg,
    turned,
):
    back = ready(back)
    seq_size, count = back.shape[0], back.shape[1]
    copies = seq_size // H
    left = lax.broadcasted_iota(jnp.int32, (count, LANES), 1) < HD
    dq, dk, dv, att = [], [], [], []
    for p in range(H // 2):
        a0, b0 = (back[2 * p * copies, :, tile(i)].astype(F32) for i in range(2))
        a1, b1 = (back[(2 * p + 1) * copies, :, tile(i)].astype(F32) for i in range(2))
        dq.append(jnp.where(left, a0, pltpu.roll(a1, HD, 1)))
        dk.append(jnp.where(left, pltpu.roll(a0, HD, 1), a1))
        dv.append(jnp.where(left, b0, pltpu.roll(b1, HD, 1)))
        att.append(jnp.where(left, pltpu.roll(b0, HD, 1), b1))
    attended = jnp.concatenate(att, axis=1).astype(BF)
    after, w_proj = ready(after, w_proj)
    width = after.shape[1]
    o_out[...] = (after[...] + dot(attended, w_proj[...])).astype(BF)
    sent(o_out)
    w_qkv, n2, cot = ready(w_qkv, n2, cot)
    grad_qkv = jnp.concatenate(dq + dk + dv, axis=1).astype(BF)
    grad_x, grad_gain = rms_back(after[...], n2[...], dot_nt(grad_qkv, w_qkv[...]))
    o_n2[...] = jnp.sum(grad_gain, axis=0, keepdims=True)
    grad_after = cot[...].astype(F32) + grad_x
    o_after[...] = grad_after
    branch = grad_after.astype(BF)
    o_branch[...] = branch
    sent(o_n2, o_after, o_branch)
    w_out, gate, ssm = ready(w_out, gate, ssm)
    inner_width = gate.shape[1]
    tiles = inner_width // LANES
    a_ref = ready(a_ref)
    states = a_ref.shape[0] // 8
    grad_gated = dot_nt(branch, w_out[...])
    gate_rows = inner_width // seq_size
    for j in range(tiles):
        v = gate[:, tile(j)].astype(F32)
        sig = jax.nn.sigmoid(v)
        grad = grad_gated[:, tile(j)]
        to_rows(o_g, j, grad * (v * sig))
        grad_gate = grad * ssm[:, tile(j)] * (sig * (1.0 + v * (1.0 - sig)))
        o_gate[:, tile(j)] = grad_gate.astype(BF)
        turned[tile(j), :] = jnp.transpose(grad_gate).astype(BF)
    for d in range(seq_size):
        o_msg[d, states * 8 :, :] = turned[d * gate_rows : (d + 1) * gate_rows, :]
    sent(o_gate, o_g)
    s_ref, smem = ready(s_ref, bc)

    def one(i, later):
        t = count - 1 - i
        s, g = block(s_ref, t), block(o_g, t)
        return tuple(
            jnp.exp2(s * block(a_ref, n)) * (g * smem[t, states + n] + later[n])
            for n in range(states)
        )

    leaving = lax.fori_loop(0, count, one, (jnp.zeros((8, LANES), F32),) * states, unroll=4)
    for n in range(0, states, 2):
        value = jnp.concatenate([leaving[n], leaving[n + 1]], axis=0).astype(BF)
        for d in range(seq_size):
            o_msg[d, 8 * n : 8 * n + 16, :] = value


def states_kernel(
    seq_size, start, a_ref, bc, s_ref, dx_ref, inner, conv_w, conv_b, seg, o_every, o_slope, ext
):
    start, a_ref, smem, s_ref, dx_ref = ready(start, a_ref, bc, s_ref, dx_ref)
    count = smem.shape[0]
    states = a_ref.shape[0] // 8
    o_every[: states * 8, :] = start[...]

    def again(t, state):
        s, dx = block(s_ref, t), block(dx_ref, t)
        state = tuple(
            jnp.exp2(s * block(a_ref, n)) * state[n] + dx * smem[t, n] for n in range(states)
        )
        for n in range(states):
            o_every[pl.ds(pl.multiple_of(((t + 1) * states + n) * 8, 8), 8), :] = state[n]
        return state

    lax.fori_loop(0, count, again, tuple(start[8 * n : 8 * n + 8, :] for n in range(states)), unroll=2)
    sent(o_every)
    inner, conv_w, conv_b, seg = ready(inner, conv_w, conv_b, seg)
    ext[...] = inner[...].astype(F32)
    offset = offsets_in_sequence(seg, seq_size)
    for j in range(o_slope.shape[1] // LANES):
        pre = conv_tile(ext, conv_w, conv_b, offset, j, count)
        sig = jax.nn.sigmoid(pre)
        o_slope[:, tile(j)] = sig * (1.0 + pre * (1.0 - sig))


def fold8(values, sub):
    low4, low2, low1 = sub < 4, (sub & 2) == 0, (sub & 1) == 0
    four = []
    for k in range(4):
        a, b = values[k], values[k + 4]
        four.append(jnp.where(low4, a, b) + pltpu.roll(jnp.where(low4, b, a), 4, 0))
    two = []
    for k in range(2):
        a, b = four[k], four[k + 2]
        two.append(jnp.where(low2, a + pltpu.roll(a, 6, 0), b + pltpu.roll(b, 2, 0)))
    a, b = two
    return jnp.where(low1, a + pltpu.roll(a, 7, 0), b + pltpu.roll(b, 1, 0))


def adjoint_kernel(
    seq_size, back, totals, a_ref, bc, s_ref, dx_ref, g_ref, mixed, step_pre, low, w_dt, w_xp, inner, slope, conv_w, d_skip,
    seg, grad_n2, every,
    o_msg, o_inner,
    held, gs_ref, ai_ref, sums, small, ext, gext, arrived,
):
    back, totals, a_ref = ready(back, totals, a_ref)
    states = a_ref.shape[0] // 8
    count = s_ref.shape[0] // 8
    zero = jnp.zeros((8, LANES), F32)
    chunks = arrived.shape[0]
    span = count // chunks
    loads = []
    for c in range(chunks):
        first, last = c * span * states * 8, ((c + 1) * span + (c == chunks - 1)) * states * 8
        loads.append(pltpu.make_async_copy(every.at[first:last], held.at[first:last], arrived.at[c]))
    for load in reversed(loads):
        load.start()

    def join(i, carry):
        d = seq_size - 1 - i
        total = total_step(totals, d, 0)
        return tuple(
            jnp.exp2(block(a_ref, n) * total) * carry[n] + state_rows(back, d, n)
            for n in range(states)
        )

    leaving = lax.fori_loop(0, seq_size - 1 - lax.axis_index("seq"), join, (zero,) * states)
    smem, s_ref, dx_ref, g_ref = ready(bc, s_ref, dx_ref, g_ref)
    sub = lax.broadcasted_iota(jnp.int32, (8, LANES), 0)

    def one(last, i, carry):
        later, grad_a = carry
        t = last - i
        s, dx, g = block(s_ref, t), block(dx_ref, t), block(g_ref, t)
        new_later, new_grad_a, with_b, with_c = [], [], [], []
        grad_step, adjoint_in = zero, zero
        for n in range(states):
            a = block(a_ref, n)
            adjoint = g * smem[t, states + n] + later[n]
            passed = jnp.exp2(s * a) * adjoint
            before = held[pl.ds(pl.multiple_of((t * states + n) * 8, 8), 8), :]
            now = held[pl.ds(pl.multiple_of(((t + 1) * states + n) * 8, 8), 8), :]
            grad_decay = passed * before
            grad_step = grad_step + grad_decay * a
            adjoint_in = adjoint_in + adjoint * smem[t, n]
            new_later.append(passed)
            new_grad_a.append(grad_a[n] + grad_decay * s)
            with_b.append(adjoint * dx)
            with_c.append(g * now)
        here = pl.ds(pl.multiple_of(t * 8, 8), 8)
        gs_ref[here, :] = grad_step
        ai_ref[here, :] = adjoint_in
        for i, part in enumerate((with_b[:8], with_b[8:], with_c[:8], with_c[8:])):
            sums[pl.ds(pl.multiple_of(t * 32 + 8 * i, 8), 8), :] = fold8(part, sub)
        return tuple(new_later), tuple(new_grad_a)

    carry = (leaving, (zero,) * states)
    for c in reversed(range(chunks)):
        loads[c].wait()
        carry = lax.fori_loop(0, span, functools.partial(one, (c + 1) * span - 1), carry)
    grad_a = carry[1]
    mixed, step_pre, low, w_dt, w_xp, inner = ready(mixed, step_pre, low, w_dt, w_xp, inner)
    slope, conv_w, d_skip, seg, grad_n2 = ready(slope, conv_w, d_skip, seg, grad_n2)
    inner_width = mixed.shape[1]
    tiles = inner_width // LANES
    rank = w_dt.shape[0]
    taps = conv_w.shape[0]
    small[...] = jnp.zeros_like(small)
    for n in range(states):
        small[(104 + n) * 8 : (105 + n) * 8, :] = grad_a[n] * (LN2 * block(a_ref, n))
    lane = lax.broadcasted_iota(jnp.int32, (count, rank + 2 * states), 1)
    grad_bc = jnp.zeros((count, rank + 2 * states), F32)
    for q in range(2 * states):
        total = jnp.sum(sums[pl.ds(q, count, stride=2 * states), :], axis=1, keepdims=True)
        grad_bc = jnp.where(lane == rank + q, total, grad_bc)
    offset = offsets_in_sequence(seg, seq_size)
    halves = []
    for j in range(tiles):
        mix = mixed[:, tile(j)].astype(F32)
        pre = step_pre[:, tile(j)]
        grad_step = LN2 * from_rows(gs_ref, j, count) + mix * from_rows(ai_ref, j, count)
        grad_pre = grad_step * jax.nn.sigmoid(pre)
        small[101 * 8 + j : 101 * 8 + j + 1, :] = jnp.sum(grad_pre, axis=0, keepdims=True)
        grad_ssm = from_rows(g_ref, j, count)
        small[102 * 8 + j : 102 * 8 + j + 1, :] = jnp.sum(grad_ssm * mix, axis=0, keepdims=True)
        halves.append(grad_pre.astype(BF))
    half = jnp.concatenate(halves, axis=1)
    grad_w_dt = dot_tn(low[...], half)
    padded_dt = jnp.concatenate([w_dt[...], jnp.zeros((2 * states, inner_width), BF)], axis=0)
    grad_selector = (dot_nt(half, padded_dt) + grad_bc).astype(BF)
    grad_w_xp = dot_tn(grad_selector, mixed[...])
    from_selector = dot(grad_selector, w_xp[...])
    ext[...] = inner[...].astype(F32)
    gext[...] = jnp.zeros_like(gext)
    for j in range(tiles):
        to_rows(small.at[pl.ds(0, 64 * 8)], j, grad_w_xp[:, tile(j)])
        to_rows(small.at[pl.ds(64 * 8, 32 * 8)], j, grad_w_dt[:, tile(j)])
        grad_mixed = (
            softplus(step_pre[:, tile(j)]) * from_rows(ai_ref, j, count)
            + from_rows(g_ref, j, count) * d_skip[:, tile(j)]
            + from_selector[:, tile(j)]
        )
        grad_pre = grad_mixed * slope[:, tile(j)]
        small[100 * 8 + j : 100 * 8 + j + 1, :] = jnp.sum(grad_pre, axis=0, keepdims=True)
        for k in range(taps):
            shifted = pl.ds(HALO - taps + 1 + k, count)
            usable = jnp.where(offset >= taps - 1 - k, grad_pre, 0.0)
            row = (96 + k) * 8 + j
            small[row : row + 1, :] = jnp.sum(usable * ext[shifted, tile(j)], axis=0, keepdims=True)
            gext[shifted, tile(j)] += conv_w[k : k + 1, tile(j)] * usable
    piece = inner_width // seq_size
    per = small.shape[0] // seq_size
    o_inner[...] = gext[...].astype(BF)
    sent(o_inner)
    for j in range(tiles):
        value = jnp.transpose(gext[HALO:, tile(j)]).astype(BF)
        for i in range(LANES // piece):
            o_msg[j * (LANES // piece) + i, :piece, :] = value[i * piece : (i + 1) * piece]
    for d in range(seq_size):
        rows = gext[:HALO, d * piece : (d + 1) * piece]
        if piece < LANES:
            rows = jnp.concatenate([rows, jnp.zeros((HALO, LANES - piece), F32)], axis=1)
        o_msg[d, piece : piece + HALO, :] = rows.astype(BF)
    width = grad_n2.shape[1]
    for j in range(width // LANES):
        small[103 * 8 + 4 + j : 103 * 8 + 5 + j, :] = grad_n2[:, tile(j)]
    for d in range(seq_size):
        o_msg[d, piece + HALO :, :] = small[d * per : (d + 1) * per, :].astype(BF)


def tokens_kernel(grad_inner, w_in, grad_gate, tok, halo, n1, grad_after, o_tok, o_halo, o_n1):
    grad_inner, w_in, grad_gate = ready(grad_inner, w_in, grad_gate)
    inner_width = grad_inner.shape[1]
    grad_normed = dot_nt(grad_inner[...], w_in[:, :inner_width])
    own = dot_nt(grad_gate[...], w_in[:, inner_width:])
    grad_normed = jnp.concatenate([grad_normed[:HALO], grad_normed[HALO:] + own], axis=0)
    tok, halo, n1, grad_after = ready(tok, halo, n1, grad_after)
    x = jnp.concatenate([halo[...], tok[...]], axis=0).astype(F32)
    grad_x, grad_gain = rms_back(x, n1[...], grad_normed)
    o_tok[...] = grad_after[...] + grad_x[HALO:]
    o_halo[...] = grad_x[HALO - 8 : HALO]
    grad_gain = jnp.sum(grad_gain, axis=0, keepdims=True)
    tiles = grad_gain.shape[1] // LANES
    rows = [grad_gain[:, tile(j)] for j in range(tiles)] + [jnp.zeros((16 - tiles, LANES), F32)]
    o_n1[...] = jnp.concatenate(rows, axis=0).astype(BF)


def head_products_kernel(width, back, cot, normed, *outs):
    back, cot, normed = ready(back, cot, normed)
    seq_size, count = back.shape[0], back.shape[1]
    both = back[...].reshape(seq_size * count, 2 * LANES)
    proj = dot_tn(both[:, LANES:], cot[...])[HD:]
    if len(outs) == 1:
        first = dot_tn(normed[:, width:], both[:, :LANES])
        second = dot_tn(normed[:, width:], both[:, LANES:])
        left = lax.broadcasted_iota(jnp.int32, (HD, LANES), 1) < HD
        for g in range(width // LANES):
            outs[0][g, :HD, :] = proj[:, tile(g)].astype(BF)
            outs[0][g, HD : 3 * HD, :] = first[tile(g)].astype(BF)
            low, high = second[g * LANES : g * LANES + HD], second[g * LANES + HD : (g + 1) * LANES]
            outs[0][g, 3 * HD :, :] = jnp.where(left, low, pltpu.roll(high, HD, 1)).astype(BF)
    else:
        outs[0][...] = proj.astype(BF)
        outs[1][: 2 * HD, :] = dot_tn(both[:, :LANES], normed[:, width:]).astype(BF)
        outs[1][2 * HD :, :] = dot_tn(both[:, LANES:], normed[:, width:])[:HD].astype(BF)


def gate_products_kernel(piece, normed, adj, *rest):
    normed, adj = ready(normed, adj)
    seq_size = adj.shape[0]
    count = normed.shape[0] // seq_size
    width = normed.shape[1]
    gate = jnp.zeros((piece, width), F32)
    for d in range(seq_size):
        gate = gate + dot(adj[d], normed[d * count : (d + 1) * count, :])
    if len(rest) == 2:
        head, pieces = rest
        head = ready(head)
        own = head.shape[1]
        for g in range(head.shape[0]):
            pieces[g, :own, :] = head[g]
            pieces[g, own:, :] = jnp.transpose(gate[:, tile(g)]).astype(BF)
    else:
        rest[0][...] = gate.astype(BF)


def late_products_kernel(piece, gated, branch, normed, tail, *outs):
    gated, branch = ready(gated, branch)
    seq_size, count = gated.shape[0], gated.shape[1]
    width = branch.shape[1]
    out = jnp.zeros((piece, width), F32)
    for d in range(seq_size):
        out = out + dot_tn(gated[d, :, :piece], branch[d * count : (d + 1) * count, :])
    normed, tail = ready(normed, tail)
    grad = jnp.zeros((piece, width), F32)
    small = jnp.zeros((tail.shape[1] - piece - HALO, LANES), F32)
    for d in range(seq_size):
        grad = grad + dot(tail[d, :piece, :], normed[d * count : (d + 1) * count, :])
        small = small + tail[d, piece + HALO :, :].astype(F32)
        if d:
            borrowed = dot_tn(tail[d, piece : piece + HALO, :], normed[d * count - HALO : d * count, :])
            grad = grad + borrowed[:piece]
    if len(outs) == 1:
        groups = outs[0].shape[0]
        rows = small.shape[0] // groups
        for g in range(groups):
            outs[0][g, :LANES, :] = jnp.transpose(grad[:, tile(g)]).astype(BF)
            outs[0][g, LANES : 2 * LANES, :] = out[:, tile(g)].astype(BF)
            outs[0][g, 2 * LANES :, :] = small[g * rows : (g + 1) * rows].astype(BF)
    else:
        outs[0][...] = grad.astype(BF)
        outs[1][...] = out.astype(BF)
        outs[2][...] = small.astype(BF)


def sum_kernel(parts, o_sum):
    parts = ready(parts)
    total = parts[0].astype(F32)
    for d in range(1, parts.shape[0]):
        total = total + parts[d].astype(F32)
    o_sum[...] = total.astype(BF)


def sum_and_spread_kernel(parts, own, o_all):
    parts, own = ready(parts, own)
    total = parts[0].astype(F32)
    for d in range(1, parts.shape[0]):
        total = total + parts[d].astype(F32)
    total = total.astype(BF)
    rows = total.shape[0]
    for d in range(o_all.shape[0]):
        o_all[d, :rows, :] = total
        o_all[d, rows:, :] = own[...]


def early_assembly_kernel(groups, early, o_proj, o_qkv, o_in, gate, sem):
    early = ready(early)
    seq_size = early.shape[0] // groups
    width = o_proj.shape[1]
    inner_width = gate.shape[1]
    left = lax.broadcasted_iota(jnp.int32, (LANES, LANES), 1) < HD

    def pairs(a, b):
        a, b = a.astype(F32), b.astype(F32)
        mask = left[: a.shape[0]]
        return jnp.where(mask, a, pltpu.roll(b, HD, 1)), jnp.where(mask, pltpu.roll(a, HD, 1), b)

    for g in range(groups):
        for s in range(seq_size):
            gate[tile(g), tile(s)] = early[g * seq_size + s, 4 * HD :, :].astype(F32)
    copy = pltpu.make_async_copy(gate, o_in.at[:, inner_width:], sem)
    copy.start()
    for g in range(groups):
        rows = tile(g)
        for s in range(seq_size):
            o_proj[s * HD : (s + 1) * HD, tile(g)] = early[g * seq_size + s, :HD, :].astype(F32)
        for p in range(seq_size // 2):
            a, b = g * seq_size + 2 * p, g * seq_size + 2 * p + 1
            q, k = pairs(early[a, HD : 3 * HD, :], early[b, HD : 3 * HD, :])
            o_qkv[rows, p * LANES : (p + 1) * LANES] = q
            o_qkv[rows, width + p * LANES : width + (p + 1) * LANES] = k
            low, high = pairs(early[a, 3 * HD : 4 * HD, :], early[b, 3 * HD : 4 * HD, :])
            o_qkv[g * LANES : g * LANES + HD, 2 * width + p * LANES : 2 * width + (p + 1) * LANES] = low
            o_qkv[g * LANES + HD : (g + 1) * LANES, 2 * width + p * LANES : 2 * width + (p + 1) * LANES] = high
    copy.wait()


def late_assembly_kernel(
    groups, mine, other, w_in, o_in, o_out, o_n1, o_conv_w, o_conv_b, o_xp, o_dt, o_dtb, o_a, o_skip, o_n2,
    inner, small, sem,
):
    mine, other = ready(mine, other)
    seq_size = mine.shape[0] * 2 // groups
    core = lax.rem(lax.axis_index("dp"), 2)
    width, inner_width = inner.shape
    rows = mine.shape[1] - 2 * LANES - 16
    for x in range(groups // 2):
        for source, side in ((mine, core), (other, 1 - core)):
            g = 2 * x + side
            at = pl.ds(pl.multiple_of(g * LANES, LANES), LANES)
            for s in range(seq_size):
                inner[at, tile(s)] = source[x * seq_size + s, :LANES, :].astype(F32)
                here = pl.ds(pl.multiple_of(s * LANES + g * rows, rows), rows)
                small[here, :] = source[x * seq_size + s, 2 * LANES : 2 * LANES + rows, :].astype(F32)
    copy = pltpu.make_async_copy(inner, o_in.at[:, :inner_width], sem)
    copy.start()
    for x in range(groups // 2):
        for side in range(2):
            for s in range(seq_size):
                piece = [ref[x * seq_size + s, LANES : 2 * LANES, :] for ref in (mine, other)]
                value = jnp.where(core == side, piece[0].astype(F32), piece[1].astype(F32))
                o_out[tile(s), tile(2 * x + side)] = value
    for j in range(inner_width // LANES):
        value = from_rows(small, j, SMALL)
        for ref, first, last in (
            (o_xp, 0, 64), (o_dt, 64, 96), (o_conv_w, 96, 100), (o_conv_b, 100, 101), (o_dtb, 101, 102),
            (o_skip, 102, 103), (o_a, 104, 120),
        ):
            ref[:, tile(j)] = value[first:last]
        if j >= width // LANES:
            o_n2[:, tile(j - width // LANES)] = value[103:104]
    gain = jnp.zeros((16, LANES), F32)
    for source in (mine, other):
        for d in range(source.shape[0]):
            gain = gain + source[d, 2 * LANES + rows :, :].astype(F32)
    for j in range(width // LANES):
        o_n1[:, tile(j)] = gain[j : j + 1]
    copy.wait()


class Held:
    def __init__(self, buffer, copy):
        self.ref, self.copy, self.shape = buffer, copy, buffer.shape
        self.done = False

    def __getitem__(self, at):
        return self.ref[at]

    def __setitem__(self, at, value):
        self.ref[at] = value


def ready(*held):
    for one in held:
        if not one.done:
            one.copy.wait()
            one.done = True
    refs = tuple(one.ref for one in held)
    return refs if len(refs) > 1 else refs[0]


def sent(*held):
    for one in held:
        if not one.done:
            one.copy.start()
            one.done = True


IN_HBM = pl.BlockSpec(memory_space=pltpu.HBM)


def call(
    kernel, outs, scratch, *args, name=None, us=1, raw=(), raw_out=(), scalars=(), views=None, aliases=None, after=(),
    vmem=60,
):
    views = views or {}
    count, first_out = len(args), len(args) + len(after)
    first_scratch = first_out + len(outs)
    buffers = []
    for i, arg in enumerate(args):
        shape = jax.eval_shape(lambda v, i=i: v[views[i]], arg).shape if i in views else arg.shape
        kind = pltpu.SMEM if i in scalars else pltpu.VMEM
        buffers.append(None if i in raw else kind(shape, arg.dtype))
    for i, (shape, dtype) in enumerate(outs):
        buffers.append(None if i in raw_out else pltpu.VMEM(shape, dtype))
    used = [b for b in buffers if b is not None]

    def run(*refs):
        given = list(refs[:count]) + list(refs[first_out:first_scratch])
        own = list(refs[first_scratch : first_scratch + len(used)])
        sems = refs[first_scratch + len(used)]
        passed = []
        for i, (ref, buffer) in enumerate(zip(given, buffers)):
            if buffer is None:
                passed.append(ref)
                continue
            buffer = own.pop(0)
            if i < count:
                source = ref.at[views[i]] if i in views else ref
                copy = pltpu.make_async_copy(source, buffer, sems.at[i])
                copy.start()
            else:
                copy = pltpu.make_async_copy(buffer, ref, sems.at[i])
            passed.append(Held(buffer, copy))
        kernel(*passed, *refs[first_scratch + len(used) + 1 :])
        ready(*[p for p in passed[:count] if isinstance(p, Held)])
        results = [p for p in passed[count:] if isinstance(p, Held)]
        sent(*results)
        for result in results:
            result.copy.wait()

    return pl.pallas_call(
        run,
        out_shape=[jax.ShapeDtypeStruct(s, d) for s, d in outs],
        in_specs=[IN_HBM] * first_out,
        out_specs=[IN_HBM] * len(outs),
        scratch_shapes=used + [pltpu.SemaphoreType.DMA((len(buffers),))] + scratch,
        compiler_params=pltpu.CompilerParams(vmem_limit_bytes=vmem * 1024 * 1024),
        cost_estimate=pl.CostEstimate(flops=us * 1000, bytes_accessed=us * 1000, transcendentals=0),
        input_output_aliases=aliases or {},
        name=name,
    )(*args, *after)


def exchange(value, axes):
    return lax.all_to_all(value, axes, 0, 0, tiled=True)


def everywhere(value):
    axes = ("dp", "seq")
    count = lax.axis_size(axes)
    return exchange(jnp.broadcast_to(value[None], (count,) + value.shape), axes)


def own_core(value, groups, seq_size):
    peers = [
        [g * seq_size + s for g in range(core, groups, 2) for s in range(seq_size)] for core in range(2)
    ]
    return lax.all_to_all(value, ("dp", "seq"), 0, 0, tiled=True, axis_index_groups=peers)


def body(
    tokens, seg_start, norm_one, w_in, conv_w, conv_b, w_xproj, w_dt, dt_bias, a_log, d_skip,
    w_out, norm_two, w_qkv, w_proj, cotangent,
):
    count, width = tokens.shape
    inner_width = w_in.shape[1] // 2
    states = a_log.shape[1]
    rank = w_dt.shape[0]
    groups, seq_size = lax.axis_size("dp"), lax.axis_size("seq")
    rows = count * seq_size
    ext_rows = HALO + count
    piece = inner_width // seq_size
    copies = seq_size // H
    tiled = piece == LANES and width == groups * LANES and copies == 1
    line = lambda v: v.reshape(1, -1)
    seg = line(seg_start)
    n1, n2, cb, dtb, skip = (line(v) for v in (norm_one, norm_two, conv_b, dt_bias, d_skip))
    vmem, smem = pltpu.VMEM, pltpu.SMEM((count, 2 * states), F32)
    sem = pltpu.SemaphoreType.DMA
    blocks = ((count * 8, LANES), F32)
    onward = [(i, i + 1) for i in range(seq_size - 1)]
    cot_all = lax.all_gather(cotangent, "seq", axis=0, tiled=True)
    ends_at = states * 8
    halo = lax.ppermute(tokens[count - HALO :], "seq", onward)
    msg, normed, inner, gate, mixed, bc, low, step_pre, s, dx, a = call(
        functools.partial(forward_kernel, seq_size),
        [
            ((seq_size, states * 8 + 32, LANES), BF), ((count, width), BF),
            ((ext_rows, inner_width), BF), ((count, inner_width), BF), ((count, inner_width), BF), ((count, 2 * states), F32), ((count, rank), BF),
            ((count, inner_width), F32), blocks, blocks, ((states * 8, LANES), F32),
        ],
        [vmem((ext_rows, inner_width), F32), smem, sem],
        tokens, halo, n1, w_in, conv_w, cb, w_xproj.T, w_dt, dtb, a_log.T, seg,
        name="forward", us=8,
    )
    msg = exchange(msg, "seq")
    qkvg, start, ssm, normed, after = call(
        middle_kernel,
        [
            ((seq_size, count, 3 * LANES), BF), ((states * 8, LANES), F32), ((count, inner_width), F32),
            ((count, 2 * width), BF), ((count, width), F32),
        ],
        [vmem((count, inner_width), BF), vmem(*blocks)],
        msg, a, bc, s, dx, mixed, gate, skip, tokens, w_out, n2, w_qkv, cotangent, w_proj, normed,
        name="middle", us=8, scalars=(2,), views={0: np.s_[:, : ends_at + 16, :]},
    )
    normed_all = lax.all_gather(normed, "seq", axis=0, tiled=True)
    qkvg = exchange(qkvg, "seq")
    (back,) = call(
        attention_kernel,
        [((seq_size, count, 2 * LANES), BF)],
        [vmem((rows, LANES), BF)] * 4 + [vmem((rows, LANES), F32)] * 2,
        qkvg, msg, name="attention", us=7,
        views={0: np.s_[:, :, : 2 * LANES], 1: np.s_[:, ends_at + 16 :, :]},
    )
    back_own = exchange(back, "seq")
    out, grad_after, branch, grad_n2, grad_gate, g, adj = call(
        backward_kernel,
        [
            ((count, width), BF), ((count, width), F32), ((count, width), BF), ((1, width), F32),
            ((count, inner_width), BF), blocks, ((seq_size, states * 8 + piece, LANES), BF),
        ],
        [vmem((inner_width, LANES), BF)],
        back_own, after, w_proj, w_qkv, n2, cotangent, w_out, gate, ssm, s, a, bc,
        name="backward", us=7, scalars=(11,),
    )
    adj = exchange(adj, "seq")
    branch_all = lax.all_gather(branch, "seq", axis=0, tiled=True)
    every, slope = call(
        functools.partial(states_kernel, seq_size),
        [(((count + 1) * states * 8, LANES), F32), ((count, inner_width), F32)],
        [vmem((ext_rows, inner_width), F32)],
        start, a, bc, s, dx, inner, conv_w, cb, seg, name="states", us=6, scalars=(2,),
    )
    gate_views = {0: np.s_[:, :width], 1: np.s_[:, ends_at:, :]}
    if tiled:
        (head,) = call(
            functools.partial(head_products_kernel, width), [((groups, 4 * HD, LANES), BF)], [],
            back, cot_all, normed_all, name="head_products", us=3,
        )
        (early,) = call(
            functools.partial(gate_products_kernel, piece), [((groups, 4 * HD + LANES, LANES), BF)], [],
            normed_all, adj, head, name="gate_products", us=2, after=(every,), views=gate_views,
        )
    else:
        proj_part, qkv_part = call(
            functools.partial(head_products_kernel, width), [((HD, width), BF), ((3 * HD, width), BF)], [],
            back, cot_all, normed_all, name="head_products", us=3,
        )
        (gate_part,) = call(
            functools.partial(gate_products_kernel, piece), [((piece, width), BF)], [],
            normed_all, adj, name="gate_products", us=2, views=gate_views,
        )
        head = jnp.concatenate([proj_part, qkv_part], axis=0)
        if copies > 1:
            own = 4 * HD // copies
            head = lax.dynamic_slice_in_dim(head, lax.axis_index("seq") % copies * own, own, 0)
        early = jnp.concatenate([v.reshape(groups, -1, LANES) for v in (head, gate_part)], axis=1)
    adjoint_in = (adj, msg, a, bc, s, dx, g, mixed, step_pre, low, w_dt, w_xproj.T, inner, slope, conv_w, skip, seg,
                  grad_n2, every)
    tail, grad_inner = call(
        functools.partial(adjoint_kernel, seq_size),
        [((seq_size, piece + HALO + SMALL * 8 // seq_size, LANES), BF), ((ext_rows, inner_width), BF)],
        [
            vmem(((count + 1) * states * 8, LANES), F32), vmem(*blocks), vmem(*blocks),
            vmem((count * 2 * states, LANES), F32), vmem((SMALL * 8, LANES), F32),
            vmem((ext_rows, inner_width), F32), vmem((ext_rows, inner_width), F32), sem((8,)),
        ],
        *adjoint_in, name="adjoint", us=15, raw=(len(adjoint_in) - 1,), scalars=(3,),
        views={0: np.s_[:, :ends_at, :], 1: np.s_[:, ends_at : ends_at + 16, :]},
    )
    early = exchange(early, "dp")
    (early,) = call(
        sum_kernel, [(early.shape[1:], BF)], [], early, name="early_sum", us=1, after=(grad_inner,)
    )
    early = lax.all_gather(early, ("dp", "seq"))
    tail = exchange(tail, "seq")
    grad_tokens, grad_halo, grad_n1 = call(
        tokens_kernel, [((count, width), F32), ((8, width), F32), ((16, LANES), BF)], [],
        grad_inner, w_in, grad_gate, tokens, halo, n1, grad_after, name="tokens", us=4,
    )
    returned = lax.ppermute(grad_halo, "seq", [(i + 1, i) for i in range(seq_size - 1)])
    grad_tokens = grad_tokens.at[count - 8 :].add(returned)
    per = SMALL * 8 // seq_size
    late_views = {0: np.s_[:, :, 2 * LANES :], 2: np.s_[:, :width]}
    if tiled:
        (late,) = call(
            functools.partial(late_products_kernel, piece), [((groups, 2 * LANES + per // groups, LANES), BF)], [],
            qkvg, branch_all, normed_all, tail, name="late_products", us=2, views=late_views,
        )
    else:
        in_part, out_part, small = call(
            functools.partial(late_products_kernel, piece), [((piece, width), BF), ((piece, width), BF), ((per, LANES), BF)],
            [], qkvg, branch_all, normed_all, tail, name="late_products", us=2, views=late_views,
        )
        late = jnp.concatenate([v.reshape(groups, -1, LANES) for v in (in_part, out_part, small)], axis=1)
    late = exchange(late, "dp")
    copies_out = groups // 2 * seq_size if tiled else 1
    (late,) = call(
        sum_and_spread_kernel, [((copies_out, late.shape[1] + 16, LANES), BF)], [], late, grad_n1, name="late_sum", us=1
    )
    if tiled:
        grad_w_proj, grad_w_qkv, half = call(
            functools.partial(early_assembly_kernel, groups),
            [((width, width), F32), ((width, 3 * width), F32), ((width, 2 * inner_width), F32)],
            [vmem((width, inner_width), F32), sem],
            early, name="early_assembly", us=6, raw_out=(2,),
        )
        mine = own_core(late, groups, seq_size)
        mine, half, grad_tokens = lax.optimization_barrier((mine, half, grad_tokens))
        other = lax.ppermute(mine, "dp", [(g, g ^ 1) for g in range(groups)])
        row = lambda n: ((n, inner_width), F32)
        grad_w_in, grad_w_out, g_n1, g_conv_w, g_conv_b, g_xp, g_dt, g_dtb, g_a, g_skip, g_n2 = call(
            functools.partial(late_assembly_kernel, groups),
            [
                ((width, 2 * inner_width), F32), ((inner_width, width), F32), ((1, width), F32), row(conv_w.shape[0]),
                row(1), row(2 * states + rank), row(rank), row(1), row(states), row(1), ((1, width), F32),
            ],
            [vmem((width, inner_width), F32), vmem((SMALL * 8, LANES), F32), sem],
            mine, other, half, name="late_assembly", us=4,
            raw=(2,), raw_out=(0,), aliases={2: 0},
        )
        flat = lambda v: v.reshape(-1)
        return (out, grad_tokens, flat(g_n1), grad_w_in, g_conv_w, flat(g_conv_b), g_xp.T, g_dt, flat(g_dtb), g_a.T,
                flat(g_skip), grad_w_out, flat(g_n2), grad_w_qkv, grad_w_proj)
    late = everywhere(late[0])

    def whole(gathered, first, last):
        part = gathered.reshape(groups, seq_size, -1, LANES)[:, :, first:last]
        return part.swapaxes(0, 1).reshape(seq_size, -1)

    def cut(sizes):
        ends, total = [], 0
        for n in sizes:
            ends.append((total, total + n // LANES // groups))
            total = ends[-1][1]
        return ends

    at_head, at_gate = cut((4 * HD * width // copies, piece * width))
    at_in, at_out, at_small = cut((piece * width, piece * width, per * LANES))
    heads = whole(early, *at_head).reshape(H, 4, HD, width)
    grad_w_proj = heads[:, 0].reshape(H * HD, width).astype(F32)
    grad_w_qkv = heads[:, 1:].transpose(3, 1, 0, 2).reshape(width, 3 * width).astype(F32)
    grad_w_out = whole(late, *at_out).reshape(inner_width, width).astype(F32)
    grad_w_in = jnp.concatenate(
        [whole(late, *at_in).reshape(inner_width, width), whole(early, *at_gate).reshape(inner_width, width)], axis=0
    ).T.astype(F32)
    small = whole(late, *at_small).reshape(SMALL, inner_width).astype(F32)
    return (
        out,
        grad_tokens,
        jnp.sum(late[:, -16:].reshape(groups * seq_size, -1)[:, :width].astype(F32), axis=0),
        grad_w_in,
        small[96:100],
        small[100],
        small[:64].T,
        small[64:96],
        small[101],
        small[104:120].T,
        small[102],
        grad_w_out,
        small[103, width:],
        grad_w_qkv,
        grad_w_proj,
    )


def solution(mesh):
    split, copied = P(("dp", "seq"), None), P()
    return jax.shard_map(
        body,
        mesh=mesh,
        in_specs=(split, P(("dp", "seq"))) + (copied,) * 13 + (split,),
        out_specs=(split, split) + (copied,) * 13,
        check_vma=False,
    )
```

```python
import functools

import jax
import jax.numpy as jnp
import numpy as np
from jax import lax
from jax.experimental import pallas as pl
from jax.experimental.pallas import tpu as pltpu
from jax.sharding import PartitionSpec as P

H = 8
HD = 64
LANES = 128
HALO = 16
SMALL = 128
RESET = 1e30
EPSILON = 1e-05
LOG2E = 1.4426950408889634
LN2 = 0.6931471805599453
BF = jnp.bfloat16
F32 = jnp.float32


def dot(a, b):
    return jnp.dot(a, b, preferred_element_type=F32)


def dot_nt(a, b):
    return lax.dot_general(a, b, (((1,), (1,)), ((), ())), preferred_element_type=F32)


def dot_tn(a, b):
    return lax.dot_general(a, b, (((0,), (0,)), ((), ())), preferred_element_type=F32)


def tile(j):
    return slice(j * LANES, (j + 1) * LANES)


def softplus(x):
    u = jnp.exp(-jnp.abs(x))
    series = u * (1.0 - u * (0.5 - u * (1.0 / 3.0 - u * 0.25)))
    return jnp.maximum(x, 0.0) + jnp.where(u < 0.015, series, jnp.log(1.0 + u))


def rms_parts(x):
    return lax.rsqrt(jnp.mean(x * x, axis=-1, keepdims=True) + EPSILON)


def rms_back(x, gain, grad):
    r = rms_parts(x)
    scaled = grad * gain
    inner = jnp.mean(x * scaled, axis=-1, keepdims=True)
    return r * scaled - x * (r * r * r * inner), grad * x * r


def to_rows(ref, j, value):
    ref[pl.ds(j, value.shape[0], stride=8), :] = value


def from_rows(ref, j, count):
    return ref[pl.ds(j, count, stride=8), :]


def block(ref, t):
    return ref[pl.ds(pl.multiple_of(t * 8, 8), 8), :]


def offsets_in_sequence(seg_ref, seq_size):
    count = seg_ref.shape[1]
    base = (lax.axis_index("dp") * seq_size + lax.axis_index("seq")) * count
    places = base + lax.broadcasted_iota(jnp.int32, (1, count), 1)
    row = (places - seg_ref[...]).astype(F32)
    return jnp.transpose(jnp.broadcast_to(row, (LANES, count)))


def conv_tile(ext_ref, w_ref, b_ref, offset, j, count):
    taps = w_ref.shape[0]
    pre = jnp.broadcast_to(b_ref[:, tile(j)], (count, LANES))
    for k in range(taps):
        rows = ext_ref[pl.ds(HALO - taps + 1 + k, count), tile(j)]
        pre = pre + jnp.where(offset >= taps - 1 - k, w_ref[k : k + 1, tile(j)] * rows, 0.0)
    return pre


def forward_kernel(
    seq_size, tok, halo, n1, w_in, conv_w, conv_b, w_xp, w_dt, dtb, a_log, seg,
    o_msg, o_normed, o_inner, o_gate, o_mixed, o_bc, o_low, o_pre, o_s, o_dx, o_a,
    ext, smem, sem,
):
    tok, halo, n1, seg = ready(tok, halo, n1, seg)
    count = tok.shape[0]
    states = a_log.shape[0]
    inner_width = conv_w.shape[1]
    tiles = inner_width // LANES
    rank = w_dt.shape[0]
    x = jnp.concatenate([halo[...], tok[...]], axis=0).astype(F32)
    normed = (x * rms_parts(x) * n1[...]).astype(BF)
    o_normed[...] = normed
    sent(o_normed)
    w_in = ready(w_in)
    inner = dot(normed, w_in[:, :inner_width]).astype(BF)
    o_inner[...] = inner
    sent(o_inner)
    ext[...] = inner.astype(F32)
    o_gate[...] = dot(normed[HALO:], w_in[:, inner_width:]).astype(BF)
    sent(o_gate)
    conv_w, conv_b, w_xp, w_dt, dtb, a_log = ready(conv_w, conv_b, w_xp, w_dt, dtb, a_log)
    offset = offsets_in_sequence(seg, seq_size)
    for j in range(tiles):
        pre = conv_tile(ext, conv_w, conv_b, offset, j, count)
        o_mixed[:, tile(j)] = (pre * jax.nn.sigmoid(pre)).astype(BF)
    sent(o_mixed)
    selector = dot_nt(o_mixed[...], w_xp[...])
    low = selector[:, :rank].astype(BF)
    o_low[...] = low
    o_bc[...] = selector[:, rank:]
    sent(o_low, o_bc)
    copy = pltpu.make_async_copy(o_bc.ref, smem, sem)
    copy.start()
    o_pre[...] = dot(low, w_dt[...]) + dtb[...]
    sent(o_pre)
    for j in range(tiles):
        step = softplus(o_pre[:, tile(j)])
        to_rows(o_s, j, jnp.where(offset == 0.0, RESET, step))
        to_rows(o_dx, j, step * o_mixed[:, tile(j)].astype(F32))
        to_rows(o_a, j, -LOG2E * jnp.exp(a_log[:, tile(j)]))
    sent(o_s, o_dx, o_a)
    copy.wait()

    def one(t, carry):
        total, state = carry
        s, dx = block(o_s, t), block(o_dx, t)
        return total + s, tuple(
            jnp.exp2(s * block(o_a, n)) * state[n] + dx * smem[t, n] for n in range(states)
        )

    zero = jnp.zeros((8, LANES), F32)
    total, state = lax.fori_loop(0, count, one, (zero, (zero,) * states), unroll=4)
    high = total.astype(BF).astype(F32)
    seg_local = (seg[...] - lax.axis_index("dp") * (seq_size * count)).astype(F32)
    seg_high = jnp.floor(seg_local * (1.0 / 64.0))
    last = jnp.concatenate([seg_high, seg_local - 64.0 * seg_high, jnp.zeros((14, LANES), F32)], axis=0)
    blocks = [jnp.concatenate([state[n], state[n + 1]], axis=0) for n in range(0, states, 2)]
    blocks += [jnp.concatenate([high, total - high], axis=0), last]
    for i, value in enumerate(blocks):
        value = value.astype(BF)
        for d in range(seq_size):
            o_msg[d, 16 * i : 16 * i + 16, :] = value


def total_step(msg, d, states):
    rows = msg[d, states * 8 : states * 8 + 16, :].astype(F32)
    return rows[:8] + rows[8:]


def state_rows(msg, d, n):
    rows = msg[d, 16 * (n // 2) : 16 * (n // 2) + 16, :].astype(F32)
    return rows[:8] if n % 2 == 0 else rows[8:]


def middle_kernel(
    msg, a_ref, bc, s_ref, dx_ref, mixed, gate, d_skip, tok, w_out, n2, w_qkv, grad_att,
    o_qkvg, o_start, o_ssm, o_after, o_gated, o_normed,
    y_ref,
):
    msg, a_ref = ready(msg, a_ref)
    states = a_ref.shape[0] // 8
    zero = jnp.zeros((8, LANES), F32)

    def join(d, carry):
        total = total_step(msg, d, states)
        return tuple(
            jnp.exp2(block(a_ref, n) * total) * carry[n] + state_rows(msg, d, n)
            for n in range(states)
        )

    start = lax.fori_loop(0, lax.axis_index("seq"), join, (zero,) * states)
    for n in range(states):
        o_start[8 * n : 8 * n + 8, :] = start[n]
    sent(o_start)
    s_ref, dx_ref, smem = ready(s_ref, dx_ref, bc)
    count = smem.shape[0]

    def one(t, state):
        s, dx = block(s_ref, t), block(dx_ref, t)
        state = tuple(
            jnp.exp2(s * block(a_ref, n)) * state[n] + dx * smem[t, n] for n in range(states)
        )
        parts = [state[n] * smem[t, states + n] for n in range(states)]
        while len(parts) > 1:
            parts = [a + b for a, b in zip(parts[::2], parts[1::2])]
        y_ref[pl.ds(pl.multiple_of(t * 8, 8), 8), :] = parts[0]
        return state

    lax.fori_loop(0, count, one, start, unroll=4)
    mixed, gate, d_skip, tok, w_out, n2 = ready(mixed, gate, d_skip, tok, w_out, n2)
    inner_width, width = mixed.shape[1], tok.shape[1]
    tiles = inner_width // LANES
    for j in range(tiles):
        ssm = from_rows(y_ref, j, count) + d_skip[:, tile(j)] * mixed[:, tile(j)].astype(F32)
        o_ssm[:, tile(j)] = ssm
        v = gate[:, tile(j)].astype(F32)
        o_gated[:, tile(j)] = (ssm * (v * jax.nn.sigmoid(v))).astype(BF)
    sent(o_ssm, o_gated)
    after = tok[...].astype(F32) + dot(o_gated[...], w_out[...])
    o_after[...] = after
    sent(o_after)
    normed = (after * rms_parts(after) * n2[...]).astype(BF)
    o_normed[...] = normed
    sent(o_normed)
    w_qkv, grad_att = ready(w_qkv, grad_att)
    qkv = dot(normed, w_qkv[...])
    copies = o_qkvg.shape[0] // H
    left = lax.broadcasted_iota(jnp.int32, (count, LANES), 1) < HD
    for p in range(H // 2):
        q, k, v = (qkv[:, i * width + p * LANES : i * width + (p + 1) * LANES] for i in range(3))
        g = grad_att[:, tile(p)].astype(F32)
        first = (jnp.where(left, q, pltpu.roll(k, HD, 1)), jnp.where(left, v, pltpu.roll(g, HD, 1)))
        second = (jnp.where(left, pltpu.roll(q, HD, 1), k), jnp.where(left, pltpu.roll(v, HD, 1), g))
        for h, pair in ((2 * p, first), (2 * p + 1, second)):
            for i, value in enumerate(pair):
                value = value.astype(BF)
                for r in range(copies):
                    o_qkvg[h * copies + r, :, tile(i)] = value


def grad_att_kernel(cot, w_proj, o_grad):
    cot, w_proj = ready(cot, w_proj)
    o_grad[...] = dot_nt(cot[...], w_proj[...]).astype(BF)


def attention_kernel(qkvg, ends, o_back, qz, kr, gz, vr, dk, dv):
    qkvg, ends = ready(qkvg, ends)
    seq_size, count = qkvg.shape[0], qkvg.shape[1]
    rows = seq_size * count
    left = lax.broadcasted_iota(jnp.int32, (count, LANES), 1) < HD
    for d in range(seq_size):
        at = slice(d * count, (d + 1) * count)
        a, b = qkvg[d, :, :LANES].astype(F32), qkvg[d, :, LANES:].astype(F32)
        qz[at, :] = jnp.where(left, a, 0.0).astype(BF)
        kr[at, :] = pltpu.roll(a, HD, 1).astype(BF)
        gz[at, :] = jnp.where(left, 0.0, b).astype(BF)
        vr[at, :] = pltpu.roll(b, HD, 1).astype(BF)
    dk[...] = jnp.zeros_like(dk)
    dv[...] = jnp.zeros_like(dv)
    scale = HD**-0.5

    def queries(b, length):
        at = pl.ds(b * count if isinstance(b, int) else pl.multiple_of(b * count, count), count)
        tail = ends[b].astype(F32)
        starts = jnp.broadcast_to(tail[0:1] * 64.0 + tail[1:2], (LANES, LANES))
        first = jnp.transpose(starts)[:, :1].astype(jnp.int32)
        column = lax.broadcasted_iota(jnp.int32, (count, length), 1)
        row = b * count + lax.broadcasted_iota(jnp.int32, (count, 1), 0)
        visible = (column <= row) & (column >= first)
        scores = jnp.where(visible, dot_nt(qz[at, :], kr[:length, :]) * scale, -1e30)
        weight = jnp.exp(scores - jnp.max(scores, axis=1, keepdims=True))
        probs = weight * (1.0 / jnp.sum(weight, axis=1, keepdims=True))
        low = probs.astype(BF)
        grad_probs = dot_nt(gz[at, :], vr[:length, :])
        delta = jnp.sum(probs * grad_probs, axis=1, keepdims=True)
        grad_scores = (probs * (grad_probs - delta)).astype(BF)
        dk[:length, :] += dot_tn(grad_scores, kr[at, :])
        dv[:length, :] += dot_tn(low, vr[at, :])
        dq = dot(grad_scores, kr[:length, :])
        attended = dot(low, vr[:length, :])
        o_back[b, :, :LANES] = (dq * scale).astype(BF)
        o_back[b, :, LANES:] = attended.astype(BF)

    if seq_size <= 8:
        for b in range(seq_size):
            queries(b, (b + 1) * count)
    else:
        lax.fori_loop(0, seq_size, lambda b, _: (queries(b, rows), 0)[1], 0)
    for d in range(seq_size):
        at = slice(d * count, (d + 1) * count)
        o_back[d, :, :LANES] = jnp.where(left, o_back[d, :, :LANES].astype(F32), dk[at, :] * scale).astype(BF)
        o_back[d, :, LANES:] = jnp.where(left, dv[at, :], o_back[d, :, LANES:].astype(F32)).astype(BF)


def backward_kernel(
    back, after, w_proj, w_qkv, n2, cot, w_out, gate, ssm, s_ref, a_ref, bc,
    o_out, o_after, o_branch, o_n2, o_gate, o_g, o_msg, o_attended, *o_more
):
    back = ready(back)
    seq_size, count = back.shape[0], back.shape[1]
    copies = seq_size // H
    left = lax.broadcasted_iota(jnp.int32, (count, LANES), 1) < HD
    dq, dk, dv, att = [], [], [], []
    for p in range(H // 2):
        a0, b0 = (back[2 * p * copies, :, tile(i)].astype(F32) for i in range(2))
        a1, b1 = (back[(2 * p + 1) * copies, :, tile(i)].astype(F32) for i in range(2))
        dq.append(jnp.where(left, a0, pltpu.roll(a1, HD, 1)))
        dk.append(jnp.where(left, pltpu.roll(a0, HD, 1), a1))
        dv.append(jnp.where(left, b0, pltpu.roll(b1, HD, 1)))
        att.append(jnp.where(left, pltpu.roll(b0, HD, 1), b1))
    attended = jnp.concatenate(att, axis=1).astype(BF)
    after, w_proj = ready(after, w_proj)
    width = after.shape[1]
    o_attended[...] = attended
    o_out[...] = (after[...] + dot(attended, w_proj[...])).astype(BF)
    sent(o_attended, o_out)
    w_qkv, n2, cot = ready(w_qkv, n2, cot)
    grad_qkv = jnp.concatenate(dq + dk + dv, axis=1).astype(BF)
    if o_more:
        o_more[0][...] = grad_qkv
    grad_x, grad_gain = rms_back(after[...], n2[...], dot_nt(grad_qkv, w_qkv[...]))
    o_n2[...] = jnp.sum(grad_gain, axis=0, keepdims=True)
    grad_after = cot[...].astype(F32) + grad_x
    o_after[...] = grad_after
    branch = grad_after.astype(BF)
    o_branch[...] = branch
    sent(o_n2, o_after, o_branch)
    w_out, gate, ssm = ready(w_out, gate, ssm)
    inner_width = gate.shape[1]
    tiles = inner_width // LANES
    a_ref = ready(a_ref)
    states = a_ref.shape[0] // 8
    grad_gated = dot_nt(branch, w_out[...])
    for j in range(tiles):
        v = gate[:, tile(j)].astype(F32)
        sig = jax.nn.sigmoid(v)
        grad = grad_gated[:, tile(j)]
        to_rows(o_g, j, grad * (v * sig))
        grad_gate = grad * ssm[:, tile(j)] * (sig * (1.0 + v * (1.0 - sig)))
        o_gate[:, tile(j)] = grad_gate.astype(BF)
    sent(o_gate, o_g)
    s_ref, smem = ready(s_ref, bc)

    def one(i, later):
        t = count - 1 - i
        s, g = block(s_ref, t), block(o_g, t)
        return tuple(
            jnp.exp2(s * block(a_ref, n)) * (g * smem[t, states + n] + later[n])
            for n in range(states)
        )

    leaving = lax.fori_loop(0, count, one, (jnp.zeros((8, LANES), F32),) * states, unroll=4)
    for n in range(0, states, 2):
        value = jnp.concatenate([leaving[n], leaving[n + 1]], axis=0).astype(BF)
        for d in range(seq_size):
            o_msg[d, 8 * n : 8 * n + 16, :] = value


def states_kernel(
    seq_size, start, a_ref, bc, s_ref, dx_ref, inner, conv_w, conv_b, seg, o_every, o_slope, ext
):
    start, a_ref, smem, s_ref, dx_ref = ready(start, a_ref, bc, s_ref, dx_ref)
    count = smem.shape[0]
    states = a_ref.shape[0] // 8
    o_every[: states * 8, :] = start[...]

    def again(t, state):
        s, dx = block(s_ref, t), block(dx_ref, t)
        state = tuple(
            jnp.exp2(s * block(a_ref, n)) * state[n] + dx * smem[t, n] for n in range(states)
        )
        for n in range(states):
            o_every[pl.ds(pl.multiple_of(((t + 1) * states + n) * 8, 8), 8), :] = state[n]
        return state

    lax.fori_loop(0, count, again, tuple(start[8 * n : 8 * n + 8, :] for n in range(states)), unroll=2)
    sent(o_every)
    inner, conv_w, conv_b, seg = ready(inner, conv_w, conv_b, seg)
    ext[...] = inner[...].astype(F32)
    offset = offsets_in_sequence(seg, seq_size)
    for j in range(o_slope.shape[1] // LANES):
        pre = conv_tile(ext, conv_w, conv_b, offset, j, count)
        sig = jax.nn.sigmoid(pre)
        o_slope[:, tile(j)] = sig * (1.0 + pre * (1.0 - sig))


def fold8(values, sub):
    low4, low2, low1 = sub < 4, (sub & 2) == 0, (sub & 1) == 0
    four = []
    for k in range(4):
        a, b = values[k], values[k + 4]
        four.append(jnp.where(low4, a, b) + pltpu.roll(jnp.where(low4, b, a), 4, 0))
    two = []
    for k in range(2):
        a, b = four[k], four[k + 2]
        two.append(jnp.where(low2, a + pltpu.roll(a, 6, 0), b + pltpu.roll(b, 2, 0)))
    a, b = two
    return jnp.where(low1, a + pltpu.roll(a, 7, 0), b + pltpu.roll(b, 1, 0))


def adjoint_kernel(
    seq_size, back, totals, a_ref, bc, s_ref, dx_ref, g_ref, every, gs_ref, ai_ref, o_bc, o_a, held, sums, arrived
):
    back, totals, a_ref = ready(back, totals, a_ref)
    states = a_ref.shape[0] // 8
    count = s_ref.shape[0] // 8
    zero = jnp.zeros((8, LANES), F32)
    chunks = arrived.shape[0]
    span = count // chunks
    loads = []
    for c in range(chunks):
        first, last = c * span * states * 8, ((c + 1) * span + (c == chunks - 1)) * states * 8
        loads.append(pltpu.make_async_copy(every.at[first:last], held.at[first:last], arrived.at[c]))
    for load in reversed(loads):
        load.start()

    def join(i, carry):
        d = seq_size - 1 - i
        total = total_step(totals, d, 0)
        return tuple(
            jnp.exp2(block(a_ref, n) * total) * carry[n] + state_rows(back, d, n)
            for n in range(states)
        )

    leaving = lax.fori_loop(0, seq_size - 1 - lax.axis_index("seq"), join, (zero,) * states)
    smem, s_ref, dx_ref, g_ref = ready(bc, s_ref, dx_ref, g_ref)
    sub = lax.broadcasted_iota(jnp.int32, (8, LANES), 0)

    def one(last, i, carry):
        later, grad_a = carry
        t = last - i
        s, dx, g = block(s_ref, t), block(dx_ref, t), block(g_ref, t)
        new_later, new_grad_a, with_b, with_c = [], [], [], []
        grad_step, adjoint_in = zero, zero
        for n in range(states):
            a = block(a_ref, n)
            adjoint = g * smem[t, states + n] + later[n]
            passed = jnp.exp2(s * a) * adjoint
            before = held[pl.ds(pl.multiple_of((t * states + n) * 8, 8), 8), :]
            now = held[pl.ds(pl.multiple_of(((t + 1) * states + n) * 8, 8), 8), :]
            grad_decay = passed * before
            grad_step = grad_step + grad_decay * a
            adjoint_in = adjoint_in + adjoint * smem[t, n]
            new_later.append(passed)
            new_grad_a.append(grad_a[n] + grad_decay * s)
            with_b.append(adjoint * dx)
            with_c.append(g * now)
        here = pl.ds(pl.multiple_of(t * 8, 8), 8)
        gs_ref[here, :] = grad_step
        ai_ref[here, :] = adjoint_in
        for i, part in enumerate((with_b[:8], with_b[8:], with_c[:8], with_c[8:])):
            sums[pl.ds(pl.multiple_of(t * 32 + 8 * i, 8), 8), :] = fold8(part, sub)
        return tuple(new_later), tuple(new_grad_a)

    carry = (leaving, (zero,) * states)
    for c in reversed(range(chunks)):
        loads[c].wait()
        carry = lax.fori_loop(0, span, functools.partial(one, (c + 1) * span - 1), carry, unroll=4)
    grad_a = carry[1]
    sent(gs_ref, ai_ref)
    for n in range(states):
        o_a[8 * n : 8 * n + 8, :] = grad_a[n] * (LN2 * block(a_ref, n))
    columns = o_bc.shape[1]
    lane = lax.broadcasted_iota(jnp.int32, (LANES, columns), 1)
    grad_bc = jnp.zeros(o_bc.shape, F32)
    for q in range(2 * states):
        rows = sums[pl.ds(q, count, stride=2 * states), :]
        high = rows.astype(BF)
        low = (rows - high.astype(F32)).astype(BF)
        to_column = (lane == columns - 2 * states + q).astype(BF)
        grad_bc = grad_bc + dot(high, to_column) + dot(low, to_column)
    o_bc[...] = grad_bc


def inner_kernel(
    seq_size, gs_ref, ai_ref, g_ref, mixed, step_pre, low, w_dt, grad_bc, grad_a, w_xp, inner, slope, conv_w, d_skip,
    seg, normed, grad_n2,
    *rest,
):
    o_first, o_second, o_inner, *own_small, ext, gext, grad_w = rest
    small = own_small[0] if own_small else o_second.ref
    gs_ref, ai_ref, g_ref = ready(gs_ref, ai_ref, g_ref)
    grad_bc, grad_a = ready(grad_bc, grad_a)
    count = g_ref.shape[0] // 8
    states = grad_a.shape[0] // 8
    mixed, step_pre, low, w_dt, w_xp, inner = ready(mixed, step_pre, low, w_dt, w_xp, inner)
    slope, conv_w, d_skip, seg, normed, grad_n2 = ready(slope, conv_w, d_skip, seg, normed, grad_n2)
    inner_width = mixed.shape[1]
    tiles = inner_width // LANES
    rank = w_dt.shape[0]
    taps = conv_w.shape[0]
    small[...] = jnp.zeros_like(small)
    small[104 * 8 : (104 + states) * 8, :] = grad_a[...]
    offset = offsets_in_sequence(seg, seq_size)
    halves = []
    for j in range(tiles):
        mix = mixed[:, tile(j)].astype(F32)
        pre = step_pre[:, tile(j)]
        grad_step = LN2 * from_rows(gs_ref, j, count) + mix * from_rows(ai_ref, j, count)
        grad_pre = grad_step * jax.nn.sigmoid(pre)
        small[101 * 8 + j : 101 * 8 + j + 1, :] = jnp.sum(grad_pre, axis=0, keepdims=True)
        grad_ssm = from_rows(g_ref, j, count)
        small[102 * 8 + j : 102 * 8 + j + 1, :] = jnp.sum(grad_ssm * mix, axis=0, keepdims=True)
        halves.append(grad_pre.astype(BF))
    half = jnp.concatenate(halves, axis=1)
    grad_w_dt = dot_tn(low[...], half)
    padded_dt = jnp.concatenate([w_dt[...], jnp.zeros((2 * states, inner_width), BF)], axis=0)
    grad_selector = (dot_nt(half, padded_dt) + grad_bc[...]).astype(BF)
    grad_w_xp = dot_tn(grad_selector, mixed[...])
    from_selector = dot(grad_selector, w_xp[...])
    ext[...] = inner[...].astype(F32)
    gext[...] = jnp.zeros_like(gext)
    for j in range(tiles):
        to_rows(small.at[pl.ds(0, 64 * 8)], j, grad_w_xp[:, tile(j)])
        to_rows(small.at[pl.ds(64 * 8, 32 * 8)], j, grad_w_dt[:, tile(j)])
        grad_mixed = (
            softplus(step_pre[:, tile(j)]) * from_rows(ai_ref, j, count)
            + from_rows(g_ref, j, count) * d_skip[:, tile(j)]
            + from_selector[:, tile(j)]
        )
        grad_pre = grad_mixed * slope[:, tile(j)]
        small[100 * 8 + j : 100 * 8 + j + 1, :] = jnp.sum(grad_pre, axis=0, keepdims=True)
        for k in range(taps):
            shifted = pl.ds(HALO - taps + 1 + k, count)
            usable = jnp.where(offset >= taps - 1 - k, grad_pre, 0.0)
            row = (96 + k) * 8 + j
            small[row : row + 1, :] = jnp.sum(usable * ext[shifted, tile(j)], axis=0, keepdims=True)
            gext[shifted, tile(j)] += conv_w[k : k + 1, tile(j)] * usable
    o_inner[...] = gext[...].astype(BF)
    sent(o_inner)
    width = grad_n2.shape[1]
    for j in range(width // LANES):
        small[103 * 8 + 4 + j : 103 * 8 + 5 + j, :] = grad_n2[:, tile(j)]
    if not own_small:
        o_first[...] = dot_tn(normed[...], o_inner[...])
        return
    grad_w[...] = dot_tn(normed[...], o_inner[...])
    for to, x, s, at in receivers((o_first, o_second), seq_size):
        to[x * seq_size + s, :LANES, :] = grad_w[pl.ds(pl.multiple_of(at * LANES, LANES), LANES), tile(s)].astype(BF)
        rows = small.shape[0] // (width // LANES * seq_size)
        here = pl.ds(pl.multiple_of((at * seq_size + s) * rows, rows), rows)
        to[x * seq_size + s, LANES:, :] = small[here, :].astype(BF)


def receivers(results, seq_size, mine=0):
    core = lax.rem(lax.axis_index("dp"), 2)
    for to, side in zip(results, (core, 1 - core)):
        for x in range(to.shape[0] // seq_size):
            for s in range(seq_size):
                yield to, x, s, 2 * lax.bitwise_xor(x, mine) + side


def partials_kernel(seq_size, gated, branch, normed, grad_gate, attended, cot, keep, send, out, gate, proj):
    gated, branch = ready(gated, branch)
    out[...] = dot_tn(gated[...], branch[...])
    normed, grad_gate = ready(normed, grad_gate)
    gate[...] = dot_tn(normed[...], grad_gate[...])
    attended, cot = ready(attended, cot)
    proj[...] = dot_tn(attended[...], cot[...])
    across = out.shape[1] // LANES
    down = seq_size // across
    mine = lax.axis_index("dp") // 2
    for to, x, s, at in receivers((keep, send), seq_size, mine):
        rows = pl.ds(pl.multiple_of((at * down + s // across) * LANES, LANES), LANES)
        to[x * seq_size + s, :LANES, :] = out[rows, tile(s % across)].astype(BF)
        rows = pl.ds(pl.multiple_of(at * LANES, LANES), LANES)
        to[x * seq_size + s, LANES : 2 * LANES, :] = gate[rows, tile(s)].astype(BF)
        rows = pl.ds(pl.multiple_of((at * down + s // across) * HD, HD), HD)
        to[x * seq_size + s, 2 * LANES :, :] = proj[rows, tile(s % across)].astype(BF)


def tokens_kernel(grad_inner, w_in, grad_gate, tok, halo, n1, grad_after, o_tok, o_halo, o_n1):
    grad_inner, w_in, grad_gate = ready(grad_inner, w_in, grad_gate)
    inner_width = grad_inner.shape[1]
    grad_normed = dot_nt(grad_inner[...], w_in[:, :inner_width])
    own = dot_nt(grad_gate[...], w_in[:, inner_width:])
    grad_normed = jnp.concatenate([grad_normed[:HALO], grad_normed[HALO:] + own], axis=0)
    tok, halo, n1, grad_after = ready(tok, halo, n1, grad_after)
    x = jnp.concatenate([halo[...], tok[...]], axis=0).astype(F32)
    grad_x, grad_gain = rms_back(x, n1[...], grad_normed)
    o_tok[...] = grad_after[...] + grad_x[HALO:]
    o_halo[...] = grad_x[HALO - 8 : HALO]
    grad_gain = jnp.sum(grad_gain, axis=0, keepdims=True)
    tiles = grad_gain.shape[1] // LANES
    rows = [grad_gain[:, tile(j)] for j in range(tiles)] + [jnp.zeros((16 - tiles, LANES), F32)]
    o_n1[...] = jnp.concatenate(rows, axis=0).astype(BF)


def head_products_kernel(normed, back, keep, send, grad, last):
    normed, back = ready(normed, back)
    both = back[...].reshape(back.shape[0] * back.shape[1], 2 * LANES)
    grad[...] = dot_tn(normed[...], both[:, :LANES])
    last[...] = dot_tn(normed[...], both[:, LANES:])
    left = lax.broadcasted_iota(jnp.int32, (HD, LANES), 1) < HD
    for to, x, _, at in receivers((keep, send), 1, lax.axis_index("dp") // 2):
        to[x, : 2 * HD, :] = grad[pl.ds(pl.multiple_of(at * LANES, LANES), LANES), :].astype(BF)
        low = last[pl.ds(pl.multiple_of(at * LANES, LANES), HD), :]
        high = last[pl.ds(pl.multiple_of(at * LANES + HD, HD), HD), :]
        to[x, 2 * HD :, :] = jnp.where(left, low, pltpu.roll(high, HD, 1)).astype(BF)


def head_middle_kernel(keep, received, near, far):
    keep, received = ready(keep, received)
    near[...] = (keep[0].astype(F32) + received[0].astype(F32)).astype(BF)
    far[...] = (keep[1].astype(F32) + received[1].astype(F32)).astype(BF)


def early_sum_kernel(parts, *heads):
    *heads, o_sum = heads
    heads, parts = ready(*heads), ready(parts)
    head = heads[0][...].astype(F32)
    for part in heads[1:]:
        head = head + part[...].astype(F32)
    total = parts[0].astype(F32)
    for d in range(1, parts.shape[0]):
        total = total + parts[d].astype(F32)
    rows = total.shape[0]
    o_sum[:rows, :] = total.astype(BF)
    o_sum[rows:, :] = head.astype(BF)


def sum_and_spread_kernel(parts, own, o_all):
    parts, own = ready(parts, own)
    total = parts[0].astype(F32)
    for d in range(1, parts.shape[0]):
        total = total + parts[d].astype(F32)
    total = total.astype(BF)
    rows = total.shape[0]
    for d in range(o_all.shape[0]):
        o_all[d, :rows, :] = total
        o_all[d, rows:, :] = own[...]


def early_assembly_kernel(groups, early, w_in, o_out, o_proj, o_qkv, o_in, pieces, out, proj, qkv, gate, loads, stores):
    seq_size = early.shape[0] // groups
    inner_width, width = gate.shape[1], proj.shape[1]
    across = width // LANES
    left = lax.broadcasted_iota(jnp.int32, (LANES, LANES), 1) < HD
    at = 2 * LANES + HD

    def pairs(a, b):
        a, b = a.astype(F32), b.astype(F32)
        mask = left[: a.shape[0]]
        return jnp.where(mask, a, pltpu.roll(b, HD, 1)), jnp.where(mask, pltpu.roll(a, HD, 1), b)

    own = [slice(g * seq_size, (g + 1) * seq_size) for g in range(groups)]
    arrivals = [pltpu.make_async_copy(early.at[own[g]], pieces.at[own[g]], loads.at[g]) for g in range(groups)]
    for copy in arrivals:
        copy.start()
    copies = []
    for g in range(groups):
        arrivals[g].wait()
        down = seq_size // across
        for s in range(seq_size):
            piece = pieces[g * seq_size + s]
            row = g * down + s // across
            out[tile(row), tile(s % across)] = piece[:LANES].astype(F32)
            gate[tile(g), tile(s)] = piece[LANES : 2 * LANES].astype(F32)
            proj[row * HD : (row + 1) * HD, tile(s % across)] = piece[2 * LANES : at].astype(F32)
        for p in range(seq_size // 2):
            a, b = pieces[g * seq_size + 2 * p], pieces[g * seq_size + 2 * p + 1]
            first, second, third = (slice(i * width + p * LANES, i * width + (p + 1) * LANES) for i in range(3))
            qkv[tile(g), first], qkv[tile(g), second] = pairs(a[at : at + LANES], b[at : at + LANES])
            low, high = pairs(a[at + LANES :], b[at + LANES :])
            qkv[g * LANES : g * LANES + HD, third] = low
            qkv[g * LANES + HD : (g + 1) * LANES, third] = high
        for i, (source, target, rows) in enumerate(
            ((out, o_out, down * LANES), (proj, o_proj, down * HD), (qkv, o_qkv, LANES), (gate, o_in, LANES))
        ):
            here = slice(g * rows, (g + 1) * rows)
            target = target.at[here, inner_width:] if i == 3 else target.at[here]
            copies.append(pltpu.make_async_copy(source.at[here], target, stores.at[4 * g + i]))
            copies[-1].start()
    for copy in copies:
        copy.wait()


def late_assembly_kernel(
    groups, mine, other, o_in, o_n1, o_conv_w, o_conv_b, o_xp, o_dt, o_dtb, o_a, o_skip, o_n2, inner, small, sems
):
    mine, other = ready(mine, other)
    seq_size = mine.shape[0] * 2 // groups
    width, inner_width = inner.shape
    rows = mine.shape[1] - LANES - 16
    copies = []
    for ref, x, s, g in receivers((mine, other), seq_size):
        at = pl.ds(pl.multiple_of(g * LANES, LANES), LANES)
        inner[at, tile(s)] = ref[x * seq_size + s, :LANES, :].astype(F32)
        here = pl.ds(pl.multiple_of((g * seq_size + s) * rows, rows), rows)
        small[here, :] = ref[x * seq_size + s, LANES : LANES + rows, :].astype(F32)
        if s == seq_size - 1:
            copies.append(pltpu.make_async_copy(inner.at[at], o_in.at[at, :inner_width], sems.at[len(copies)]))
            copies[-1].start()
    for j in range(inner_width // LANES):
        value = from_rows(small, j, SMALL)
        for ref, first, last in (
            (o_xp, 0, 64), (o_dt, 64, 96), (o_conv_w, 96, 100), (o_conv_b, 100, 101), (o_dtb, 101, 102),
            (o_skip, 102, 103), (o_a, 104, 120),
        ):
            ref[:, tile(j)] = value[first:last]
        if j >= width // LANES:
            o_n2[:, tile(j - width // LANES)] = value[103:104]
    sent(o_conv_w, o_conv_b, o_xp, o_dt, o_dtb, o_a, o_skip, o_n2)
    gain = jnp.zeros((16, LANES), F32)
    for source in (mine, other):
        for d in range(source.shape[0]):
            gain = gain + source[d, LANES + rows :, :].astype(F32)
    for j in range(width // LANES):
        o_n1[:, tile(j)] = gain[j : j + 1]
    for copy in copies:
        copy.wait()


class Held:
    def __init__(self, buffer, copy):
        self.ref, self.copy, self.shape = buffer, copy, buffer.shape
        self.done = False

    def __getitem__(self, at):
        return self.ref[at]

    def __setitem__(self, at, value):
        self.ref[at] = value


def ready(*held):
    for one in held:
        if not one.done:
            one.copy.wait()
            one.done = True
    refs = tuple(one.ref for one in held)
    return refs[0] if len(refs) == 1 else refs


def sent(*held):
    for one in held:
        if not one.done:
            one.copy.start()
            one.done = True


IN_HBM = pl.BlockSpec(memory_space=pltpu.HBM)


def call(
    kernel, outs, scratch, *args, name=None, us=1, raw=(), raw_out=(), scalars=(), views=None, aliases=None, after=(),
    near=(), vmem=60,
):
    views = views or {}
    count, first_out = len(args), len(args) + len(after)
    first_scratch = first_out + len(outs)
    buffers = []
    for i, arg in enumerate(args):
        shape = jax.eval_shape(lambda v, i=i: v[views[i]], arg).shape if i in views else arg.shape
        kind = pltpu.SMEM if i in scalars else pltpu.VMEM
        buffers.append(None if i in raw else kind(shape, arg.dtype))
    for i, (shape, dtype) in enumerate(outs):
        buffers.append(None if i in raw_out else pltpu.VMEM(shape, dtype))
    used = [b for b in buffers if b is not None]

    def run(*refs):
        given = list(refs[:count]) + list(refs[first_out:first_scratch])
        own = list(refs[first_scratch : first_scratch + len(used)])
        sems = refs[first_scratch + len(used)]
        passed = []
        for i, (ref, buffer) in enumerate(zip(given, buffers)):
            if buffer is None:
                passed.append(ref)
                continue
            buffer = own.pop(0)
            if i < count:
                source = ref.at[views[i]] if i in views else ref
                copy = pltpu.make_async_copy(source, buffer, sems.at[i])
                copy.start()
            else:
                copy = pltpu.make_async_copy(buffer, ref, sems.at[i])
            passed.append(Held(buffer, copy))
        kernel(*passed, *refs[first_scratch + len(used) + 1 :])
        ready(*[p for p in passed[:count] if isinstance(p, Held)])
        results = [p for p in passed[count:] if isinstance(p, Held)]
        sent(*results)
        for result in results:
            result.copy.wait()

    return pl.pallas_call(
        run,
        out_shape=[jax.ShapeDtypeStruct(s, d) for s, d in outs],
        in_specs=[pl.BlockSpec(memory_space=pl.ANY) if i in near else IN_HBM for i in range(first_out)],
        out_specs=[IN_HBM] * len(outs),
        scratch_shapes=used + [pltpu.SemaphoreType.DMA((len(buffers),))] + scratch,
        compiler_params=pltpu.CompilerParams(vmem_limit_bytes=vmem * 1024 * 1024),
        cost_estimate=pl.CostEstimate(flops=us * 10**9 + 1000, bytes_accessed=1000, transcendentals=0),
        input_output_aliases=aliases or {},
        name=name,
    )(*args, *after)


def exchange(value, axes):
    return lax.all_to_all(value, axes, 0, 0, tiled=True)


def own_core(value, groups, seq_size):
    peers = [
        [g * seq_size + s for g in range(core, groups, 2) for s in range(seq_size)] for core in range(2)
    ]
    return lax.all_to_all(value, ("dp", "seq"), 0, 0, tiled=True, axis_index_groups=peers)


def other_core(value, groups):
    return lax.ppermute(value, "dp", [(g, g ^ 1) for g in range(groups)])


def body(
    tokens, seg_start, norm_one, w_in, conv_w, conv_b, w_xproj, w_dt, dt_bias, a_log, d_skip,
    w_out, norm_two, w_qkv, w_proj, cotangent,
):
    count, width = tokens.shape
    inner_width = w_in.shape[1] // 2
    states = a_log.shape[1]
    rank = w_dt.shape[0]
    taps = conv_w.shape[0]
    groups, seq_size = lax.axis_size("dp"), lax.axis_size("seq")
    rows = count * seq_size
    ext_rows = HALO + count
    tiled = inner_width == seq_size * LANES and width == groups * LANES and seq_size == H
    peers = groups // 2 * seq_size
    line = lambda v: v.reshape(1, -1)
    seg = line(seg_start)
    n1, n2, cb, dtb, skip = (line(v) for v in (norm_one, norm_two, conv_b, dt_bias, d_skip))
    vmem, smem = pltpu.VMEM, pltpu.SMEM((count, 2 * states), F32)
    sem = pltpu.SemaphoreType.DMA
    blocks = ((count * 8, LANES), F32)
    ends_at = states * 8
    halo = lax.ppermute(tokens[count - HALO :], "seq", [(i, i + 1) for i in range(seq_size - 1)])
    msg, normed, inner, gate, mixed, bc, low, step_pre, s, dx, a = call(
        functools.partial(forward_kernel, seq_size),
        [
            ((seq_size, states * 8 + 32, LANES), BF), ((ext_rows, width), BF),
            ((ext_rows, inner_width), BF), ((count, inner_width), BF), ((count, inner_width), BF), ((count, 2 * states), F32),
            ((count, rank), BF), ((count, inner_width), F32), blocks, blocks, ((states * 8, LANES), F32),
        ],
        [vmem((ext_rows, inner_width), F32), smem, sem],
        tokens, halo, n1, w_in, conv_w, cb, w_xproj.T, w_dt, dtb, a_log.T, seg,
        name="forward", us=0, near=(1,),
    )
    msg = exchange(msg, "seq")
    (grad_att,) = call(
        grad_att_kernel, [((count, width), BF)], [], cotangent, w_proj, name="grad_att", us=0
    )
    qkvg, start, ssm, after, gated, normed_two = call(
        middle_kernel,
        [
            ((seq_size, count, 2 * LANES), BF), ((states * 8, LANES), F32), ((count, inner_width), F32),
            ((count, width), F32), ((count, inner_width), BF), ((count, width), BF),
        ],
        [vmem(*blocks)],
        msg, a, bc, s, dx, mixed, gate, skip, tokens, w_out, n2, w_qkv, grad_att,
        name="middle", us=0, scalars=(2,), views={0: np.s_[:, : ends_at + 16, :]}, near=(0,),
    )
    qkvg = exchange(qkvg, "seq")
    every, slope = call(
        functools.partial(states_kernel, seq_size),
        [(((count + 1) * states * 8, LANES), F32), ((count, inner_width), F32)],
        [vmem((ext_rows, inner_width), F32)],
        start, a, bc, s, dx, inner, conv_w, cb, seg, name="states", us=0, scalars=(2,),
    )
    (back,) = call(
        attention_kernel,
        [((seq_size, count, 2 * LANES), BF)],
        [vmem((rows, LANES), BF)] * 4 + [vmem((rows, LANES), F32)] * 2,
        qkvg, msg, name="attention", us=0, views={1: np.s_[:, ends_at + 16 :, :]}, after=(every,), near=(0,),
    )
    back_own = exchange(back, "seq")
    out, grad_after, branch, grad_n2, grad_gate, g, adj, attended, *more = call(
        backward_kernel,
        [
            ((count, width), BF), ((count, width), F32), ((count, width), BF), ((1, width), F32),
            ((count, inner_width), BF), blocks, ((seq_size, states * 8, LANES), BF),
            ((count, width), BF),
        ] + ([] if tiled else [((count, 3 * width), BF)]),
        [],
        back_own, after, w_proj, w_qkv, n2, cotangent, w_out, gate, ssm, s, a, bc,
        name="backward", us=0, scalars=(11,), near=(0,),
    )
    adj = exchange(adj, "seq")
    between = ()
    if tiled:
        normed_two_all = lax.all_gather(normed_two, "seq", axis=0, tiled=True)
        keep, send = call(
            functools.partial(partials_kernel, seq_size), [((peers, 2 * LANES + HD, LANES), BF)] * 2,
            [vmem((inner_width, width), F32), vmem((width, inner_width), F32), vmem((width, width), F32)],
            gated, branch, normed, grad_gate, attended, cotangent, name="partials", us=0, views={2: np.s_[HALO:, :]},
        )
        add = lambda *parts: sum(part.astype(F32) for part in parts).astype(BF)
        received = other_core(send, groups)
        across = add(keep[seq_size:], received[seq_size:])
        across = lax.ppermute(across, "dp", [(g, g ^ 2) for g in range(groups)])
        part = add(keep[:seq_size], received[:seq_size], across)
        between = (part,)
        part = exchange(part, "seq")
    gs, ai, grad_bc, grad_a = call(
        functools.partial(adjoint_kernel, seq_size),
        [blocks, blocks, ((count, rank + 2 * states), F32), ((states * 8, LANES), F32)],
        [vmem(((count + 1) * states * 8, LANES), F32), vmem((count * 2 * states, LANES), F32), sem((8,))],
        adj, msg, a, bc, s, dx, g, every, name="adjoint", us=0, raw=(7,), scalars=(3,), near=(0,),
        views={1: np.s_[:, ends_at : ends_at + 16, :]}, after=between,
    )
    small_rows = SMALL * 8 // (groups * seq_size)
    *sums, small, grad_inner = call(
        functools.partial(inner_kernel, seq_size),
        ([((peers, LANES + small_rows, LANES), BF)] * 2 if tiled else [((width, inner_width), F32), ((SMALL * 8, LANES), F32)])
        + [((ext_rows, inner_width), BF)],
        ([vmem((SMALL * 8, LANES), F32)] if tiled else [])
        + [vmem((ext_rows, inner_width), F32), vmem((ext_rows, inner_width), F32), vmem((width, inner_width), F32)],
        gs, ai, g, mixed, step_pre, low, w_dt, grad_bc, grad_a, w_xproj.T, inner, slope, conv_w, skip, seg, normed, grad_n2,
        name="inner", us=0,
    )
    grad_tokens, grad_halo, grad_n1 = call(
        tokens_kernel, [((count, width), F32), ((8, width), F32), ((16, LANES), BF)], [],
        grad_inner, w_in, grad_gate, tokens, halo, n1, grad_after, name="tokens", us=0,
    )
    returned = lax.ppermute(grad_halo, "seq", [(i + 1, i) for i in range(seq_size - 1)])
    grad_tokens = grad_tokens.at[count - 8 :].add(returned)
    flat = lambda v: v.reshape(-1)
    if tiled:
        late = add(sums[0], other_core(small, groups))
        late = own_core(late, groups, seq_size)
        keep, send = call(
            head_products_kernel, [((groups // 2, 3 * HD, LANES), BF)] * 2, [vmem((width, LANES), F32)] * 2,
            normed_two_all, back, name="head_products", us=0, after=(grad_n1,),
        )
        head, far = call(
            head_middle_kernel, [((3 * HD, LANES), BF)] * 2, [], keep, other_core(send, groups), name="head_middle", us=0,
            near=(1,),
        )
        heads = [lax.ppermute(far, "dp", [(g, g ^ 2) for g in range(groups)])]
        (early,) = call(
            early_sum_kernel, [((part.shape[1] + head.shape[0], LANES), BF)], [], part, head, *heads,
            name="early_sum", us=0, after=(grad_n1,), near=(0, 2),
        )
        early = lax.all_gather(early, ("dp", "seq"))
        (late,) = call(
            sum_and_spread_kernel, [((peers, late.shape[1] + 16, LANES), BF)], [], late, grad_n1, name="late_sum", us=0,
            near=(0,),
        )
        mine = own_core(late, groups, seq_size)
        mine, grad_tokens = lax.optimization_barrier((mine, grad_tokens))
        row = lambda n: ((n, inner_width), F32)
        half, g_n1, g_conv_w, g_conv_b, g_xp, g_dt, g_dtb, g_a, g_skip, g_n2 = call(
            functools.partial(late_assembly_kernel, groups),
            [
                ((width, 2 * inner_width), F32), ((1, width), F32), row(taps), row(1), row(2 * states + rank), row(rank),
                row(1), row(states), row(1), ((1, width), F32),
            ],
            [vmem((width, inner_width), F32), vmem((SMALL * 8, LANES), F32), sem((4,))],
            mine, other_core(mine, groups), name="late_assembly", us=0, raw_out=(0,), near=(0, 1),
        )
        whole = [((inner_width, width), F32), ((width, width), F32), ((width, 3 * width), F32)]
        grad_w_out, grad_w_proj, grad_w_qkv, grad_w_in = call(
            functools.partial(early_assembly_kernel, groups),
            whole + [((width, 2 * inner_width), F32)],
            [vmem(early.shape, BF)] + [vmem(*v) for v in whole] + [vmem((width, inner_width), F32), sem((4,)), sem((16,))],
            early, half, name="early_assembly", us=0, raw=(0, 1), raw_out=(0, 1, 2, 3), aliases={1: 3},
        )
        g_xp, g_a, g_n1, g_n2 = g_xp.T, g_a.T, flat(g_n1), flat(g_n2)
    else:
        (grad_qkv,) = more
        small = small.reshape(SMALL, inner_width)
        g_n1 = flat(grad_n1[: width // LANES].astype(F32))
        both = jnp.concatenate([sums[0], dot_tn(normed[HALO:], grad_gate)], axis=1)
        grad_w_in, grad_w_out, grad_w_qkv, grad_w_proj, small, g_n1 = lax.psum(
            (both, dot_tn(gated, branch), dot_tn(normed_two, grad_qkv), dot_tn(attended, cotangent), small, g_n1), ("dp", "seq")
        )
        g_xp, g_dt, g_conv_w, g_conv_b, g_dtb = small[:64].T, small[64:96], small[96:100], small[100], small[101]
        g_skip, g_n2, g_a = small[102], small[103, width:], small[104:120].T
    return (out, grad_tokens, g_n1, grad_w_in, g_conv_w, flat(g_conv_b), g_xp, g_dt, flat(g_dtb), g_a, flat(g_skip),
            grad_w_out, g_n2, grad_w_qkv, grad_w_proj)


def solution(mesh):
    split, copied = P(("dp", "seq"), None), P()
    return jax.shard_map(
        body,
        mesh=mesh,
        in_specs=(split, P(("dp", "seq"))) + (copied,) * 13 + (split,),
        out_specs=(split, split) + (copied,) * 13,
        check_vma=False,
    )
```

```python
import functools

import jax
import jax.numpy as jnp
import numpy as np
from jax import lax
from jax.experimental import pallas as pl
from jax.experimental.pallas import tpu as pltpu
from jax.sharding import PartitionSpec as P

H = 8
HD = 64
LANES = 128
HALO = 16
SMALL = 128
RESET = 1e30
EPSILON = 1e-05
LOG2E = 1.4426950408889634
LN2 = 0.6931471805599453
BF = jnp.bfloat16
F32 = jnp.float32


def dot(a, b):
    return jnp.dot(a, b, preferred_element_type=F32)


def dot_nt(a, b):
    return lax.dot_general(a, b, (((1,), (1,)), ((), ())), preferred_element_type=F32)


def dot_tn(a, b):
    return lax.dot_general(a, b, (((0,), (0,)), ((), ())), preferred_element_type=F32)


def tile(j):
    return slice(j * LANES, (j + 1) * LANES)


def softplus(x):
    u = jnp.exp(-jnp.abs(x))
    series = u * (1.0 - u * (0.5 - u * (1.0 / 3.0 - u * 0.25)))
    return jnp.maximum(x, 0.0) + jnp.where(u < 0.015, series, jnp.log(1.0 + u))


def rms_parts(x):
    return lax.rsqrt(jnp.mean(x * x, axis=-1, keepdims=True) + EPSILON)


def rms_back(x, gain, grad):
    r = rms_parts(x)
    scaled = grad * gain
    inner = jnp.mean(x * scaled, axis=-1, keepdims=True)
    return r * scaled - x * (r * r * r * inner), grad * x * r


def to_rows(ref, j, value):
    ref[pl.ds(j, value.shape[0], stride=8), :] = value


def from_rows(ref, j, count):
    return ref[pl.ds(j, count, stride=8), :]


def block(ref, t):
    return ref[pl.ds(pl.multiple_of(t * 8, 8), 8), :]


def offsets_in_sequence(seg_ref, seq_size):
    count = seg_ref.shape[1]
    base = (lax.axis_index("dp") * seq_size + lax.axis_index("seq")) * count
    places = base + lax.broadcasted_iota(jnp.int32, (1, count), 1)
    row = (places - seg_ref[...]).astype(F32)
    return jnp.transpose(jnp.broadcast_to(row, (LANES, count)))


def conv_tile(ext_ref, w_ref, b_ref, offset, j, count):
    taps = w_ref.shape[0]
    pre = jnp.broadcast_to(b_ref[:, tile(j)], (count, LANES))
    for k in range(taps):
        rows = ext_ref[pl.ds(HALO - taps + 1 + k, count), tile(j)]
        pre = pre + jnp.where(offset >= taps - 1 - k, w_ref[k : k + 1, tile(j)] * rows, 0.0)
    return pre


def forward_kernel(
    seq_size, tok, halo, n1, w_in, conv_w, conv_b, w_xp, w_dt, dtb, a_log, seg,
    o_msg, o_normed, o_inner, o_gate, o_mixed, o_bc, o_low, o_pre, o_s, o_dx, o_a,
    ext, smem, sem,
):
    tok, halo, n1, seg = ready(tok, halo, n1, seg)
    count = tok.shape[0]
    states = a_log.shape[0]
    inner_width = conv_w.shape[1]
    tiles = inner_width // LANES
    rank = w_dt.shape[0]
    x = jnp.concatenate([halo[...], tok[...]], axis=0).astype(F32)
    normed = (x * rms_parts(x) * n1[...]).astype(BF)
    o_normed[...] = normed
    sent(o_normed)
    w_in = ready(w_in)
    inner = dot(normed, w_in[:, :inner_width]).astype(BF)
    o_inner[...] = inner
    sent(o_inner)
    ext[...] = inner.astype(F32)
    o_gate[...] = dot(normed[HALO:], w_in[:, inner_width:]).astype(BF)
    sent(o_gate)
    conv_w, conv_b, w_xp, w_dt, dtb, a_log = ready(conv_w, conv_b, w_xp, w_dt, dtb, a_log)
    offset = offsets_in_sequence(seg, seq_size)
    for j in range(tiles):
        pre = conv_tile(ext, conv_w, conv_b, offset, j, count)
        o_mixed[:, tile(j)] = (pre * jax.nn.sigmoid(pre)).astype(BF)
    sent(o_mixed)
    selector = dot_nt(o_mixed[...], w_xp[...])
    low = selector[:, :rank].astype(BF)
    o_low[...] = low
    o_bc[...] = selector[:, rank:]
    sent(o_low, o_bc)
    copy = pltpu.make_async_copy(o_bc.ref, smem, sem)
    copy.start()
    o_pre[...] = dot(low, w_dt[...]) + dtb[...]
    sent(o_pre)
    for j in range(tiles):
        step = softplus(o_pre[:, tile(j)])
        to_rows(o_s, j, jnp.where(offset == 0.0, RESET, step))
        to_rows(o_dx, j, step * o_mixed[:, tile(j)].astype(F32))
        to_rows(o_a, j, -LOG2E * jnp.exp(a_log[:, tile(j)]))
    sent(o_s, o_dx, o_a)
    copy.wait()

    def one(t, carry):
        total, state = carry
        s, dx = block(o_s, t), block(o_dx, t)
        return total + s, tuple(
            jnp.exp2(s * block(o_a, n)) * state[n] + dx * smem[t, n] for n in range(states)
        )

    zero = jnp.zeros((8, LANES), F32)
    total, state = lax.fori_loop(0, count, one, (zero, (zero,) * states), unroll=4)
    high = total.astype(BF).astype(F32)
    seg_local = (seg[...] - lax.axis_index("dp") * (seq_size * count)).astype(F32)
    seg_high = jnp.floor(seg_local * (1.0 / 64.0))
    last = jnp.concatenate([seg_high, seg_local - 64.0 * seg_high, jnp.zeros((14, LANES), F32)], axis=0)
    blocks = [jnp.concatenate([state[n], state[n + 1]], axis=0) for n in range(0, states, 2)]
    blocks += [jnp.concatenate([high, total - high], axis=0), last]
    for i, value in enumerate(blocks):
        value = value.astype(BF)
        for d in range(seq_size):
            o_msg[d, 16 * i : 16 * i + 16, :] = value


def total_step(msg, d, states):
    rows = msg[d, states * 8 : states * 8 + 16, :].astype(F32)
    return rows[:8] + rows[8:]


def state_rows(msg, d, n):
    rows = msg[d, 16 * (n // 2) : 16 * (n // 2) + 16, :].astype(F32)
    return rows[:8] if n % 2 == 0 else rows[8:]


def middle_kernel(
    msg, a_ref, bc, s_ref, dx_ref, mixed, gate, d_skip, tok, w_out, n2, w_qkv, grad_att,
    o_qkvg, o_start, o_ssm, o_after, o_gated, o_normed,
    y_ref,
):
    msg, a_ref = ready(msg, a_ref)
    states = a_ref.shape[0] // 8
    zero = jnp.zeros((8, LANES), F32)

    def join(d, carry):
        total = total_step(msg, d, states)
        return tuple(
            jnp.exp2(block(a_ref, n) * total) * carry[n] + state_rows(msg, d, n)
            for n in range(states)
        )

    start = lax.fori_loop(0, lax.axis_index("seq"), join, (zero,) * states)
    for n in range(states):
        o_start[8 * n : 8 * n + 8, :] = start[n]
    sent(o_start)
    s_ref, dx_ref, smem = ready(s_ref, dx_ref, bc)
    count = smem.shape[0]

    def one(t, state):
        s, dx = block(s_ref, t), block(dx_ref, t)
        state = tuple(
            jnp.exp2(s * block(a_ref, n)) * state[n] + dx * smem[t, n] for n in range(states)
        )
        parts = [state[n] * smem[t, states + n] for n in range(states)]
        while len(parts) > 1:
            parts = [a + b for a, b in zip(parts[::2], parts[1::2])]
        y_ref[pl.ds(pl.multiple_of(t * 8, 8), 8), :] = parts[0]
        return state

    lax.fori_loop(0, count, one, start, unroll=4)
    mixed, gate, d_skip, tok, w_out, n2 = ready(mixed, gate, d_skip, tok, w_out, n2)
    inner_width, width = mixed.shape[1], tok.shape[1]
    tiles = inner_width // LANES
    for j in range(tiles):
        ssm = from_rows(y_ref, j, count) + d_skip[:, tile(j)] * mixed[:, tile(j)].astype(F32)
        o_ssm[:, tile(j)] = ssm
        v = gate[:, tile(j)].astype(F32)
        o_gated[:, tile(j)] = (ssm * (v * jax.nn.sigmoid(v))).astype(BF)
    sent(o_ssm, o_gated)
    after = tok[...].astype(F32) + dot(o_gated[...], w_out[...])
    o_after[...] = after
    sent(o_after)
    normed = (after * rms_parts(after) * n2[...]).astype(BF)
    o_normed[...] = normed
    sent(o_normed)
    w_qkv, grad_att = ready(w_qkv, grad_att)
    qkv = dot(normed, w_qkv[...])
    copies = o_qkvg.shape[0] // H
    left = lax.broadcasted_iota(jnp.int32, (count, LANES), 1) < HD
    for p in range(H // 2):
        q, k, v = (qkv[:, i * width + p * LANES : i * width + (p + 1) * LANES] for i in range(3))
        g = grad_att[:, tile(p)].astype(F32)
        first = (jnp.where(left, q, pltpu.roll(k, HD, 1)), jnp.where(left, v, pltpu.roll(g, HD, 1)))
        second = (jnp.where(left, pltpu.roll(q, HD, 1), k), jnp.where(left, pltpu.roll(v, HD, 1), g))
        for h, pair in ((2 * p, first), (2 * p + 1, second)):
            for i, value in enumerate(pair):
                value = value.astype(BF)
                for r in range(copies):
                    o_qkvg[h * copies + r, :, tile(i)] = value


def grad_att_kernel(cot, w_proj, o_grad):
    cot, w_proj = ready(cot, w_proj)
    o_grad[...] = dot_nt(cot[...], w_proj[...]).astype(BF)


def attention_kernel(qkvg, ends, o_back, qz, kr, gz, vr, dk, dv):
    qkvg, ends = ready(qkvg, ends)
    seq_size, count = qkvg.shape[0], qkvg.shape[1]
    rows = seq_size * count
    left = lax.broadcasted_iota(jnp.int32, (count, LANES), 1) < HD
    for d in range(seq_size):
        at = slice(d * count, (d + 1) * count)
        a, b = qkvg[d, :, :LANES].astype(F32), qkvg[d, :, LANES:].astype(F32)
        qz[at, :] = jnp.where(left, a, 0.0).astype(BF)
        kr[at, :] = pltpu.roll(a, HD, 1).astype(BF)
        gz[at, :] = jnp.where(left, 0.0, b).astype(BF)
        vr[at, :] = pltpu.roll(b, HD, 1).astype(BF)
    dk[...] = jnp.zeros_like(dk)
    dv[...] = jnp.zeros_like(dv)
    scale = HD**-0.5

    def queries(b, length):
        at = pl.ds(b * count if isinstance(b, int) else pl.multiple_of(b * count, count), count)
        tail = ends[b].astype(F32)
        starts = jnp.broadcast_to(tail[0:1] * 64.0 + tail[1:2], (LANES, LANES))
        first = jnp.transpose(starts)[:, :1].astype(jnp.int32)
        column = lax.broadcasted_iota(jnp.int32, (count, length), 1)
        row = b * count + lax.broadcasted_iota(jnp.int32, (count, 1), 0)
        visible = (column <= row) & (column >= first)
        scores = jnp.where(visible, dot_nt(qz[at, :], kr[:length, :]) * scale, -1e30)
        weight = jnp.exp(scores - jnp.max(scores, axis=1, keepdims=True))
        probs = weight * (1.0 / jnp.sum(weight, axis=1, keepdims=True))
        low = probs.astype(BF)
        grad_probs = dot_nt(gz[at, :], vr[:length, :])
        delta = jnp.sum(probs * grad_probs, axis=1, keepdims=True)
        grad_scores = (probs * (grad_probs - delta)).astype(BF)
        dk[:length, :] += dot_tn(grad_scores, kr[at, :])
        dv[:length, :] += dot_tn(low, vr[at, :])
        dq = dot(grad_scores, kr[:length, :])
        attended = dot(low, vr[:length, :])
        o_back[b, :, :LANES] = (dq * scale).astype(BF)
        o_back[b, :, LANES:] = attended.astype(BF)

    if seq_size <= 8:
        for b in range(seq_size):
            queries(b, (b + 1) * count)
    else:
        lax.fori_loop(0, seq_size, lambda b, _: (queries(b, rows), 0)[1], 0)
    for d in range(seq_size):
        at = slice(d * count, (d + 1) * count)
        o_back[d, :, :LANES] = jnp.where(left, o_back[d, :, :LANES].astype(F32), dk[at, :] * scale).astype(BF)
        o_back[d, :, LANES:] = jnp.where(left, dv[at, :], o_back[d, :, LANES:].astype(F32)).astype(BF)


def backward_kernel(
    tiled, back, after, w_proj, w_qkv, n2, cot, w_out, gate, ssm, gated, normed, s_ref, a_ref, bc,
    o_out, o_after, o_n2, o_gate, o_g, o_msg, *o_more
):
    back = ready(back)
    seq_size, count = back.shape[0], back.shape[1]
    copies = seq_size // H
    left = lax.broadcasted_iota(jnp.int32, (count, LANES), 1) < HD
    dq, dk, dv, att = [], [], [], []
    for p in range(H // 2):
        a0, b0 = (back[2 * p * copies, :, tile(i)].astype(F32) for i in range(2))
        a1, b1 = (back[(2 * p + 1) * copies, :, tile(i)].astype(F32) for i in range(2))
        dq.append(jnp.where(left, a0, pltpu.roll(a1, HD, 1)))
        dk.append(jnp.where(left, pltpu.roll(a0, HD, 1), a1))
        dv.append(jnp.where(left, b0, pltpu.roll(b1, HD, 1)))
        att.append(jnp.where(left, pltpu.roll(b0, HD, 1), b1))
    attended = jnp.concatenate(att, axis=1).astype(BF)
    after, w_proj = ready(after, w_proj)
    width = after.shape[1]
    o_out[...] = (after[...] + dot(attended, w_proj[...])).astype(BF)
    sent(o_out)
    w_qkv, n2, cot = ready(w_qkv, n2, cot)
    grad_qkv = jnp.concatenate(dq + dk + dv, axis=1).astype(BF)
    if not tiled:
        o_more[0][...] = attended
        o_more[1][...] = grad_qkv
    grad_x, grad_gain = rms_back(after[...], n2[...], dot_nt(grad_qkv, w_qkv[...]))
    o_n2[...] = jnp.sum(grad_gain, axis=0, keepdims=True)
    grad_after = cot[...].astype(F32) + grad_x
    o_after[...] = grad_after
    branch = grad_after.astype(BF)
    if not tiled:
        o_more[2][...] = branch
    sent(o_n2, o_after)
    w_out, gate, ssm = ready(w_out, gate, ssm)
    inner_width = gate.shape[1]
    tiles = inner_width // LANES
    a_ref = ready(a_ref)
    states = a_ref.shape[0] // 8
    grad_gated = dot_nt(branch, w_out[...])
    for j in range(tiles):
        v = gate[:, tile(j)].astype(F32)
        sig = jax.nn.sigmoid(v)
        grad = grad_gated[:, tile(j)]
        to_rows(o_g, j, grad * (v * sig))
        grad_gate = grad * ssm[:, tile(j)] * (sig * (1.0 + v * (1.0 - sig)))
        o_gate[:, tile(j)] = grad_gate.astype(BF)
    sent(o_gate, o_g)
    gated, normed = ready(gated, normed)
    if tiled:
        partials(seq_size, gated, branch, normed, o_gate, attended, cot, *o_more)
        sent(*o_more[:2])
    s_ref, smem = ready(s_ref, bc)

    def one(i, later):
        t = count - 1 - i
        s, g = block(s_ref, t), block(o_g, t)
        return tuple(
            jnp.exp2(s * block(a_ref, n)) * (g * smem[t, states + n] + later[n])
            for n in range(states)
        )

    leaving = lax.fori_loop(0, count, one, (jnp.zeros((8, LANES), F32),) * states, unroll=4)
    for n in range(0, states, 2):
        value = jnp.concatenate([leaving[n], leaving[n + 1]], axis=0).astype(BF)
        for d in range(seq_size):
            o_msg[d, 8 * n : 8 * n + 16, :] = value


def states_kernel(
    seq_size, start, a_ref, bc, s_ref, dx_ref, inner, conv_w, conv_b, seg, o_every, o_slope, ext
):
    start, a_ref, smem, s_ref, dx_ref = ready(start, a_ref, bc, s_ref, dx_ref)
    count = smem.shape[0]
    states = a_ref.shape[0] // 8
    o_every[: states * 8, :] = start[...]

    def again(t, state):
        s, dx = block(s_ref, t), block(dx_ref, t)
        state = tuple(
            jnp.exp2(s * block(a_ref, n)) * state[n] + dx * smem[t, n] for n in range(states)
        )
        for n in range(states):
            o_every[pl.ds(pl.multiple_of(((t + 1) * states + n) * 8, 8), 8), :] = state[n]
        return state

    lax.fori_loop(0, count, again, tuple(start[8 * n : 8 * n + 8, :] for n in range(states)), unroll=2)
    sent(o_every)
    inner, conv_w, conv_b, seg = ready(inner, conv_w, conv_b, seg)
    ext[...] = inner[...].astype(F32)
    offset = offsets_in_sequence(seg, seq_size)
    for j in range(o_slope.shape[1] // LANES):
        pre = conv_tile(ext, conv_w, conv_b, offset, j, count)
        sig = jax.nn.sigmoid(pre)
        o_slope[:, tile(j)] = sig * (1.0 + pre * (1.0 - sig))


def fold8(values, sub):
    low4, low2, low1 = sub < 4, (sub & 2) == 0, (sub & 1) == 0
    four = []
    for k in range(4):
        a, b = values[k], values[k + 4]
        four.append(jnp.where(low4, a, b) + pltpu.roll(jnp.where(low4, b, a), 4, 0))
    two = []
    for k in range(2):
        a, b = four[k], four[k + 2]
        two.append(jnp.where(low2, a + pltpu.roll(a, 6, 0), b + pltpu.roll(b, 2, 0)))
    a, b = two
    return jnp.where(low1, a + pltpu.roll(a, 7, 0), b + pltpu.roll(b, 1, 0))


def adjoint_kernel(
    seq_size, back, totals, a_ref, bc, s_ref, dx_ref, g_ref, every, gs_ref, ai_ref, o_bc, o_a, held, sums, arrived
):
    back, totals, a_ref = ready(back, totals, a_ref)
    states = a_ref.shape[0] // 8
    count = s_ref.shape[0] // 8
    zero = jnp.zeros((8, LANES), F32)
    chunks = arrived.shape[0]
    span = count // chunks
    loads = []
    for c in range(chunks):
        first, last = c * span * states * 8, ((c + 1) * span + (c == chunks - 1)) * states * 8
        loads.append(pltpu.make_async_copy(every.at[first:last], held.at[first:last], arrived.at[c]))
    for load in reversed(loads):
        load.start()

    def join(i, carry):
        d = seq_size - 1 - i
        total = total_step(totals, d, 0)
        return tuple(
            jnp.exp2(block(a_ref, n) * total) * carry[n] + state_rows(back, d, n)
            for n in range(states)
        )

    leaving = lax.fori_loop(0, seq_size - 1 - lax.axis_index("seq"), join, (zero,) * states)
    smem, s_ref, dx_ref, g_ref = ready(bc, s_ref, dx_ref, g_ref)
    sub = lax.broadcasted_iota(jnp.int32, (8, LANES), 0)

    def one(last, i, carry):
        later, grad_a = carry
        t = last - i
        s, dx, g = block(s_ref, t), block(dx_ref, t), block(g_ref, t)
        new_later, new_grad_a, with_b, with_c = [], [], [], []
        grad_step, adjoint_in = zero, zero
        for n in range(states):
            a = block(a_ref, n)
            adjoint = g * smem[t, states + n] + later[n]
            passed = jnp.exp2(s * a) * adjoint
            before = held[pl.ds(pl.multiple_of((t * states + n) * 8, 8), 8), :]
            now = held[pl.ds(pl.multiple_of(((t + 1) * states + n) * 8, 8), 8), :]
            grad_decay = passed * before
            grad_step = grad_step + grad_decay * a
            adjoint_in = adjoint_in + adjoint * smem[t, n]
            new_later.append(passed)
            new_grad_a.append(grad_a[n] + grad_decay * s)
            with_b.append(adjoint * dx)
            with_c.append(g * now)
        here = pl.ds(pl.multiple_of(t * 8, 8), 8)
        gs_ref[here, :] = grad_step
        ai_ref[here, :] = adjoint_in
        for i, part in enumerate((with_b[:8], with_b[8:], with_c[:8], with_c[8:])):
            sums[pl.ds(pl.multiple_of(t * 32 + 8 * i, 8), 8), :] = fold8(part, sub)
        return tuple(new_later), tuple(new_grad_a)

    carry = (leaving, (zero,) * states)
    for c in reversed(range(chunks)):
        loads[c].wait()
        carry = lax.fori_loop(0, span, functools.partial(one, (c + 1) * span - 1), carry, unroll=4)
    grad_a = carry[1]
    sent(gs_ref, ai_ref)
    for n in range(states):
        o_a[8 * n : 8 * n + 8, :] = grad_a[n] * (LN2 * block(a_ref, n))
    columns = o_bc.shape[1]
    lane = lax.broadcasted_iota(jnp.int32, (LANES, columns), 1)
    grad_bc = jnp.zeros(o_bc.shape, F32)
    for q in range(2 * states):
        rows = sums[pl.ds(q, count, stride=2 * states), :]
        high = rows.astype(BF)
        low = (rows - high.astype(F32)).astype(BF)
        to_column = (lane == columns - 2 * states + q).astype(BF)
        grad_bc = grad_bc + dot(high, to_column) + dot(low, to_column)
    o_bc[...] = grad_bc


def inner_kernel(
    seq_size, gs_ref, ai_ref, g_ref, mixed, step_pre, low, w_dt, grad_bc, grad_a, w_xp, inner, slope, conv_w, d_skip,
    seg, normed, grad_n2,
    *rest,
):
    o_first, o_second, o_inner, *own_small, ext, gext, grad_w = rest
    small = own_small[0] if own_small else o_second.ref
    gs_ref, ai_ref, g_ref = ready(gs_ref, ai_ref, g_ref)
    grad_bc, grad_a = ready(grad_bc, grad_a)
    count = g_ref.shape[0] // 8
    states = grad_a.shape[0] // 8
    mixed, step_pre, low, w_dt, w_xp, inner = ready(mixed, step_pre, low, w_dt, w_xp, inner)
    slope, conv_w, d_skip, seg, normed, grad_n2 = ready(slope, conv_w, d_skip, seg, normed, grad_n2)
    inner_width = mixed.shape[1]
    tiles = inner_width // LANES
    rank = w_dt.shape[0]
    taps = conv_w.shape[0]
    small[...] = jnp.zeros_like(small)
    small[104 * 8 : (104 + states) * 8, :] = grad_a[...]
    offset = offsets_in_sequence(seg, seq_size)
    halves = []
    for j in range(tiles):
        mix = mixed[:, tile(j)].astype(F32)
        pre = step_pre[:, tile(j)]
        grad_step = LN2 * from_rows(gs_ref, j, count) + mix * from_rows(ai_ref, j, count)
        grad_pre = grad_step * jax.nn.sigmoid(pre)
        small[101 * 8 + j : 101 * 8 + j + 1, :] = jnp.sum(grad_pre, axis=0, keepdims=True)
        grad_ssm = from_rows(g_ref, j, count)
        small[102 * 8 + j : 102 * 8 + j + 1, :] = jnp.sum(grad_ssm * mix, axis=0, keepdims=True)
        halves.append(grad_pre.astype(BF))
    half = jnp.concatenate(halves, axis=1)
    grad_w_dt = dot_tn(low[...], half)
    padded_dt = jnp.concatenate([w_dt[...], jnp.zeros((2 * states, inner_width), BF)], axis=0)
    grad_selector = (dot_nt(half, padded_dt) + grad_bc[...]).astype(BF)
    grad_w_xp = dot_tn(grad_selector, mixed[...])
    from_selector = dot(grad_selector, w_xp[...])
    ext[...] = inner[...].astype(F32)
    gext[...] = jnp.zeros_like(gext)
    for j in range(tiles):
        to_rows(small.at[pl.ds(0, 64 * 8)], j, grad_w_xp[:, tile(j)])
        to_rows(small.at[pl.ds(64 * 8, 32 * 8)], j, grad_w_dt[:, tile(j)])
        grad_mixed = (
            softplus(step_pre[:, tile(j)]) * from_rows(ai_ref, j, count)
            + from_rows(g_ref, j, count) * d_skip[:, tile(j)]
            + from_selector[:, tile(j)]
        )
        grad_pre = grad_mixed * slope[:, tile(j)]
        small[100 * 8 + j : 100 * 8 + j + 1, :] = jnp.sum(grad_pre, axis=0, keepdims=True)
        for k in range(taps):
            shifted = pl.ds(HALO - taps + 1 + k, count)
            usable = jnp.where(offset >= taps - 1 - k, grad_pre, 0.0)
            row = (96 + k) * 8 + j
            small[row : row + 1, :] = jnp.sum(usable * ext[shifted, tile(j)], axis=0, keepdims=True)
            gext[shifted, tile(j)] += conv_w[k : k + 1, tile(j)] * usable
    o_inner[...] = gext[...].astype(BF)
    sent(o_inner)
    width = grad_n2.shape[1]
    for j in range(width // LANES):
        small[103 * 8 + 4 + j : 103 * 8 + 5 + j, :] = grad_n2[:, tile(j)]
    if not own_small:
        o_first[...] = dot_tn(normed[...], o_inner[...])
        return
    grad_w[...] = dot_tn(normed[...], o_inner[...])
    for to, x, s, at in receivers((o_first, o_second), seq_size):
        to[x * seq_size + s, :LANES, :] = grad_w[pl.ds(pl.multiple_of(at * LANES, LANES), LANES), tile(s)].astype(BF)
        rows = small.shape[0] // (width // LANES * seq_size)
        here = pl.ds(pl.multiple_of((at * seq_size + s) * rows, rows), rows)
        to[x * seq_size + s, LANES:, :] = small[here, :].astype(BF)


def receivers(results, seq_size, mine=0):
    core = lax.rem(lax.axis_index("dp"), 2)
    for to, side in zip(results, (core, 1 - core)):
        for x in range(to.shape[0] // seq_size):
            for s in range(seq_size):
                yield to, x, s, 2 * lax.bitwise_xor(x, mine) + side


def partials(seq_size, gated, branch, normed, grad_gate, attended, cot, keep, send, out, gate, proj):
    out[...] = dot_tn(gated[...], branch)
    gate[...] = dot_tn(normed[...], grad_gate[...])
    proj[...] = dot_tn(attended, cot[...])
    across = out.shape[1] // LANES
    down = seq_size // across
    mine = lax.axis_index("dp") // 2
    for to, x, s, at in receivers((keep, send), seq_size, mine):
        rows = pl.ds(pl.multiple_of((at * down + s // across) * LANES, LANES), LANES)
        to[x * seq_size + s, :LANES, :] = out[rows, tile(s % across)].astype(BF)
        rows = pl.ds(pl.multiple_of(at * LANES, LANES), LANES)
        to[x * seq_size + s, LANES : 2 * LANES, :] = gate[rows, tile(s)].astype(BF)
        rows = pl.ds(pl.multiple_of((at * down + s // across) * HD, HD), HD)
        to[x * seq_size + s, 2 * LANES :, :] = proj[rows, tile(s % across)].astype(BF)


def tokens_kernel(grad_inner, w_in, grad_gate, tok, halo, n1, grad_after, o_tok, o_halo, o_n1):
    grad_inner, w_in, grad_gate = ready(grad_inner, w_in, grad_gate)
    inner_width = grad_inner.shape[1]
    grad_normed = dot_nt(grad_inner[...], w_in[:, :inner_width])
    own = dot_nt(grad_gate[...], w_in[:, inner_width:])
    grad_normed = jnp.concatenate([grad_normed[:HALO], grad_normed[HALO:] + own], axis=0)
    tok, halo, n1, grad_after = ready(tok, halo, n1, grad_after)
    x = jnp.concatenate([halo[...], tok[...]], axis=0).astype(F32)
    grad_x, grad_gain = rms_back(x, n1[...], grad_normed)
    o_tok[...] = grad_after[...] + grad_x[HALO:]
    o_halo[...] = grad_x[HALO - 8 : HALO]
    grad_gain = jnp.sum(grad_gain, axis=0, keepdims=True)
    tiles = grad_gain.shape[1] // LANES
    rows = [grad_gain[:, tile(j)] for j in range(tiles)] + [jnp.zeros((16 - tiles, LANES), F32)]
    o_n1[...] = jnp.concatenate(rows, axis=0).astype(BF)


def head_products_kernel(normed, back, *rest):
    *outs, grad, last = rest
    normed, back = ready(normed, back)
    both = back[...].reshape(back.shape[0] * back.shape[1], 2 * LANES)
    grad[...] = dot_tn(normed[...], both[:, :LANES])
    last[...] = dot_tn(normed[...], both[:, LANES:])
    left = lax.broadcasted_iota(jnp.int32, (HD, LANES), 1) < HD
    for distance, to in enumerate(outs):
        g = lax.bitwise_xor(lax.axis_index("dp"), distance)
        to[: 2 * HD, :] = grad[pl.ds(pl.multiple_of(g * LANES, LANES), LANES), :].astype(BF)
        low = last[pl.ds(pl.multiple_of(g * LANES, LANES), HD), :]
        high = last[pl.ds(pl.multiple_of(g * LANES + HD, HD), HD), :]
        to[2 * HD :, :] = jnp.where(left, low, pltpu.roll(high, HD, 1)).astype(BF)


def early_sum_kernel(parts, *heads):
    *heads, o_sum = heads
    heads, parts = ready(*heads), ready(parts)
    head = heads[0][...].astype(F32)
    for part in heads[1:]:
        head = head + part[...].astype(F32)
    total = parts[0].astype(F32)
    for d in range(1, parts.shape[0]):
        total = total + parts[d].astype(F32)
    rows = total.shape[0]
    o_sum[:rows, :] = total.astype(BF)
    o_sum[rows:, :] = head.astype(BF)


def sum_and_spread_kernel(parts, own, o_all):
    parts, own = ready(parts, own)
    total = parts[0].astype(F32)
    for d in range(1, parts.shape[0]):
        total = total + parts[d].astype(F32)
    total = total.astype(BF)
    rows = total.shape[0]
    for d in range(o_all.shape[0]):
        o_all[d, :rows, :] = total
        o_all[d, rows:, :] = own[...]


def early_assembly_kernel(groups, early, w_in, o_out, o_proj, o_qkv, o_in, pieces, out, proj, qkv, gate, loads, stores):
    seq_size = early.shape[0] // groups
    inner_width, width = gate.shape[1], proj.shape[1]
    across = width // LANES
    left = lax.broadcasted_iota(jnp.int32, (LANES, LANES), 1) < HD
    at = 2 * LANES + HD

    def pairs(a, b):
        a, b = a.astype(F32), b.astype(F32)
        mask = left[: a.shape[0]]
        return jnp.where(mask, a, pltpu.roll(b, HD, 1)), jnp.where(mask, pltpu.roll(a, HD, 1), b)

    own = [slice(g * seq_size, (g + 1) * seq_size) for g in range(groups)]
    arrivals = [pltpu.make_async_copy(early.at[own[g]], pieces.at[own[g]], loads.at[g]) for g in range(groups)]
    for copy in arrivals:
        copy.start()
    copies = []
    for g in range(groups):
        arrivals[g].wait()
        down = seq_size // across
        for s in range(seq_size):
            piece = pieces[g * seq_size + s]
            row = g * down + s // across
            out[tile(row), tile(s % across)] = piece[:LANES].astype(F32)
            gate[tile(g), tile(s)] = piece[LANES : 2 * LANES].astype(F32)
            proj[row * HD : (row + 1) * HD, tile(s % across)] = piece[2 * LANES : at].astype(F32)
        for p in range(seq_size // 2):
            a, b = pieces[g * seq_size + 2 * p], pieces[g * seq_size + 2 * p + 1]
            first, second, third = (slice(i * width + p * LANES, i * width + (p + 1) * LANES) for i in range(3))
            qkv[tile(g), first], qkv[tile(g), second] = pairs(a[at : at + LANES], b[at : at + LANES])
            low, high = pairs(a[at + LANES :], b[at + LANES :])
            qkv[g * LANES : g * LANES + HD, third] = low
            qkv[g * LANES + HD : (g + 1) * LANES, third] = high
        for i, (source, target, rows) in enumerate(
            ((out, o_out, down * LANES), (proj, o_proj, down * HD), (qkv, o_qkv, LANES), (gate, o_in, LANES))
        ):
            here = slice(g * rows, (g + 1) * rows)
            target = target.at[here, inner_width:] if i == 3 else target.at[here]
            copies.append(pltpu.make_async_copy(source.at[here], target, stores.at[4 * g + i]))
            copies[-1].start()
    for copy in copies:
        copy.wait()


def late_assembly_kernel(
    groups, mine, other, o_in, o_n1, o_conv_w, o_conv_b, o_xp, o_dt, o_dtb, o_a, o_skip, o_n2, inner, small, sems
):
    mine, other = ready(mine, other)
    seq_size = mine.shape[0] * 2 // groups
    width, inner_width = inner.shape
    rows = mine.shape[1] - LANES - 16
    copies = []
    for ref, x, s, g in receivers((mine, other), seq_size):
        at = pl.ds(pl.multiple_of(g * LANES, LANES), LANES)
        inner[at, tile(s)] = ref[x * seq_size + s, :LANES, :].astype(F32)
        here = pl.ds(pl.multiple_of((g * seq_size + s) * rows, rows), rows)
        small[here, :] = ref[x * seq_size + s, LANES : LANES + rows, :].astype(F32)
        if s == seq_size - 1:
            copies.append(pltpu.make_async_copy(inner.at[at], o_in.at[at, :inner_width], sems.at[len(copies)]))
            copies[-1].start()
    for j in range(inner_width // LANES):
        value = from_rows(small, j, SMALL)
        for ref, first, last in (
            (o_xp, 0, 64), (o_dt, 64, 96), (o_conv_w, 96, 100), (o_conv_b, 100, 101), (o_dtb, 101, 102),
            (o_skip, 102, 103), (o_a, 104, 120),
        ):
            ref[:, tile(j)] = value[first:last]
        if j >= width // LANES:
            o_n2[:, tile(j - width // LANES)] = value[103:104]
    sent(o_conv_w, o_conv_b, o_xp, o_dt, o_dtb, o_a, o_skip, o_n2)
    gain = jnp.zeros((16, LANES), F32)
    for source in (mine, other):
        for d in range(source.shape[0]):
            gain = gain + source[d, LANES + rows :, :].astype(F32)
    for j in range(width // LANES):
        o_n1[:, tile(j)] = gain[j : j + 1]
    for copy in copies:
        copy.wait()


class Held:
    def __init__(self, buffer, copy):
        self.ref, self.copy, self.shape = buffer, copy, buffer.shape
        self.done = False

    def __getitem__(self, at):
        return self.ref[at]

    def __setitem__(self, at, value):
        self.ref[at] = value


def ready(*held):
    for one in held:
        if not one.done:
            one.copy.wait()
            one.done = True
    refs = tuple(one.ref for one in held)
    return refs[0] if len(refs) == 1 else refs


def sent(*held):
    for one in held:
        if not one.done:
            one.copy.start()
            one.done = True


IN_HBM = pl.BlockSpec(memory_space=pltpu.HBM)


def call(
    kernel, outs, scratch, *args, name=None, us=1, raw=(), raw_out=(), scalars=(), views=None, aliases=None, after=(),
    near=(), vmem=60,
):
    views = views or {}
    count, first_out = len(args), len(args) + len(after)
    first_scratch = first_out + len(outs)
    buffers = []
    for i, arg in enumerate(args):
        shape = jax.eval_shape(lambda v, i=i: v[views[i]], arg).shape if i in views else arg.shape
        kind = pltpu.SMEM if i in scalars else pltpu.VMEM
        buffers.append(None if i in raw else kind(shape, arg.dtype))
    for i, (shape, dtype) in enumerate(outs):
        buffers.append(None if i in raw_out else pltpu.VMEM(shape, dtype))
    used = [b for b in buffers if b is not None]

    def run(*refs):
        given = list(refs[:count]) + list(refs[first_out:first_scratch])
        own = list(refs[first_scratch : first_scratch + len(used)])
        sems = refs[first_scratch + len(used)]
        passed = []
        for i, (ref, buffer) in enumerate(zip(given, buffers)):
            if buffer is None:
                passed.append(ref)
                continue
            buffer = own.pop(0)
            if i < count:
                source = ref.at[views[i]] if i in views else ref
                copy = pltpu.make_async_copy(source, buffer, sems.at[i])
                copy.start()
            else:
                copy = pltpu.make_async_copy(buffer, ref, sems.at[i])
            passed.append(Held(buffer, copy))
        kernel(*passed, *refs[first_scratch + len(used) + 1 :])
        ready(*[p for p in passed[:count] if isinstance(p, Held)])
        results = [p for p in passed[count:] if isinstance(p, Held)]
        sent(*results)
        for result in results:
            result.copy.wait()

    return pl.pallas_call(
        run,
        out_shape=[jax.ShapeDtypeStruct(s, d) for s, d in outs],
        in_specs=[pl.BlockSpec(memory_space=pl.ANY) if i in near else IN_HBM for i in range(first_out)],
        out_specs=[IN_HBM] * len(outs),
        scratch_shapes=used + [pltpu.SemaphoreType.DMA((len(buffers),))] + scratch,
        compiler_params=pltpu.CompilerParams(vmem_limit_bytes=vmem * 1024 * 1024),
        cost_estimate=pl.CostEstimate(flops=us * 10**9 + 1000, bytes_accessed=1000, transcendentals=0),
        input_output_aliases=aliases or {},
        name=name,
    )(*args, *after)


def exchange(value, axes):
    return lax.all_to_all(value, axes, 0, 0, tiled=True)


def own_core(value, groups, seq_size):
    peers = [
        [g * seq_size + s for g in range(core, groups, 2) for s in range(seq_size)] for core in range(2)
    ]
    return lax.all_to_all(value, ("dp", "seq"), 0, 0, tiled=True, axis_index_groups=peers)


def other_core(value, groups):
    return lax.ppermute(value, "dp", [(g, g ^ 1) for g in range(groups)])


def body(
    tokens, seg_start, norm_one, w_in, conv_w, conv_b, w_xproj, w_dt, dt_bias, a_log, d_skip,
    w_out, norm_two, w_qkv, w_proj, cotangent,
):
    count, width = tokens.shape
    inner_width = w_in.shape[1] // 2
    states = a_log.shape[1]
    rank = w_dt.shape[0]
    taps = conv_w.shape[0]
    groups, seq_size = lax.axis_size("dp"), lax.axis_size("seq")
    rows = count * seq_size
    ext_rows = HALO + count
    tiled = inner_width == seq_size * LANES and width == groups * LANES and seq_size == H
    peers = groups // 2 * seq_size
    line = lambda v: v.reshape(1, -1)
    seg = line(seg_start)
    n1, n2, cb, dtb, skip = (line(v) for v in (norm_one, norm_two, conv_b, dt_bias, d_skip))
    vmem, smem = pltpu.VMEM, pltpu.SMEM((count, 2 * states), F32)
    sem = pltpu.SemaphoreType.DMA
    blocks = ((count * 8, LANES), F32)
    ends_at = states * 8
    halo = lax.ppermute(tokens[count - HALO :], "seq", [(i, i + 1) for i in range(seq_size - 1)])
    msg, normed, inner, gate, mixed, bc, low, step_pre, s, dx, a = call(
        functools.partial(forward_kernel, seq_size),
        [
            ((seq_size, states * 8 + 32, LANES), BF), ((ext_rows, width), BF),
            ((ext_rows, inner_width), BF), ((count, inner_width), BF), ((count, inner_width), BF), ((count, 2 * states), F32),
            ((count, rank), BF), ((count, inner_width), F32), blocks, blocks, ((states * 8, LANES), F32),
        ],
        [vmem((ext_rows, inner_width), F32), smem, sem],
        tokens, halo, n1, w_in, conv_w, cb, w_xproj.T, w_dt, dtb, a_log.T, seg,
        name="forward", us=0, near=(1,),
    )
    msg = exchange(msg, "seq")
    (grad_att,) = call(
        grad_att_kernel, [((count, width), BF)], [], cotangent, w_proj, name="grad_att", us=0
    )
    qkvg, start, ssm, after, gated, normed_two = call(
        middle_kernel,
        [
            ((seq_size, count, 2 * LANES), BF), ((states * 8, LANES), F32), ((count, inner_width), F32),
            ((count, width), F32), ((count, inner_width), BF), ((count, width), BF),
        ],
        [vmem(*blocks)],
        msg, a, bc, s, dx, mixed, gate, skip, tokens, w_out, n2, w_qkv, grad_att,
        name="middle", us=0, scalars=(2,), views={0: np.s_[:, : ends_at + 16, :]}, near=(0,),
    )
    qkvg = exchange(qkvg, "seq")
    every, slope = call(
        functools.partial(states_kernel, seq_size),
        [(((count + 1) * states * 8, LANES), F32), ((count, inner_width), F32)],
        [vmem((ext_rows, inner_width), F32)],
        start, a, bc, s, dx, inner, conv_w, cb, seg, name="states", us=0, scalars=(2,),
    )
    (back,) = call(
        attention_kernel,
        [((seq_size, count, 2 * LANES), BF)],
        [vmem((rows, LANES), BF)] * 4 + [vmem((rows, LANES), F32)] * 2,
        qkvg, msg, name="attention", us=0, views={1: np.s_[:, ends_at + 16 :, :]}, after=(every,), near=(0,),
    )
    back_own = exchange(back, "seq")
    pieces = [((peers, 2 * LANES + HD, LANES), BF)] * 2
    rest = [((count, width), BF), ((count, 3 * width), BF), ((count, width), BF)]
    out, grad_after, grad_n2, grad_gate, g, adj, *more = call(
        functools.partial(backward_kernel, tiled),
        [
            ((count, width), BF), ((count, width), F32), ((1, width), F32), ((count, inner_width), BF), blocks,
            ((seq_size, states * 8, LANES), BF),
        ] + (pieces if tiled else rest),
        [vmem((inner_width, width), F32), vmem((width, inner_width), F32), vmem((width, width), F32)] if tiled else [],
        back_own, after, w_proj, w_qkv, n2, cotangent, w_out, gate, ssm, gated, normed, s, a, bc,
        name="backward", us=0, scalars=(13,), views={10: np.s_[HALO:, :]}, near=(0,),
    )
    adj = exchange(adj, "seq")
    between = ()
    if tiled:
        normed_two_all = lax.all_gather(normed_two, "seq", axis=0, tiled=True)
        keep, send = more
        add = lambda *parts: sum(part.astype(F32) for part in parts).astype(BF)
        received = other_core(send, groups)
        across = add(keep[seq_size:], received[seq_size:])
        across = lax.ppermute(across, "dp", [(g, g ^ 2) for g in range(groups)])
        part = add(keep[:seq_size], received[:seq_size], across)
        between = (part,)
        part = exchange(part, "seq")
    gs, ai, grad_bc, grad_a = call(
        functools.partial(adjoint_kernel, seq_size),
        [blocks, blocks, ((count, rank + 2 * states), F32), ((states * 8, LANES), F32)],
        [vmem(((count + 1) * states * 8, LANES), F32), vmem((count * 2 * states, LANES), F32), sem((8,))],
        adj, msg, a, bc, s, dx, g, every, name="adjoint", us=0, raw=(7,), scalars=(3,), near=(0,),
        views={1: np.s_[:, ends_at : ends_at + 16, :]}, after=between,
    )
    small_rows = SMALL * 8 // (groups * seq_size)
    *sums, small, grad_inner = call(
        functools.partial(inner_kernel, seq_size),
        ([((peers, LANES + small_rows, LANES), BF)] * 2 if tiled else [((width, inner_width), F32), ((SMALL * 8, LANES), F32)])
        + [((ext_rows, inner_width), BF)],
        ([vmem((SMALL * 8, LANES), F32)] if tiled else [])
        + [vmem((ext_rows, inner_width), F32), vmem((ext_rows, inner_width), F32), vmem((width, inner_width), F32)],
        gs, ai, g, mixed, step_pre, low, w_dt, grad_bc, grad_a, w_xproj.T, inner, slope, conv_w, skip, seg, normed, grad_n2,
        name="inner", us=0,
    )
    grad_tokens, grad_halo, grad_n1 = call(
        tokens_kernel, [((count, width), F32), ((8, width), F32), ((16, LANES), BF)], [],
        grad_inner, w_in, grad_gate, tokens, halo, n1, grad_after, name="tokens", us=0,
    )
    returned = lax.ppermute(grad_halo, "seq", [(i + 1, i) for i in range(seq_size - 1)])
    grad_tokens = grad_tokens.at[count - 8 :].add(returned)
    flat = lambda v: v.reshape(-1)
    if tiled:
        head, *heads = call(
            head_products_kernel, [((3 * HD, LANES), BF)] * groups, [vmem((width, LANES), F32)] * 2,
            normed_two_all, back, name="head_products", us=0, after=(grad_n1,),
        )
        heads = [
            lax.ppermute(piece, "dp", [(g, g ^ distance) for g in range(groups)])
            for distance, piece in enumerate(heads, 1)
        ]
        (early,) = call(
            early_sum_kernel, [((part.shape[1] + head.shape[0], LANES), BF)], [], part, head, *heads,
            name="early_sum", us=0, after=(grad_n1,), near=(0, 2, 3, 4),
        )
        late = add(sums[0], other_core(small, groups))
        late, early = lax.optimization_barrier((late, early))
        late = own_core(late, groups, seq_size)
        early = lax.all_gather(early, ("dp", "seq"))
        (late,) = call(
            sum_and_spread_kernel, [((peers, late.shape[1] + 16, LANES), BF)], [], late, grad_n1, name="late_sum", us=0,
            near=(0,),
        )
        mine = own_core(late, groups, seq_size)
        mine, grad_tokens = lax.optimization_barrier((mine, grad_tokens))
        row = lambda n: ((n, inner_width), F32)
        half, g_n1, g_conv_w, g_conv_b, g_xp, g_dt, g_dtb, g_a, g_skip, g_n2 = call(
            functools.partial(late_assembly_kernel, groups),
            [
                ((width, 2 * inner_width), F32), ((1, width), F32), row(taps), row(1), row(2 * states + rank), row(rank),
                row(1), row(states), row(1), ((1, width), F32),
            ],
            [vmem((width, inner_width), F32), vmem((SMALL * 8, LANES), F32), sem((4,))],
            mine, other_core(mine, groups), name="late_assembly", us=0, raw_out=(0,), near=(0, 1),
        )
        whole = [((inner_width, width), F32), ((width, width), F32), ((width, 3 * width), F32)]
        grad_w_out, grad_w_proj, grad_w_qkv, grad_w_in = call(
            functools.partial(early_assembly_kernel, groups),
            whole + [((width, 2 * inner_width), F32)],
            [vmem(early.shape, BF)] + [vmem(*v) for v in whole] + [vmem((width, inner_width), F32), sem((4,)), sem((16,))],
            early, half, name="early_assembly", us=0, raw=(0, 1), raw_out=(0, 1, 2, 3), aliases={1: 3},
        )
        g_xp, g_a, g_n1, g_n2 = g_xp.T, g_a.T, flat(g_n1), flat(g_n2)
    else:
        attended, grad_qkv, branch = more
        small = small.reshape(SMALL, inner_width)
        g_n1 = flat(grad_n1[: width // LANES].astype(F32))
        both = jnp.concatenate([sums[0], dot_tn(normed[HALO:], grad_gate)], axis=1)
        grad_w_in, grad_w_out, grad_w_qkv, grad_w_proj, small, g_n1 = lax.psum(
            (both, dot_tn(gated, branch), dot_tn(normed_two, grad_qkv), dot_tn(attended, cotangent), small, g_n1), ("dp", "seq")
        )
        g_xp, g_dt, g_conv_w, g_conv_b, g_dtb = small[:64].T, small[64:96], small[96:100], small[100], small[101]
        g_skip, g_n2, g_a = small[102], small[103, width:], small[104:120].T
    return (out, grad_tokens, g_n1, grad_w_in, g_conv_w, flat(g_conv_b), g_xp, g_dt, flat(g_dtb), g_a, flat(g_skip),
            grad_w_out, g_n2, grad_w_qkv, grad_w_proj)


def solution(mesh):
    split, copied = P(("dp", "seq"), None), P()
    return jax.shard_map(
        body,
        mesh=mesh,
        in_specs=(split, P(("dp", "seq"))) + (copied,) * 13 + (split,),
        out_specs=(split, split) + (copied,) * 13,
        check_vma=False,
    )
```

```python
import functools

import jax
import jax.numpy as jnp
import numpy as np
from jax import lax
from jax.experimental import pallas as pl
from jax.experimental.pallas import tpu as pltpu
from jax.sharding import PartitionSpec as P

H = 8
HD = 64
LANES = 128
HALO = 16
SMALL = 128
RESET = 1e30
EPSILON = 1e-05
LOG2E = 1.4426950408889634
LN2 = 0.6931471805599453
BF = jnp.bfloat16
F32 = jnp.float32


def dot(a, b):
    return jnp.dot(a, b, preferred_element_type=F32)


def dot_nt(a, b):
    return lax.dot_general(a, b, (((1,), (1,)), ((), ())), preferred_element_type=F32)


def dot_tn(a, b):
    return lax.dot_general(a, b, (((0,), (0,)), ((), ())), preferred_element_type=F32)


def tile(j):
    return slice(j * LANES, (j + 1) * LANES)


def softplus(x):
    u = jnp.exp(-jnp.abs(x))
    series = u * (1.0 - u * (0.5 - u * (1.0 / 3.0 - u * 0.25)))
    return jnp.maximum(x, 0.0) + jnp.where(u < 0.015, series, jnp.log(1.0 + u))


def rms_parts(x):
    return lax.rsqrt(jnp.mean(x * x, axis=-1, keepdims=True) + EPSILON)


def rms_back(x, gain, grad):
    r = rms_parts(x)
    scaled = grad * gain
    inner = jnp.mean(x * scaled, axis=-1, keepdims=True)
    return r * scaled - x * (r * r * r * inner), grad * x * r


def to_rows(ref, j, value):
    ref[pl.ds(j, value.shape[0], stride=8), :] = value


def from_rows(ref, j, count):
    return ref[pl.ds(j, count, stride=8), :]


def block(ref, t):
    return ref[pl.ds(pl.multiple_of(t * 8, 8), 8), :]


def offsets_in_sequence(seg_ref, seq_size):
    count = seg_ref.shape[1]
    base = (lax.axis_index("dp") * seq_size + lax.axis_index("seq")) * count
    places = base + lax.broadcasted_iota(jnp.int32, (1, count), 1)
    row = (places - seg_ref[...]).astype(F32)
    return jnp.transpose(jnp.broadcast_to(row, (LANES, count)))


def conv_tile(ext_ref, w_ref, b_ref, offset, j, count):
    taps = w_ref.shape[0]
    pre = jnp.broadcast_to(b_ref[:, tile(j)], (count, LANES))
    for k in range(taps):
        rows = ext_ref[pl.ds(HALO - taps + 1 + k, count), tile(j)]
        pre = pre + jnp.where(offset >= taps - 1 - k, w_ref[k : k + 1, tile(j)] * rows, 0.0)
    return pre


def forward_kernel(
    seq_size, tok, halo, n1, w_in, conv_w, conv_b, w_xp, w_dt, dtb, a_log, seg,
    o_msg, o_normed, o_inner, o_gate, o_mixed, o_bc, o_low, o_pre, o_s, o_dx, o_a,
    ext, smem, sem,
):
    tok, halo, n1, seg = ready(tok, halo, n1, seg)
    count = tok.shape[0]
    states = a_log.shape[0]
    inner_width = conv_w.shape[1]
    tiles = inner_width // LANES
    rank = w_dt.shape[0]
    x = jnp.concatenate([halo[...], tok[...]], axis=0).astype(F32)
    normed = (x * rms_parts(x) * n1[...]).astype(BF)
    o_normed[...] = normed
    sent(o_normed)
    w_in = ready(w_in)
    inner = dot(normed, w_in[:, :inner_width]).astype(BF)
    o_inner[...] = inner
    sent(o_inner)
    ext[...] = inner.astype(F32)
    conv_w, conv_b, w_xp, w_dt, dtb, a_log = ready(conv_w, conv_b, w_xp, w_dt, dtb, a_log)
    offset = offsets_in_sequence(seg, seq_size)
    for j in range(tiles):
        pre = conv_tile(ext, conv_w, conv_b, offset, j, count)
        o_mixed[:, tile(j)] = (pre * jax.nn.sigmoid(pre)).astype(BF)
    sent(o_mixed)
    selector = dot_nt(o_mixed[...], w_xp[...])
    low = selector[:, :rank].astype(BF)
    o_low[...] = low
    o_bc[...] = selector[:, rank:]
    sent(o_low, o_bc)
    copy = pltpu.make_async_copy(o_bc.ref, smem, sem)
    copy.start()
    o_pre[...] = dot(low, w_dt[...]) + dtb[...]
    sent(o_pre)
    o_gate[...] = dot(normed[HALO:], w_in[:, inner_width:]).astype(BF)
    sent(o_gate)
    for j in range(tiles):
        step = softplus(o_pre[:, tile(j)])
        to_rows(o_s, j, jnp.where(offset == 0.0, RESET, step))
        to_rows(o_dx, j, step * o_mixed[:, tile(j)].astype(F32))
        to_rows(o_a, j, -LOG2E * jnp.exp(a_log[:, tile(j)]))
    sent(o_s, o_dx, o_a)
    copy.wait()

    def one(t, carry):
        total, state = carry
        s, dx = block(o_s, t), block(o_dx, t)
        return total + s, tuple(
            jnp.exp2(s * block(o_a, n)) * state[n] + dx * smem[t, n] for n in range(states)
        )

    zero = jnp.zeros((8, LANES), F32)
    total, state = lax.fori_loop(0, count, one, (zero, (zero,) * states), unroll=4)
    high = total.astype(BF).astype(F32)
    seg_local = (seg[...] - lax.axis_index("dp") * (seq_size * count)).astype(F32)
    seg_high = jnp.floor(seg_local * (1.0 / 64.0))
    last = jnp.concatenate([seg_high, seg_local - 64.0 * seg_high, jnp.zeros((14, LANES), F32)], axis=0)
    blocks = [jnp.concatenate([state[n], state[n + 1]], axis=0) for n in range(0, states, 2)]
    blocks += [jnp.concatenate([high, total - high], axis=0), last]
    for i, value in enumerate(blocks):
        value = value.astype(BF)
        for d in range(seq_size):
            o_msg[d, 16 * i : 16 * i + 16, :] = value


def total_step(msg, d, states):
    rows = msg[d, states * 8 : states * 8 + 16, :].astype(F32)
    return rows[:8] + rows[8:]


def state_rows(msg, d, n):
    rows = msg[d, 16 * (n // 2) : 16 * (n // 2) + 16, :].astype(F32)
    return rows[:8] if n % 2 == 0 else rows[8:]


def middle_kernel(
    msg, a_ref, bc, s_ref, dx_ref, mixed, gate, d_skip, tok, w_out, n2, w_qkv, grad_att,
    o_qkvg, o_start, o_ssm, o_after, o_gated, o_normed,
    y_ref,
):
    msg, a_ref = ready(msg, a_ref)
    states = a_ref.shape[0] // 8
    zero = jnp.zeros((8, LANES), F32)

    def join(d, carry):
        total = total_step(msg, d, states)
        return tuple(
            jnp.exp2(block(a_ref, n) * total) * carry[n] + state_rows(msg, d, n)
            for n in range(states)
        )

    start = lax.fori_loop(0, lax.axis_index("seq"), join, (zero,) * states)
    for n in range(states):
        o_start[8 * n : 8 * n + 8, :] = start[n]
    sent(o_start)
    s_ref, dx_ref, smem = ready(s_ref, dx_ref, bc)
    count = smem.shape[0]

    def one(t, state):
        s, dx = block(s_ref, t), block(dx_ref, t)
        state = tuple(
            jnp.exp2(s * block(a_ref, n)) * state[n] + dx * smem[t, n] for n in range(states)
        )
        parts = [state[n] * smem[t, states + n] for n in range(states)]
        while len(parts) > 1:
            parts = [a + b for a, b in zip(parts[::2], parts[1::2])]
        y_ref[pl.ds(pl.multiple_of(t * 8, 8), 8), :] = parts[0]
        return state

    lax.fori_loop(0, count, one, start, unroll=4)
    mixed, gate, d_skip, tok, w_out, n2 = ready(mixed, gate, d_skip, tok, w_out, n2)
    inner_width, width = mixed.shape[1], tok.shape[1]
    tiles = inner_width // LANES
    for j in range(tiles):
        ssm = from_rows(y_ref, j, count) + d_skip[:, tile(j)] * mixed[:, tile(j)].astype(F32)
        o_ssm[:, tile(j)] = ssm
        v = gate[:, tile(j)].astype(F32)
        o_gated[:, tile(j)] = (ssm * (v * jax.nn.sigmoid(v))).astype(BF)
    sent(o_ssm, o_gated)
    after = tok[...].astype(F32) + dot(o_gated[...], w_out[...])
    o_after[...] = after
    sent(o_after)
    normed = (after * rms_parts(after) * n2[...]).astype(BF)
    o_normed[...] = normed
    sent(o_normed)
    w_qkv, grad_att = ready(w_qkv, grad_att)
    qkv = dot(normed, w_qkv[...])
    copies = o_qkvg.shape[0] // H
    left = lax.broadcasted_iota(jnp.int32, (count, LANES), 1) < HD
    for p in range(H // 2):
        q, k, v = (qkv[:, i * width + p * LANES : i * width + (p + 1) * LANES] for i in range(3))
        g = grad_att[:, tile(p)].astype(F32)
        first = (jnp.where(left, q, pltpu.roll(k, HD, 1)), jnp.where(left, v, pltpu.roll(g, HD, 1)))
        second = (jnp.where(left, pltpu.roll(q, HD, 1), k), jnp.where(left, pltpu.roll(v, HD, 1), g))
        for h, pair in ((2 * p, first), (2 * p + 1, second)):
            for i, value in enumerate(pair):
                value = value.astype(BF)
                for r in range(copies):
                    o_qkvg[h * copies + r, :, tile(i)] = value


def grad_att_kernel(cot, w_proj, o_grad):
    cot, w_proj = ready(cot, w_proj)
    o_grad[...] = dot_nt(cot[...], w_proj[...]).astype(BF)


def attention_kernel(qkvg, ends, o_back, qz, kr, gz, vr, dk, dv):
    qkvg, ends = ready(qkvg, ends)
    seq_size, count = qkvg.shape[0], qkvg.shape[1]
    rows = seq_size * count
    left = lax.broadcasted_iota(jnp.int32, (count, LANES), 1) < HD
    for d in range(seq_size):
        at = slice(d * count, (d + 1) * count)
        a, b = qkvg[d, :, :LANES].astype(F32), qkvg[d, :, LANES:].astype(F32)
        qz[at, :] = jnp.where(left, a, 0.0).astype(BF)
        kr[at, :] = pltpu.roll(a, HD, 1).astype(BF)
        gz[at, :] = jnp.where(left, 0.0, b).astype(BF)
        vr[at, :] = pltpu.roll(b, HD, 1).astype(BF)
    dk[...] = jnp.zeros_like(dk)
    dv[...] = jnp.zeros_like(dv)
    scale = HD**-0.5

    def queries(b, length, blocks):
        tall = blocks * count
        at = pl.ds(b * count if isinstance(b, int) else pl.multiple_of(b * count, count), tall)
        firsts = []
        for i in range(blocks):
            tail = ends[b + i].astype(F32)
            starts = jnp.broadcast_to(tail[0:1] * 64.0 + tail[1:2], (LANES, LANES))
            firsts.append(jnp.transpose(starts)[:, :1])
        first = jnp.concatenate(firsts, axis=0).astype(jnp.int32)
        column = lax.broadcasted_iota(jnp.int32, (tall, length), 1)
        row = b * count + lax.broadcasted_iota(jnp.int32, (tall, 1), 0)
        visible = (column <= row) & (column >= first)
        scores = jnp.where(visible, dot_nt(qz[at, :], kr[:length, :]) * scale, -1e30)
        weight = jnp.exp(scores - jnp.max(scores, axis=1, keepdims=True))
        probs = weight * (1.0 / jnp.sum(weight, axis=1, keepdims=True))
        low = probs.astype(BF)
        grad_probs = dot_nt(gz[at, :], vr[:length, :])
        delta = jnp.sum(probs * grad_probs, axis=1, keepdims=True)
        grad_scores = (probs * (grad_probs - delta)).astype(BF)
        dk[:length, :] += dot_tn(grad_scores, kr[at, :])
        dv[:length, :] += dot_tn(low, vr[at, :])
        dq = (dot(grad_scores, kr[:length, :]) * scale).astype(BF)
        attended = dot(low, vr[:length, :]).astype(BF)
        for i in range(blocks):
            o_back[b + i, :, :LANES] = dq[i * count : (i + 1) * count]
            o_back[b + i, :, LANES:] = attended[i * count : (i + 1) * count]

    if seq_size <= 8:
        for b in range(0, seq_size, 2):
            queries(b, (b + 2) * count, 2)
    else:
        lax.fori_loop(0, seq_size, lambda b, _: (queries(b, rows, 1), 0)[1], 0)
    for d in range(seq_size):
        at = slice(d * count, (d + 1) * count)
        o_back[d, :, :LANES] = jnp.where(left, o_back[d, :, :LANES].astype(F32), dk[at, :] * scale).astype(BF)
        o_back[d, :, LANES:] = jnp.where(left, dv[at, :], o_back[d, :, LANES:].astype(F32)).astype(BF)


def backward_kernel(
    tiled, back, after, w_proj, w_qkv, n2, cot, w_out, gate, ssm, gated, normed, s_ref, a_ref, bc,
    o_out, o_after, o_n2, o_gate, o_g, o_msg, *o_more
):
    back = ready(back)
    seq_size, count = back.shape[0], back.shape[1]
    copies = seq_size // H
    left = lax.broadcasted_iota(jnp.int32, (count, LANES), 1) < HD
    dq, dk, dv, att = [], [], [], []
    for p in range(H // 2):
        a0, b0 = (back[2 * p * copies, :, tile(i)].astype(F32) for i in range(2))
        a1, b1 = (back[(2 * p + 1) * copies, :, tile(i)].astype(F32) for i in range(2))
        dq.append(jnp.where(left, a0, pltpu.roll(a1, HD, 1)))
        dk.append(jnp.where(left, pltpu.roll(a0, HD, 1), a1))
        dv.append(jnp.where(left, b0, pltpu.roll(b1, HD, 1)))
        att.append(jnp.where(left, pltpu.roll(b0, HD, 1), b1))
    attended = jnp.concatenate(att, axis=1).astype(BF)
    after, w_proj = ready(after, w_proj)
    width = after.shape[1]
    o_out[...] = (after[...] + dot(attended, w_proj[...])).astype(BF)
    sent(o_out)
    w_qkv, n2, cot = ready(w_qkv, n2, cot)
    grad_qkv = jnp.concatenate(dq + dk + dv, axis=1).astype(BF)
    if not tiled:
        o_more[0][...] = attended
        o_more[1][...] = grad_qkv
    grad_x, grad_gain = rms_back(after[...], n2[...], dot_nt(grad_qkv, w_qkv[...]))
    o_n2[...] = jnp.sum(grad_gain, axis=0, keepdims=True)
    grad_after = cot[...].astype(F32) + grad_x
    o_after[...] = grad_after
    branch = grad_after.astype(BF)
    if not tiled:
        o_more[2][...] = branch
    sent(o_n2, o_after)
    w_out, gate, ssm = ready(w_out, gate, ssm)
    inner_width = gate.shape[1]
    tiles = inner_width // LANES
    a_ref = ready(a_ref)
    states = a_ref.shape[0] // 8
    grad_gated = dot_nt(branch, w_out[...])
    for j in range(tiles):
        v = gate[:, tile(j)].astype(F32)
        sig = jax.nn.sigmoid(v)
        grad = grad_gated[:, tile(j)]
        to_rows(o_g, j, grad * (v * sig))
        grad_gate = grad * ssm[:, tile(j)] * (sig * (1.0 + v * (1.0 - sig)))
        o_gate[:, tile(j)] = grad_gate.astype(BF)
    sent(o_gate, o_g)
    gated, normed = ready(gated, normed)
    if tiled:
        partials(seq_size, gated, branch, normed, o_gate, attended, cot, *o_more)
        sent(*o_more[:2])
    s_ref, smem = ready(s_ref, bc)

    def one(i, later):
        t = count - 1 - i
        s, g = block(s_ref, t), block(o_g, t)
        return tuple(
            jnp.exp2(s * block(a_ref, n)) * (g * smem[t, states + n] + later[n])
            for n in range(states)
        )

    leaving = lax.fori_loop(0, count, one, (jnp.zeros((8, LANES), F32),) * states, unroll=4)
    for n in range(0, states, 2):
        value = jnp.concatenate([leaving[n], leaving[n + 1]], axis=0).astype(BF)
        for d in range(seq_size):
            o_msg[d, 8 * n : 8 * n + 16, :] = value


def states_kernel(
    seq_size, start, a_ref, bc, s_ref, dx_ref, inner, conv_w, conv_b, seg, o_every, o_slope, ext
):
    start, a_ref, smem, s_ref, dx_ref = ready(start, a_ref, bc, s_ref, dx_ref)
    count = smem.shape[0]
    states = a_ref.shape[0] // 8
    o_every[: states * 8, :] = start[...]

    def again(t, state):
        s, dx = block(s_ref, t), block(dx_ref, t)
        state = tuple(
            jnp.exp2(s * block(a_ref, n)) * state[n] + dx * smem[t, n] for n in range(states)
        )
        for n in range(states):
            o_every[pl.ds(pl.multiple_of(((t + 1) * states + n) * 8, 8), 8), :] = state[n]
        return state

    lax.fori_loop(0, count, again, tuple(start[8 * n : 8 * n + 8, :] for n in range(states)), unroll=2)
    sent(o_every)
    inner, conv_w, conv_b, seg = ready(inner, conv_w, conv_b, seg)
    ext[...] = inner[...].astype(F32)
    offset = offsets_in_sequence(seg, seq_size)
    for j in range(o_slope.shape[1] // LANES):
        pre = conv_tile(ext, conv_w, conv_b, offset, j, count)
        sig = jax.nn.sigmoid(pre)
        o_slope[:, tile(j)] = sig * (1.0 + pre * (1.0 - sig))


def fold8(values, sub):
    low4, low2, low1 = sub < 4, (sub & 2) == 0, (sub & 1) == 0
    four = []
    for k in range(4):
        a, b = values[k], values[k + 4]
        four.append(jnp.where(low4, a, b) + pltpu.roll(jnp.where(low4, b, a), 4, 0))
    two = []
    for k in range(2):
        a, b = four[k], four[k + 2]
        two.append(jnp.where(low2, a + pltpu.roll(a, 6, 0), b + pltpu.roll(b, 2, 0)))
    a, b = two
    return jnp.where(low1, a + pltpu.roll(a, 7, 0), b + pltpu.roll(b, 1, 0))


def adjoint_kernel(
    seq_size, back, totals, a_ref, bc, s_ref, dx_ref, g_ref, every, gs_ref, ai_ref, o_bc, o_a, held, sums, arrived
):
    back, totals, a_ref = ready(back, totals, a_ref)
    states = a_ref.shape[0] // 8
    count = s_ref.shape[0] // 8
    zero = jnp.zeros((8, LANES), F32)
    chunks = arrived.shape[0]
    span = count // chunks
    loads = []
    for c in range(chunks):
        first, last = c * span * states * 8, ((c + 1) * span + (c == chunks - 1)) * states * 8
        loads.append(pltpu.make_async_copy(every.at[first:last], held.at[first:last], arrived.at[c]))
    for load in reversed(loads):
        load.start()

    def join(i, carry):
        d = seq_size - 1 - i
        total = total_step(totals, d, 0)
        return tuple(
            jnp.exp2(block(a_ref, n) * total) * carry[n] + state_rows(back, d, n)
            for n in range(states)
        )

    leaving = lax.fori_loop(0, seq_size - 1 - lax.axis_index("seq"), join, (zero,) * states)
    smem, s_ref, dx_ref, g_ref = ready(bc, s_ref, dx_ref, g_ref)
    sub = lax.broadcasted_iota(jnp.int32, (8, LANES), 0)

    def one(last, i, carry):
        later, grad_a = carry
        t = last - i
        s, dx, g = block(s_ref, t), block(dx_ref, t), block(g_ref, t)
        new_later, new_grad_a, with_b, with_c = [], [], [], []
        grad_step, adjoint_in = zero, zero
        for n in range(states):
            a = block(a_ref, n)
            adjoint = g * smem[t, states + n] + later[n]
            passed = jnp.exp2(s * a) * adjoint
            before = held[pl.ds(pl.multiple_of((t * states + n) * 8, 8), 8), :]
            now = held[pl.ds(pl.multiple_of(((t + 1) * states + n) * 8, 8), 8), :]
            grad_decay = passed * before
            grad_step = grad_step + grad_decay * a
            adjoint_in = adjoint_in + adjoint * smem[t, n]
            new_later.append(passed)
            new_grad_a.append(grad_a[n] + grad_decay * s)
            with_b.append(adjoint * dx)
            with_c.append(g * now)
        here = pl.ds(pl.multiple_of(t * 8, 8), 8)
        gs_ref[here, :] = grad_step
        ai_ref[here, :] = adjoint_in
        for i, part in enumerate((with_b[:8], with_b[8:], with_c[:8], with_c[8:])):
            sums[pl.ds(pl.multiple_of(t * 32 + 8 * i, 8), 8), :] = fold8(part, sub)
        return tuple(new_later), tuple(new_grad_a)

    carry = (leaving, (zero,) * states)
    for c in reversed(range(chunks)):
        loads[c].wait()
        carry = lax.fori_loop(0, span, functools.partial(one, (c + 1) * span - 1), carry, unroll=4)
    grad_a = carry[1]
    sent(gs_ref, ai_ref)
    for n in range(states):
        o_a[8 * n : 8 * n + 8, :] = grad_a[n] * (LN2 * block(a_ref, n))
    columns = o_bc.shape[1]
    lane = lax.broadcasted_iota(jnp.int32, (LANES, columns), 1)
    grad_bc = jnp.zeros(o_bc.shape, F32)
    for q in range(2 * states):
        rows = sums[pl.ds(q, count, stride=2 * states), :]
        high = rows.astype(BF)
        low = (rows - high.astype(F32)).astype(BF)
        to_column = (lane == columns - 2 * states + q).astype(BF)
        grad_bc = grad_bc + dot(high, to_column) + dot(low, to_column)
    o_bc[...] = grad_bc


def inner_kernel(
    seq_size, gs_ref, ai_ref, g_ref, mixed, step_pre, low, w_dt, grad_bc, grad_a, w_xp, inner, slope, conv_w, d_skip,
    seg, normed, grad_n2,
    *rest,
):
    o_first, o_second, o_inner, *own_small, ext, gext, grad_w = rest
    small = own_small[0] if own_small else o_second.ref
    gs_ref, ai_ref, g_ref = ready(gs_ref, ai_ref, g_ref)
    grad_bc, grad_a = ready(grad_bc, grad_a)
    count = g_ref.shape[0] // 8
    states = grad_a.shape[0] // 8
    mixed, step_pre, low, w_dt, w_xp, inner = ready(mixed, step_pre, low, w_dt, w_xp, inner)
    slope, conv_w, d_skip, seg, normed, grad_n2 = ready(slope, conv_w, d_skip, seg, normed, grad_n2)
    inner_width = mixed.shape[1]
    tiles = inner_width // LANES
    rank = w_dt.shape[0]
    taps = conv_w.shape[0]
    small[...] = jnp.zeros_like(small)
    small[104 * 8 : (104 + states) * 8, :] = grad_a[...]
    offset = offsets_in_sequence(seg, seq_size)
    halves = []
    for j in range(tiles):
        mix = mixed[:, tile(j)].astype(F32)
        pre = step_pre[:, tile(j)]
        grad_step = LN2 * from_rows(gs_ref, j, count) + mix * from_rows(ai_ref, j, count)
        grad_pre = grad_step * jax.nn.sigmoid(pre)
        small[101 * 8 + j : 101 * 8 + j + 1, :] = jnp.sum(grad_pre, axis=0, keepdims=True)
        grad_ssm = from_rows(g_ref, j, count)
        small[102 * 8 + j : 102 * 8 + j + 1, :] = jnp.sum(grad_ssm * mix, axis=0, keepdims=True)
        halves.append(grad_pre.astype(BF))
    half = jnp.concatenate(halves, axis=1)
    grad_w_dt = dot_tn(low[...], half)
    padded_dt = jnp.concatenate([w_dt[...], jnp.zeros((2 * states, inner_width), BF)], axis=0)
    grad_selector = (dot_nt(half, padded_dt) + grad_bc[...]).astype(BF)
    grad_w_xp = dot_tn(grad_selector, mixed[...])
    from_selector = dot(grad_selector, w_xp[...])
    ext[...] = inner[...].astype(F32)
    gext[...] = jnp.zeros_like(gext)
    for j in range(tiles):
        to_rows(small.at[pl.ds(0, 64 * 8)], j, grad_w_xp[:, tile(j)])
        to_rows(small.at[pl.ds(64 * 8, 32 * 8)], j, grad_w_dt[:, tile(j)])
        grad_mixed = (
            softplus(step_pre[:, tile(j)]) * from_rows(ai_ref, j, count)
            + from_rows(g_ref, j, count) * d_skip[:, tile(j)]
            + from_selector[:, tile(j)]
        )
        grad_pre = grad_mixed * slope[:, tile(j)]
        small[100 * 8 + j : 100 * 8 + j + 1, :] = jnp.sum(grad_pre, axis=0, keepdims=True)
        for k in range(taps):
            shifted = pl.ds(HALO - taps + 1 + k, count)
            usable = jnp.where(offset >= taps - 1 - k, grad_pre, 0.0)
            row = (96 + k) * 8 + j
            small[row : row + 1, :] = jnp.sum(usable * ext[shifted, tile(j)], axis=0, keepdims=True)
            gext[shifted, tile(j)] += conv_w[k : k + 1, tile(j)] * usable
    o_inner[...] = gext[...].astype(BF)
    sent(o_inner)
    width = grad_n2.shape[1]
    for j in range(width // LANES):
        small[103 * 8 + 4 + j : 103 * 8 + 5 + j, :] = grad_n2[:, tile(j)]
    if not own_small:
        o_first[...] = dot_tn(normed[...], o_inner[...])
        return
    grad_w[...] = dot_tn(normed[...], o_inner[...])
    for to, x, s, at in receivers((o_first, o_second), seq_size):
        to[x * seq_size + s, :LANES, :] = grad_w[pl.ds(pl.multiple_of(at * LANES, LANES), LANES), tile(s)].astype(BF)
        rows = small.shape[0] // (width // LANES * seq_size)
        here = pl.ds(pl.multiple_of((at * seq_size + s) * rows, rows), rows)
        to[x * seq_size + s, LANES:, :] = small[here, :].astype(BF)


def receivers(results, seq_size, mine=0):
    core = lax.rem(lax.axis_index("dp"), 2)
    for to, side in zip(results, (core, 1 - core)):
        for x in range(to.shape[0] // seq_size):
            for s in range(seq_size):
                yield to, x, s, 2 * lax.bitwise_xor(x, mine) + side


def partials(seq_size, gated, branch, normed, grad_gate, attended, cot, keep, send, out, gate, proj):
    out[...] = dot_tn(gated[...], branch)
    gate[...] = dot_tn(normed[...], grad_gate[...])
    proj[...] = dot_tn(attended, cot[...])
    across = out.shape[1] // LANES
    down = seq_size // across
    mine = lax.axis_index("dp") // 2
    for to, x, s, at in receivers((keep, send), seq_size, mine):
        rows = pl.ds(pl.multiple_of((at * down + s // across) * LANES, LANES), LANES)
        to[x * seq_size + s, :LANES, :] = out[rows, tile(s % across)].astype(BF)
        rows = pl.ds(pl.multiple_of(at * LANES, LANES), LANES)
        to[x * seq_size + s, LANES : 2 * LANES, :] = gate[rows, tile(s)].astype(BF)
        rows = pl.ds(pl.multiple_of((at * down + s // across) * HD, HD), HD)
        to[x * seq_size + s, 2 * LANES :, :] = proj[rows, tile(s % across)].astype(BF)


def tokens_kernel(grad_inner, w_in, grad_gate, tok, halo, n1, grad_after, o_tok, o_halo, o_n1):
    grad_inner, w_in, grad_gate = ready(grad_inner, w_in, grad_gate)
    inner_width = grad_inner.shape[1]
    grad_normed = dot_nt(grad_inner[...], w_in[:, :inner_width])
    own = dot_nt(grad_gate[...], w_in[:, inner_width:])
    grad_normed = jnp.concatenate([grad_normed[:HALO], grad_normed[HALO:] + own], axis=0)
    tok, halo, n1, grad_after = ready(tok, halo, n1, grad_after)
    x = jnp.concatenate([halo[...], tok[...]], axis=0).astype(F32)
    grad_x, grad_gain = rms_back(x, n1[...], grad_normed)
    o_tok[...] = grad_after[...] + grad_x[HALO:]
    o_halo[...] = grad_x[HALO - 8 : HALO]
    grad_gain = jnp.sum(grad_gain, axis=0, keepdims=True)
    tiles = grad_gain.shape[1] // LANES
    rows = [grad_gain[:, tile(j)] for j in range(tiles)] + [jnp.zeros((16 - tiles, LANES), F32)]
    o_n1[...] = jnp.concatenate(rows, axis=0).astype(BF)


def head_products_kernel(normed, back, *rest):
    *outs, grad, last = rest
    normed, back = ready(normed, back)
    both = back[...].reshape(back.shape[0] * back.shape[1], 2 * LANES)
    grad[...] = dot_tn(normed[...], both[:, :LANES])
    last[...] = dot_tn(normed[...], both[:, LANES:])
    left = lax.broadcasted_iota(jnp.int32, (HD, LANES), 1) < HD
    for distance, to in enumerate(outs):
        g = lax.bitwise_xor(lax.axis_index("dp"), distance)
        to[: 2 * HD, :] = grad[pl.ds(pl.multiple_of(g * LANES, LANES), LANES), :].astype(BF)
        low = last[pl.ds(pl.multiple_of(g * LANES, LANES), HD), :]
        high = last[pl.ds(pl.multiple_of(g * LANES + HD, HD), HD), :]
        to[2 * HD :, :] = jnp.where(left, low, pltpu.roll(high, HD, 1)).astype(BF)


def early_sum_kernel(parts, *heads):
    *heads, o_sum = heads
    heads, parts = ready(*heads), ready(parts)
    head = heads[0][...].astype(F32)
    for part in heads[1:]:
        head = head + part[...].astype(F32)
    total = parts[0].astype(F32)
    for d in range(1, parts.shape[0]):
        total = total + parts[d].astype(F32)
    rows = total.shape[0]
    o_sum[:rows, :] = total.astype(BF)
    o_sum[rows:, :] = head.astype(BF)


def sum_and_spread_kernel(parts, own, o_all):
    parts, own = ready(parts, own)
    total = parts[0].astype(F32)
    for d in range(1, parts.shape[0]):
        total = total + parts[d].astype(F32)
    total = total.astype(BF)
    rows = total.shape[0]
    for d in range(o_all.shape[0]):
        o_all[d, :rows, :] = total
        o_all[d, rows:, :] = own[...]


def early_assembly_kernel(groups, early, w_in, o_out, o_proj, o_qkv, o_in, pieces, out, proj, qkv, gate, loads, stores):
    seq_size = early.shape[0] // groups
    inner_width, width = gate.shape[1], proj.shape[1]
    across = width // LANES
    left = lax.broadcasted_iota(jnp.int32, (LANES, LANES), 1) < HD
    at = 2 * LANES + HD

    def pairs(a, b):
        a, b = a.astype(F32), b.astype(F32)
        mask = left[: a.shape[0]]
        return jnp.where(mask, a, pltpu.roll(b, HD, 1)), jnp.where(mask, pltpu.roll(a, HD, 1), b)

    own = [slice(g * seq_size, (g + 1) * seq_size) for g in range(groups)]
    arrivals = [pltpu.make_async_copy(early.at[own[g]], pieces.at[own[g]], loads.at[g]) for g in range(groups)]
    for copy in arrivals:
        copy.start()
    copies = []
    for g in range(groups):
        arrivals[g].wait()
        down = seq_size // across
        for s in range(seq_size):
            piece = pieces[g * seq_size + s]
            row = g * down + s // across
            out[tile(row), tile(s % across)] = piece[:LANES].astype(F32)
            gate[tile(g), tile(s)] = piece[LANES : 2 * LANES].astype(F32)
            proj[row * HD : (row + 1) * HD, tile(s % across)] = piece[2 * LANES : at].astype(F32)
        for p in range(seq_size // 2):
            a, b = pieces[g * seq_size + 2 * p], pieces[g * seq_size + 2 * p + 1]
            first, second, third = (slice(i * width + p * LANES, i * width + (p + 1) * LANES) for i in range(3))
            qkv[tile(g), first], qkv[tile(g), second] = pairs(a[at : at + LANES], b[at : at + LANES])
            low, high = pairs(a[at + LANES :], b[at + LANES :])
            qkv[g * LANES : g * LANES + HD, third] = low
            qkv[g * LANES + HD : (g + 1) * LANES, third] = high
        for i, (source, target, rows) in enumerate(
            ((out, o_out, down * LANES), (proj, o_proj, down * HD), (qkv, o_qkv, LANES), (gate, o_in, LANES))
        ):
            here = slice(g * rows, (g + 1) * rows)
            target = target.at[here, inner_width:] if i == 3 else target.at[here]
            copies.append(pltpu.make_async_copy(source.at[here], target, stores.at[4 * g + i]))
            copies[-1].start()
    for copy in copies:
        copy.wait()


def late_assembly_kernel(
    groups, mine, other, o_in, o_n1, o_conv_w, o_conv_b, o_xp, o_dt, o_dtb, o_a, o_skip, o_n2, inner, small, sems
):
    mine, other = ready(mine, other)
    seq_size = mine.shape[0] * 2 // groups
    width, inner_width = inner.shape
    rows = mine.shape[1] - LANES - 16
    copies = []
    for ref, x, s, g in receivers((mine, other), seq_size):
        at = pl.ds(pl.multiple_of(g * LANES, LANES), LANES)
        inner[at, tile(s)] = ref[x * seq_size + s, :LANES, :].astype(F32)
        here = pl.ds(pl.multiple_of((g * seq_size + s) * rows, rows), rows)
        small[here, :] = ref[x * seq_size + s, LANES : LANES + rows, :].astype(F32)
        if s == seq_size - 1:
            copies.append(pltpu.make_async_copy(inner.at[at], o_in.at[at, :inner_width], sems.at[len(copies)]))
            copies[-1].start()
    for j in range(inner_width // LANES):
        value = from_rows(small, j, SMALL)
        for ref, first, last in (
            (o_xp, 0, 64), (o_dt, 64, 96), (o_conv_w, 96, 100), (o_conv_b, 100, 101), (o_dtb, 101, 102),
            (o_skip, 102, 103), (o_a, 104, 120),
        ):
            ref[:, tile(j)] = value[first:last]
        if j >= width // LANES:
            o_n2[:, tile(j - width // LANES)] = value[103:104]
    sent(o_conv_w, o_conv_b, o_xp, o_dt, o_dtb, o_a, o_skip, o_n2)
    gain = jnp.zeros((16, LANES), F32)
    for source in (mine, other):
        for d in range(source.shape[0]):
            gain = gain + source[d, LANES + rows :, :].astype(F32)
    for j in range(width // LANES):
        o_n1[:, tile(j)] = gain[j : j + 1]
    for copy in copies:
        copy.wait()


class Held:
    def __init__(self, buffer, copy):
        self.ref, self.copy, self.shape = buffer, copy, buffer.shape
        self.done = False

    def __getitem__(self, at):
        return self.ref[at]

    def __setitem__(self, at, value):
        self.ref[at] = value


def ready(*held):
    for one in held:
        if not one.done:
            one.copy.wait()
            one.done = True
    refs = tuple(one.ref for one in held)
    return refs[0] if len(refs) == 1 else refs


def sent(*held):
    for one in held:
        if not one.done:
            one.copy.start()
            one.done = True


IN_HBM = pl.BlockSpec(memory_space=pltpu.HBM)


def call(
    kernel, outs, scratch, *args, name=None, us=1, raw=(), raw_out=(), scalars=(), views=None, aliases=None, after=(),
    near=(), vmem=60,
):
    views = views or {}
    count, first_out = len(args), len(args) + len(after)
    first_scratch = first_out + len(outs)
    buffers = []
    for i, arg in enumerate(args):
        shape = jax.eval_shape(lambda v, i=i: v[views[i]], arg).shape if i in views else arg.shape
        kind = pltpu.SMEM if i in scalars else pltpu.VMEM
        buffers.append(None if i in raw else kind(shape, arg.dtype))
    for i, (shape, dtype) in enumerate(outs):
        buffers.append(None if i in raw_out else pltpu.VMEM(shape, dtype))
    used = [b for b in buffers if b is not None]

    def run(*refs):
        given = list(refs[:count]) + list(refs[first_out:first_scratch])
        own = list(refs[first_scratch : first_scratch + len(used)])
        sems = refs[first_scratch + len(used)]
        passed = []
        for i, (ref, buffer) in enumerate(zip(given, buffers)):
            if buffer is None:
                passed.append(ref)
                continue
            buffer = own.pop(0)
            if i < count:
                source = ref.at[views[i]] if i in views else ref
                copy = pltpu.make_async_copy(source, buffer, sems.at[i])
                copy.start()
            else:
                copy = pltpu.make_async_copy(buffer, ref, sems.at[i])
            passed.append(Held(buffer, copy))
        kernel(*passed, *refs[first_scratch + len(used) + 1 :])
        ready(*[p for p in passed[:count] if isinstance(p, Held)])
        results = [p for p in passed[count:] if isinstance(p, Held)]
        sent(*results)
        for result in results:
            result.copy.wait()

    return pl.pallas_call(
        run,
        out_shape=[jax.ShapeDtypeStruct(s, d) for s, d in outs],
        in_specs=[pl.BlockSpec(memory_space=pl.ANY) if i in near else IN_HBM for i in range(first_out)],
        out_specs=[IN_HBM] * len(outs),
        scratch_shapes=used + [pltpu.SemaphoreType.DMA((len(buffers),))] + scratch,
        compiler_params=pltpu.CompilerParams(vmem_limit_bytes=vmem * 1024 * 1024),
        cost_estimate=pl.CostEstimate(flops=us * 10**9 + 1000, bytes_accessed=1000, transcendentals=0),
        input_output_aliases=aliases or {},
        name=name,
    )(*args, *after)


def exchange(value, axes):
    return lax.all_to_all(value, axes, 0, 0, tiled=True)


def own_core(value, groups, seq_size):
    peers = [
        [g * seq_size + s for g in range(core, groups, 2) for s in range(seq_size)] for core in range(2)
    ]
    return lax.all_to_all(value, ("dp", "seq"), 0, 0, tiled=True, axis_index_groups=peers)


def other_core(value, groups):
    return lax.ppermute(value, "dp", [(g, g ^ 1) for g in range(groups)])


def body(
    tokens, seg_start, norm_one, w_in, conv_w, conv_b, w_xproj, w_dt, dt_bias, a_log, d_skip,
    w_out, norm_two, w_qkv, w_proj, cotangent,
):
    count, width = tokens.shape
    inner_width = w_in.shape[1] // 2
    states = a_log.shape[1]
    rank = w_dt.shape[0]
    taps = conv_w.shape[0]
    groups, seq_size = lax.axis_size("dp"), lax.axis_size("seq")
    rows = count * seq_size
    ext_rows = HALO + count
    tiled = inner_width == seq_size * LANES and width == groups * LANES and seq_size == H
    peers = groups // 2 * seq_size
    line = lambda v: v.reshape(1, -1)
    seg = line(seg_start)
    n1, n2, cb, dtb, skip = (line(v) for v in (norm_one, norm_two, conv_b, dt_bias, d_skip))
    vmem, smem = pltpu.VMEM, pltpu.SMEM((count, 2 * states), F32)
    sem = pltpu.SemaphoreType.DMA
    blocks = ((count * 8, LANES), F32)
    ends_at = states * 8
    halo = lax.ppermute(tokens[count - HALO :], "seq", [(i, i + 1) for i in range(seq_size - 1)])
    msg, normed, inner, gate, mixed, bc, low, step_pre, s, dx, a = call(
        functools.partial(forward_kernel, seq_size),
        [
            ((seq_size, states * 8 + 32, LANES), BF), ((ext_rows, width), BF),
            ((ext_rows, inner_width), BF), ((count, inner_width), BF), ((count, inner_width), BF), ((count, 2 * states), F32),
            ((count, rank), BF), ((count, inner_width), F32), blocks, blocks, ((states * 8, LANES), F32),
        ],
        [vmem((ext_rows, inner_width), F32), smem, sem],
        tokens, halo, n1, w_in, conv_w, cb, w_xproj.T, w_dt, dtb, a_log.T, seg,
        name="forward", us=0, near=(1,),
    )
    msg = exchange(msg, "seq")
    (grad_att,) = call(
        grad_att_kernel, [((count, width), BF)], [], cotangent, w_proj, name="grad_att", us=0
    )
    qkvg, start, ssm, after, gated, normed_two = call(
        middle_kernel,
        [
            ((seq_size, count, 2 * LANES), BF), ((states * 8, LANES), F32), ((count, inner_width), F32),
            ((count, width), F32), ((count, inner_width), BF), ((count, width), BF),
        ],
        [vmem(*blocks)],
        msg, a, bc, s, dx, mixed, gate, skip, tokens, w_out, n2, w_qkv, grad_att,
        name="middle", us=0, scalars=(2,), views={0: np.s_[:, : ends_at + 16, :]}, near=(0,),
    )
    qkvg = exchange(qkvg, "seq")
    every, slope = call(
        functools.partial(states_kernel, seq_size),
        [(((count + 1) * states * 8, LANES), F32), ((count, inner_width), F32)],
        [vmem((ext_rows, inner_width), F32)],
        start, a, bc, s, dx, inner, conv_w, cb, seg, name="states", us=0, scalars=(2,),
    )
    (back,) = call(
        attention_kernel,
        [((seq_size, count, 2 * LANES), BF)],
        [vmem((rows, LANES), BF)] * 4 + [vmem((rows, LANES), F32)] * 2,
        qkvg, msg, name="attention", us=0, views={1: np.s_[:, ends_at + 16 :, :]}, after=(every,), near=(0,),
    )
    back_own = exchange(back, "seq")
    pieces = [((peers, 2 * LANES + HD, LANES), BF)] * 2
    rest = [((count, width), BF), ((count, 3 * width), BF), ((count, width), BF)]
    out, grad_after, grad_n2, grad_gate, g, adj, *more = call(
        functools.partial(backward_kernel, tiled),
        [
            ((count, width), BF), ((count, width), F32), ((1, width), F32), ((count, inner_width), BF), blocks,
            ((seq_size, states * 8, LANES), BF),
        ] + (pieces if tiled else rest),
        [vmem((inner_width, width), F32), vmem((width, inner_width), F32), vmem((width, width), F32)] if tiled else [],
        back_own, after, w_proj, w_qkv, n2, cotangent, w_out, gate, ssm, gated, normed, s, a, bc,
        name="backward", us=0, scalars=(13,), views={10: np.s_[HALO:, :]}, near=(0,),
    )
    adj = exchange(adj, "seq")
    between = ()
    if tiled:
        normed_two_all = lax.all_gather(normed_two, "seq", axis=0, tiled=True)
        keep, send = more
        add = lambda *parts: sum(part.astype(F32) for part in parts).astype(BF)
        received = other_core(send, groups)
        across = add(keep[seq_size:], received[seq_size:])
        across = lax.ppermute(across, "dp", [(g, g ^ 2) for g in range(groups)])
        part = add(keep[:seq_size], received[:seq_size], across)
        between = (part,)
        part = exchange(part, "seq")
    gs, ai, grad_bc, grad_a = call(
        functools.partial(adjoint_kernel, seq_size),
        [blocks, blocks, ((count, rank + 2 * states), F32), ((states * 8, LANES), F32)],
        [vmem(((count + 1) * states * 8, LANES), F32), vmem((count * 2 * states, LANES), F32), sem((8,))],
        adj, msg, a, bc, s, dx, g, every, name="adjoint", us=0, raw=(7,), scalars=(3,), near=(0,),
        views={1: np.s_[:, ends_at : ends_at + 16, :]}, after=between,
    )
    small_rows = SMALL * 8 // (groups * seq_size)
    *sums, small, grad_inner = call(
        functools.partial(inner_kernel, seq_size),
        ([((peers, LANES + small_rows, LANES), BF)] * 2 if tiled else [((width, inner_width), F32), ((SMALL * 8, LANES), F32)])
        + [((ext_rows, inner_width), BF)],
        ([vmem((SMALL * 8, LANES), F32)] if tiled else [])
        + [vmem((ext_rows, inner_width), F32), vmem((ext_rows, inner_width), F32), vmem((width, inner_width), F32)],
        gs, ai, g, mixed, step_pre, low, w_dt, grad_bc, grad_a, w_xproj.T, inner, slope, conv_w, skip, seg, normed, grad_n2,
        name="inner", us=0,
    )
    grad_tokens, grad_halo, grad_n1 = call(
        tokens_kernel, [((count, width), F32), ((8, width), F32), ((16, LANES), BF)], [],
        grad_inner, w_in, grad_gate, tokens, halo, n1, grad_after, name="tokens", us=0,
    )
    returned = lax.ppermute(grad_halo, "seq", [(i + 1, i) for i in range(seq_size - 1)])
    grad_tokens = grad_tokens.at[count - 8 :].add(returned)
    flat = lambda v: v.reshape(-1)
    if tiled:
        head, *heads = call(
            head_products_kernel, [((3 * HD, LANES), BF)] * groups, [vmem((width, LANES), F32)] * 2,
            normed_two_all, back, name="head_products", us=0, after=(grad_n1,),
        )
        heads = [
            lax.ppermute(piece, "dp", [(g, g ^ distance) for g in range(groups)])
            for distance, piece in enumerate(heads, 1)
        ]
        (early,) = call(
            early_sum_kernel, [((part.shape[1] + head.shape[0], LANES), BF)], [], part, head, *heads,
            name="early_sum", us=0, vmem=40, after=(grad_n1,), near=(0, 2, 3, 4),
        )
        late = add(sums[0], other_core(small, groups))
        late, early = lax.optimization_barrier((late, early))
        late = own_core(late, groups, seq_size)
        early = lax.all_gather(early, ("dp", "seq"))
        (late,) = call(
            sum_and_spread_kernel, [((peers, late.shape[1] + 16, LANES), BF)], [], late, grad_n1, name="late_sum", us=0, vmem=40,
            near=(0,),
        )
        mine = own_core(late, groups, seq_size)
        mine, grad_tokens = lax.optimization_barrier((mine, grad_tokens))
        row = lambda n: ((n, inner_width), F32)
        half, g_n1, g_conv_w, g_conv_b, g_xp, g_dt, g_dtb, g_a, g_skip, g_n2 = call(
            functools.partial(late_assembly_kernel, groups),
            [
                ((width, 2 * inner_width), F32), ((1, width), F32), row(taps), row(1), row(2 * states + rank), row(rank),
                row(1), row(states), row(1), ((1, width), F32),
            ],
            [vmem((width, inner_width), F32), vmem((SMALL * 8, LANES), F32), sem((4,))],
            mine, other_core(mine, groups), name="late_assembly", us=0, vmem=40, raw_out=(0,), near=(0, 1),
        )
        whole = [((inner_width, width), F32), ((width, width), F32), ((width, 3 * width), F32)]
        grad_w_out, grad_w_proj, grad_w_qkv, grad_w_in = call(
            functools.partial(early_assembly_kernel, groups),
            whole + [((width, 2 * inner_width), F32)],
            [vmem(early.shape, BF)] + [vmem(*v) for v in whole] + [vmem((width, inner_width), F32), sem((4,)), sem((16,))],
            early, half, name="early_assembly", us=0, raw=(0, 1), raw_out=(0, 1, 2, 3), aliases={1: 3},
        )
        g_xp, g_a, g_n1, g_n2 = g_xp.T, g_a.T, flat(g_n1), flat(g_n2)
    else:
        attended, grad_qkv, branch = more
        small = small.reshape(SMALL, inner_width)
        g_n1 = flat(grad_n1[: width // LANES].astype(F32))
        both = jnp.concatenate([sums[0], dot_tn(normed[HALO:], grad_gate)], axis=1)
        grad_w_in, grad_w_out, grad_w_qkv, grad_w_proj, small, g_n1 = lax.psum(
            (both, dot_tn(gated, branch), dot_tn(normed_two, grad_qkv), dot_tn(attended, cotangent), small, g_n1), ("dp", "seq")
        )
        g_xp, g_dt, g_conv_w, g_conv_b, g_dtb = small[:64].T, small[64:96], small[96:100], small[100], small[101]
        g_skip, g_n2, g_a = small[102], small[103, width:], small[104:120].T
    return (out, grad_tokens, g_n1, grad_w_in, g_conv_w, flat(g_conv_b), g_xp, g_dt, flat(g_dtb), g_a, flat(g_skip),
            grad_w_out, g_n2, grad_w_qkv, grad_w_proj)


def solution(mesh):
    split, copied = P(("dp", "seq"), None), P()
    return jax.shard_map(
        body,
        mesh=mesh,
        in_specs=(split, P(("dp", "seq"))) + (copied,) * 13 + (split,),
        out_specs=(split, split) + (copied,) * 13,
        check_vma=False,
    )
```

```python
import functools

import jax
import jax.numpy as jnp
import numpy as np
from jax import lax
from jax.experimental import pallas as pl
from jax.experimental.pallas import tpu as pltpu
from jax.sharding import PartitionSpec as P

H = 8
HD = 64
LANES = 128
HALO = 16
SMALL = 128
RESET = 1e30
EPSILON = 1e-05
LOG2E = 1.4426950408889634
LN2 = 0.6931471805599453
BF = jnp.bfloat16
F32 = jnp.float32


def dot(a, b):
    return jnp.dot(a, b, preferred_element_type=F32)


def dot_nt(a, b):
    return lax.dot_general(a, b, (((1,), (1,)), ((), ())), preferred_element_type=F32)


def dot_tn(a, b):
    return lax.dot_general(a, b, (((0,), (0,)), ((), ())), preferred_element_type=F32)


def tile(j):
    return slice(j * LANES, (j + 1) * LANES)


def softplus(x):
    u = jnp.exp(-jnp.abs(x))
    series = u * (1.0 - u * (0.5 - u * (1.0 / 3.0 - u * 0.25)))
    return jnp.maximum(x, 0.0) + jnp.where(u < 0.015, series, jnp.log(1.0 + u))


def rms_parts(x):
    return lax.rsqrt(jnp.mean(x * x, axis=-1, keepdims=True) + EPSILON)


def rms_back(x, gain, grad):
    r = rms_parts(x)
    scaled = grad * gain
    inner = jnp.mean(x * scaled, axis=-1, keepdims=True)
    return r * scaled - x * (r * r * r * inner), grad * x * r


def to_rows(ref, j, value):
    ref[pl.ds(j, value.shape[0], stride=8), :] = value


def from_rows(ref, j, count):
    return ref[pl.ds(j, count, stride=8), :]


def block(ref, t):
    return ref[pl.ds(pl.multiple_of(t * 8, 8), 8), :]


def offsets_in_sequence(seg_ref, seq_size):
    count = seg_ref.shape[1]
    base = (lax.axis_index("dp") * seq_size + lax.axis_index("seq")) * count
    places = base + lax.broadcasted_iota(jnp.int32, (1, count), 1)
    row = (places - seg_ref[...]).astype(F32)
    return jnp.transpose(jnp.broadcast_to(row, (LANES, count)))


def conv_tile(ext_ref, w_ref, b_ref, offset, j, count):
    taps = w_ref.shape[0]
    pre = jnp.broadcast_to(b_ref[:, tile(j)], (count, LANES))
    for k in range(taps):
        rows = ext_ref[pl.ds(HALO - taps + 1 + k, count), tile(j)]
        pre = pre + jnp.where(offset >= taps - 1 - k, w_ref[k : k + 1, tile(j)] * rows, 0.0)
    return pre


def forward_kernel(
    seq_size, tok, halo, n1, w_in, conv_w, conv_b, w_xp, w_dt, dtb, a_log, seg,
    o_msg, o_normed, o_inner, o_gate, o_mixed, o_bc, o_low, o_pre, o_s, o_dx, o_a,
    ext, smem, sem,
):
    tok, halo, n1, seg = ready(tok, halo, n1, seg)
    count = tok.shape[0]
    states = a_log.shape[0]
    inner_width = conv_w.shape[1]
    tiles = inner_width // LANES
    rank = w_dt.shape[0]
    x = jnp.concatenate([halo[...], tok[...]], axis=0).astype(F32)
    normed = (x * rms_parts(x) * n1[...]).astype(BF)
    o_normed[...] = normed
    sent(o_normed)
    w_in = ready(w_in)
    inner = dot(normed, w_in[:, :inner_width]).astype(BF)
    o_inner[...] = inner
    sent(o_inner)
    ext[...] = inner.astype(F32)
    conv_w, conv_b, w_xp, w_dt, dtb, a_log = ready(conv_w, conv_b, w_xp, w_dt, dtb, a_log)
    offset = offsets_in_sequence(seg, seq_size)
    for j in range(tiles):
        pre = conv_tile(ext, conv_w, conv_b, offset, j, count)
        o_mixed[:, tile(j)] = (pre * jax.nn.sigmoid(pre)).astype(BF)
    sent(o_mixed)
    selector = dot_nt(o_mixed[...], w_xp[...])
    low = selector[:, :rank].astype(BF)
    o_low[...] = low
    o_bc[...] = selector[:, rank:]
    sent(o_low, o_bc)
    copy = pltpu.make_async_copy(o_bc.ref, smem, sem)
    copy.start()
    o_pre[...] = dot(low, w_dt[...]) + dtb[...]
    sent(o_pre)
    o_gate[...] = dot(normed[HALO:], w_in[:, inner_width:]).astype(BF)
    sent(o_gate)
    for j in range(tiles):
        step = softplus(o_pre[:, tile(j)])
        to_rows(o_s, j, jnp.where(offset == 0.0, RESET, step))
        to_rows(o_dx, j, step * o_mixed[:, tile(j)].astype(F32))
        to_rows(o_a, j, -LOG2E * jnp.exp(a_log[:, tile(j)]))
    sent(o_s, o_dx, o_a)
    copy.wait()

    def one(t, carry):
        total, state = carry
        s, dx = block(o_s, t), block(o_dx, t)
        return total + s, tuple(
            jnp.exp2(s * block(o_a, n)) * state[n] + dx * smem[t, n] for n in range(states)
        )

    zero = jnp.zeros((8, LANES), F32)
    total, state = lax.fori_loop(0, count, one, (zero, (zero,) * states), unroll=4)
    high = total.astype(BF).astype(F32)
    seg_local = (seg[...] - lax.axis_index("dp") * (seq_size * count)).astype(F32)
    seg_high = jnp.floor(seg_local * (1.0 / 64.0))
    last = jnp.concatenate([seg_high, seg_local - 64.0 * seg_high, jnp.zeros((14, LANES), F32)], axis=0)
    blocks = [jnp.concatenate([state[n], state[n + 1]], axis=0) for n in range(0, states, 2)]
    blocks += [jnp.concatenate([high, total - high], axis=0), last]
    for i, value in enumerate(blocks):
        value = value.astype(BF)
        for d in range(seq_size):
            o_msg[d, 16 * i : 16 * i + 16, :] = value


def total_step(msg, d, states):
    rows = msg[d, states * 8 : states * 8 + 16, :].astype(F32)
    return rows[:8] + rows[8:]


def state_rows(msg, d, n):
    rows = msg[d, 16 * (n // 2) : 16 * (n // 2) + 16, :].astype(F32)
    return rows[:8] if n % 2 == 0 else rows[8:]


def middle_kernel(
    msg, a_ref, bc, s_ref, dx_ref, mixed, gate, d_skip, tok, w_out, n2, w_qkv, cot, w_proj,
    o_qkvg, o_start, o_ssm, o_after, o_gated, o_normed,
    y_ref,
):
    msg, a_ref = ready(msg, a_ref)
    states = a_ref.shape[0] // 8
    zero = jnp.zeros((8, LANES), F32)

    def join(d, carry):
        total = total_step(msg, d, states)
        return tuple(
            jnp.exp2(block(a_ref, n) * total) * carry[n] + state_rows(msg, d, n)
            for n in range(states)
        )

    start = lax.fori_loop(0, lax.axis_index("seq"), join, (zero,) * states)
    for n in range(states):
        o_start[8 * n : 8 * n + 8, :] = start[n]
    sent(o_start)
    s_ref, dx_ref, smem = ready(s_ref, dx_ref, bc)
    count = smem.shape[0]

    def one(t, state):
        s, dx = block(s_ref, t), block(dx_ref, t)
        state = tuple(
            jnp.exp2(s * block(a_ref, n)) * state[n] + dx * smem[t, n] for n in range(states)
        )
        parts = [state[n] * smem[t, states + n] for n in range(states)]
        while len(parts) > 1:
            parts = [a + b for a, b in zip(parts[::2], parts[1::2])]
        y_ref[pl.ds(pl.multiple_of(t * 8, 8), 8), :] = parts[0]
        return state

    lax.fori_loop(0, count, one, start, unroll=4)
    mixed, gate, d_skip, tok, w_out, n2 = ready(mixed, gate, d_skip, tok, w_out, n2)
    inner_width, width = mixed.shape[1], tok.shape[1]
    tiles = inner_width // LANES
    for j in range(tiles):
        ssm = from_rows(y_ref, j, count) + d_skip[:, tile(j)] * mixed[:, tile(j)].astype(F32)
        o_ssm[:, tile(j)] = ssm
        v = gate[:, tile(j)].astype(F32)
        o_gated[:, tile(j)] = (ssm * (v * jax.nn.sigmoid(v))).astype(BF)
    sent(o_ssm, o_gated)
    after = tok[...].astype(F32) + dot(o_gated[...], w_out[...])
    o_after[...] = after
    sent(o_after)
    normed = (after * rms_parts(after) * n2[...]).astype(BF)
    o_normed[...] = normed
    sent(o_normed)
    w_qkv, cot, w_proj = ready(w_qkv, cot, w_proj)
    qkv = dot(normed, w_qkv[...])
    grad_att = dot_nt(cot[...], w_proj[...])
    copies = o_qkvg.shape[0] // H
    left = lax.broadcasted_iota(jnp.int32, (count, LANES), 1) < HD
    for p in range(H // 2):
        q, k, v = (qkv[:, i * width + p * LANES : i * width + (p + 1) * LANES] for i in range(3))
        g = grad_att[:, tile(p)]
        first = (jnp.where(left, q, pltpu.roll(k, HD, 1)), jnp.where(left, v, pltpu.roll(g, HD, 1)))
        second = (jnp.where(left, pltpu.roll(q, HD, 1), k), jnp.where(left, pltpu.roll(v, HD, 1), g))
        for h, pair in ((2 * p, first), (2 * p + 1, second)):
            for i, value in enumerate(pair):
                value = value.astype(BF)
                for r in range(copies):
                    o_qkvg[h * copies + r, :, tile(i)] = value


def attention_kernel(qkvg, ends, o_back, qz, kr, gz, vr, dk, dv):
    qkvg, ends = ready(qkvg, ends)
    seq_size, count = qkvg.shape[0], qkvg.shape[1]
    rows = seq_size * count
    left = lax.broadcasted_iota(jnp.int32, (count, LANES), 1) < HD
    for d in range(seq_size):
        at = slice(d * count, (d + 1) * count)
        a, b = qkvg[d, :, :LANES].astype(F32), qkvg[d, :, LANES:].astype(F32)
        qz[at, :] = jnp.where(left, a, 0.0).astype(BF)
        kr[at, :] = pltpu.roll(a, HD, 1).astype(BF)
        gz[at, :] = jnp.where(left, 0.0, b).astype(BF)
        vr[at, :] = pltpu.roll(b, HD, 1).astype(BF)
    dk[...] = jnp.zeros_like(dk)
    dv[...] = jnp.zeros_like(dv)
    scale = HD**-0.5

    def queries(b, length, blocks):
        tall = blocks * count
        at = pl.ds(b * count if isinstance(b, int) else pl.multiple_of(b * count, count), tall)
        firsts = []
        for i in range(blocks):
            tail = ends[b + i].astype(F32)
            starts = jnp.broadcast_to(tail[0:1] * 64.0 + tail[1:2], (LANES, LANES))
            firsts.append(jnp.transpose(starts)[:, :1])
        first = jnp.concatenate(firsts, axis=0).astype(jnp.int32)
        column = lax.broadcasted_iota(jnp.int32, (tall, length), 1)
        row = b * count + lax.broadcasted_iota(jnp.int32, (tall, 1), 0)
        visible = (column <= row) & (column >= first)
        scores = jnp.where(visible, dot_nt(qz[at, :], kr[:length, :]) * scale, -1e30)
        weight = jnp.exp(scores - jnp.max(scores, axis=1, keepdims=True))
        probs = weight * (1.0 / jnp.sum(weight, axis=1, keepdims=True))
        low = probs.astype(BF)
        grad_probs = dot_nt(gz[at, :], vr[:length, :])
        delta = jnp.sum(probs * grad_probs, axis=1, keepdims=True)
        grad_scores = (probs * (grad_probs - delta)).astype(BF)
        dk[:length, :] += dot_tn(grad_scores, kr[at, :])
        dv[:length, :] += dot_tn(low, vr[at, :])
        dq = (dot(grad_scores, kr[:length, :]) * scale).astype(BF)
        attended = dot(low, vr[:length, :]).astype(BF)
        for i in range(blocks):
            o_back[b + i, :, :LANES] = dq[i * count : (i + 1) * count]
            o_back[b + i, :, LANES:] = attended[i * count : (i + 1) * count]

    if seq_size <= 8:
        for b in range(0, seq_size, 2):
            queries(b, (b + 2) * count, 2)
    else:
        lax.fori_loop(0, seq_size, lambda b, _: (queries(b, rows, 1), 0)[1], 0)
    for d in range(seq_size):
        at = slice(d * count, (d + 1) * count)
        o_back[d, :, :LANES] = jnp.where(left, o_back[d, :, :LANES].astype(F32), dk[at, :] * scale).astype(BF)
        o_back[d, :, LANES:] = jnp.where(left, dv[at, :], o_back[d, :, LANES:].astype(F32)).astype(BF)


def backward_kernel(
    tiled, back, after, w_proj, w_qkv, n2, cot, w_out, gate, ssm, gated, normed, s_ref, a_ref, bc,
    o_out, o_after, o_n2, o_gate, o_g, o_msg, *o_more
):
    back = ready(back)
    seq_size, count = back.shape[0], back.shape[1]
    copies = seq_size // H
    left = lax.broadcasted_iota(jnp.int32, (count, LANES), 1) < HD
    dq, dk, dv, att = [], [], [], []
    for p in range(H // 2):
        a0, b0 = (back[2 * p * copies, :, tile(i)].astype(F32) for i in range(2))
        a1, b1 = (back[(2 * p + 1) * copies, :, tile(i)].astype(F32) for i in range(2))
        dq.append(jnp.where(left, a0, pltpu.roll(a1, HD, 1)))
        dk.append(jnp.where(left, pltpu.roll(a0, HD, 1), a1))
        dv.append(jnp.where(left, b0, pltpu.roll(b1, HD, 1)))
        att.append(jnp.where(left, pltpu.roll(b0, HD, 1), b1))
    attended = jnp.concatenate(att, axis=1).astype(BF)
    after, w_proj = ready(after, w_proj)
    width = after.shape[1]
    o_out[...] = (after[...] + dot(attended, w_proj[...])).astype(BF)
    sent(o_out)
    w_qkv, n2, cot = ready(w_qkv, n2, cot)
    grad_qkv = jnp.concatenate(dq + dk + dv, axis=1).astype(BF)
    if not tiled:
        o_more[0][...] = attended
        o_more[1][...] = grad_qkv
    grad_x, grad_gain = rms_back(after[...], n2[...], dot_nt(grad_qkv, w_qkv[...]))
    o_n2[...] = jnp.sum(grad_gain, axis=0, keepdims=True)
    grad_after = cot[...].astype(F32) + grad_x
    o_after[...] = grad_after
    branch = grad_after.astype(BF)
    if not tiled:
        o_more[2][...] = branch
    sent(o_n2, o_after)
    w_out, gate, ssm = ready(w_out, gate, ssm)
    inner_width = gate.shape[1]
    tiles = inner_width // LANES
    a_ref = ready(a_ref)
    states = a_ref.shape[0] // 8
    grad_gated = dot_nt(branch, w_out[...])
    for j in range(tiles):
        v = gate[:, tile(j)].astype(F32)
        sig = jax.nn.sigmoid(v)
        grad = grad_gated[:, tile(j)]
        to_rows(o_g, j, grad * (v * sig))
        grad_gate = grad * ssm[:, tile(j)] * (sig * (1.0 + v * (1.0 - sig)))
        o_gate[:, tile(j)] = grad_gate.astype(BF)
    sent(o_gate, o_g)
    gated, normed = ready(gated, normed)
    if tiled:
        partials(seq_size, gated, branch, normed, o_gate, attended, cot, *o_more)
        sent(*o_more[:2])
    s_ref, smem = ready(s_ref, bc)

    def one(i, later):
        t = count - 1 - i
        s, g = block(s_ref, t), block(o_g, t)
        return tuple(
            jnp.exp2(s * block(a_ref, n)) * (g * smem[t, states + n] + later[n])
            for n in range(states)
        )

    leaving = lax.fori_loop(0, count, one, (jnp.zeros((8, LANES), F32),) * states, unroll=4)
    for n in range(0, states, 2):
        value = jnp.concatenate([leaving[n], leaving[n + 1]], axis=0).astype(BF)
        for d in range(seq_size):
            o_msg[d, 8 * n : 8 * n + 16, :] = value


def states_kernel(
    seq_size, start, a_ref, bc, s_ref, dx_ref, inner, conv_w, conv_b, seg, o_every, o_slope, ext
):
    start, a_ref, smem, s_ref, dx_ref = ready(start, a_ref, bc, s_ref, dx_ref)
    count = smem.shape[0]
    states = a_ref.shape[0] // 8
    o_every[: states * 8, :] = start[...]

    def again(t, state):
        s, dx = block(s_ref, t), block(dx_ref, t)
        state = tuple(
            jnp.exp2(s * block(a_ref, n)) * state[n] + dx * smem[t, n] for n in range(states)
        )
        for n in range(states):
            o_every[pl.ds(pl.multiple_of(((t + 1) * states + n) * 8, 8), 8), :] = state[n]
        return state

    lax.fori_loop(0, count, again, tuple(start[8 * n : 8 * n + 8, :] for n in range(states)), unroll=2)
    sent(o_every)
    inner, conv_w, conv_b, seg = ready(inner, conv_w, conv_b, seg)
    ext[...] = inner[...].astype(F32)
    offset = offsets_in_sequence(seg, seq_size)
    for j in range(o_slope.shape[1] // LANES):
        pre = conv_tile(ext, conv_w, conv_b, offset, j, count)
        sig = jax.nn.sigmoid(pre)
        o_slope[:, tile(j)] = sig * (1.0 + pre * (1.0 - sig))


def fold8(values, sub):
    low4, low2, low1 = sub < 4, (sub & 2) == 0, (sub & 1) == 0
    four = []
    for k in range(4):
        a, b = values[k], values[k + 4]
        four.append(jnp.where(low4, a, b) + pltpu.roll(jnp.where(low4, b, a), 4, 0))
    two = []
    for k in range(2):
        a, b = four[k], four[k + 2]
        two.append(jnp.where(low2, a + pltpu.roll(a, 6, 0), b + pltpu.roll(b, 2, 0)))
    a, b = two
    return jnp.where(low1, a + pltpu.roll(a, 7, 0), b + pltpu.roll(b, 1, 0))


def adjoint_kernel(
    seq_size, back, totals, a_ref, bc, s_ref, dx_ref, g_ref, every, gs_ref, ai_ref, o_bc, o_a, held, sums, arrived
):
    back, totals, a_ref = ready(back, totals, a_ref)
    states = a_ref.shape[0] // 8
    count = s_ref.shape[0] // 8
    zero = jnp.zeros((8, LANES), F32)
    chunks = arrived.shape[0]
    span = count // chunks
    loads = []
    for c in range(chunks):
        first, last = c * span * states * 8, ((c + 1) * span + (c == chunks - 1)) * states * 8
        loads.append(pltpu.make_async_copy(every.at[first:last], held.at[first:last], arrived.at[c]))
    for load in reversed(loads):
        load.start()

    def join(i, carry):
        d = seq_size - 1 - i
        total = total_step(totals, d, 0)
        return tuple(
            jnp.exp2(block(a_ref, n) * total) * carry[n] + state_rows(back, d, n)
            for n in range(states)
        )

    leaving = lax.fori_loop(0, seq_size - 1 - lax.axis_index("seq"), join, (zero,) * states)
    smem, s_ref, dx_ref, g_ref = ready(bc, s_ref, dx_ref, g_ref)
    sub = lax.broadcasted_iota(jnp.int32, (8, LANES), 0)

    def one(last, i, carry):
        later, grad_a = carry
        t = last - i
        s, dx, g = block(s_ref, t), block(dx_ref, t), block(g_ref, t)
        new_later, new_grad_a, with_b, with_c = [], [], [], []
        grad_step, adjoint_in = zero, zero
        for n in range(states):
            a = block(a_ref, n)
            adjoint = g * smem[t, states + n] + later[n]
            passed = jnp.exp2(s * a) * adjoint
            before = held[pl.ds(pl.multiple_of((t * states + n) * 8, 8), 8), :]
            now = held[pl.ds(pl.multiple_of(((t + 1) * states + n) * 8, 8), 8), :]
            grad_decay = passed * before
            grad_step = grad_step + grad_decay * a
            adjoint_in = adjoint_in + adjoint * smem[t, n]
            new_later.append(passed)
            new_grad_a.append(grad_a[n] + grad_decay * s)
            with_b.append(adjoint * dx)
            with_c.append(g * now)
        here = pl.ds(pl.multiple_of(t * 8, 8), 8)
        gs_ref[here, :] = grad_step
        ai_ref[here, :] = adjoint_in
        for i, part in enumerate((with_b[:8], with_b[8:], with_c[:8], with_c[8:])):
            sums[pl.ds(pl.multiple_of(t * 32 + 8 * i, 8), 8), :] = fold8(part, sub)
        return tuple(new_later), tuple(new_grad_a)

    carry = (leaving, (zero,) * states)
    for c in reversed(range(chunks)):
        loads[c].wait()
        carry = lax.fori_loop(0, span, functools.partial(one, (c + 1) * span - 1), carry, unroll=4)
    grad_a = carry[1]
    sent(gs_ref, ai_ref)
    for n in range(states):
        o_a[8 * n : 8 * n + 8, :] = grad_a[n] * (LN2 * block(a_ref, n))
    columns = o_bc.shape[1]
    lane = lax.broadcasted_iota(jnp.int32, (LANES, columns), 1)
    grad_bc = jnp.zeros(o_bc.shape, F32)
    for q in range(2 * states):
        rows = sums[pl.ds(q, count, stride=2 * states), :]
        high = rows.astype(BF)
        low = (rows - high.astype(F32)).astype(BF)
        to_column = (lane == columns - 2 * states + q).astype(BF)
        grad_bc = grad_bc + dot(high, to_column) + dot(low, to_column)
    o_bc[...] = grad_bc


def inner_kernel(
    seq_size, gs_ref, ai_ref, g_ref, mixed, step_pre, low, w_dt, grad_bc, grad_a, w_xp, inner, slope, conv_w, d_skip,
    seg, normed, grad_n2,
    *rest,
):
    o_first, o_second, o_inner, *own_small, ext, gext, grad_w = rest
    small = own_small[0] if own_small else o_second.ref
    gs_ref, ai_ref, g_ref = ready(gs_ref, ai_ref, g_ref)
    grad_bc, grad_a = ready(grad_bc, grad_a)
    count = g_ref.shape[0] // 8
    states = grad_a.shape[0] // 8
    mixed, step_pre, low, w_dt, w_xp, inner = ready(mixed, step_pre, low, w_dt, w_xp, inner)
    slope, conv_w, d_skip, seg, normed, grad_n2 = ready(slope, conv_w, d_skip, seg, normed, grad_n2)
    inner_width = mixed.shape[1]
    tiles = inner_width // LANES
    rank = w_dt.shape[0]
    taps = conv_w.shape[0]
    small[...] = jnp.zeros_like(small)
    small[104 * 8 : (104 + states) * 8, :] = grad_a[...]
    offset = offsets_in_sequence(seg, seq_size)
    halves = []
    for j in range(tiles):
        mix = mixed[:, tile(j)].astype(F32)
        pre = step_pre[:, tile(j)]
        grad_step = LN2 * from_rows(gs_ref, j, count) + mix * from_rows(ai_ref, j, count)
        grad_pre = grad_step * jax.nn.sigmoid(pre)
        small[101 * 8 + j : 101 * 8 + j + 1, :] = jnp.sum(grad_pre, axis=0, keepdims=True)
        grad_ssm = from_rows(g_ref, j, count)
        small[102 * 8 + j : 102 * 8 + j + 1, :] = jnp.sum(grad_ssm * mix, axis=0, keepdims=True)
        halves.append(grad_pre.astype(BF))
    half = jnp.concatenate(halves, axis=1)
    grad_w_dt = dot_tn(low[...], half)
    padded_dt = jnp.concatenate([w_dt[...], jnp.zeros((2 * states, inner_width), BF)], axis=0)
    grad_selector = (dot_nt(half, padded_dt) + grad_bc[...]).astype(BF)
    grad_w_xp = dot_tn(grad_selector, mixed[...])
    from_selector = dot(grad_selector, w_xp[...])
    ext[...] = inner[...].astype(F32)
    gext[...] = jnp.zeros_like(gext)
    for j in range(tiles):
        to_rows(small.at[pl.ds(0, 64 * 8)], j, grad_w_xp[:, tile(j)])
        to_rows(small.at[pl.ds(64 * 8, 32 * 8)], j, grad_w_dt[:, tile(j)])
        grad_mixed = (
            softplus(step_pre[:, tile(j)]) * from_rows(ai_ref, j, count)
            + from_rows(g_ref, j, count) * d_skip[:, tile(j)]
            + from_selector[:, tile(j)]
        )
        grad_pre = grad_mixed * slope[:, tile(j)]
        small[100 * 8 + j : 100 * 8 + j + 1, :] = jnp.sum(grad_pre, axis=0, keepdims=True)
        for k in range(taps):
            shifted = pl.ds(HALO - taps + 1 + k, count)
            usable = jnp.where(offset >= taps - 1 - k, grad_pre, 0.0)
            row = (96 + k) * 8 + j
            small[row : row + 1, :] = jnp.sum(usable * ext[shifted, tile(j)], axis=0, keepdims=True)
            gext[shifted, tile(j)] += conv_w[k : k + 1, tile(j)] * usable
    o_inner[...] = gext[...].astype(BF)
    sent(o_inner)
    width = grad_n2.shape[1]
    for j in range(width // LANES):
        small[103 * 8 + 4 + j : 103 * 8 + 5 + j, :] = grad_n2[:, tile(j)]
    if not own_small:
        o_first[...] = dot_tn(normed[...], o_inner[...])
        return
    grad_w[...] = dot_tn(normed[...], o_inner[...])
    for to, x, s, at in receivers((o_first, o_second), seq_size):
        to[x * seq_size + s, :LANES, :] = grad_w[pl.ds(pl.multiple_of(at * LANES, LANES), LANES), tile(s)].astype(BF)
        rows = small.shape[0] // (width // LANES * seq_size)
        here = pl.ds(pl.multiple_of((at * seq_size + s) * rows, rows), rows)
        to[x * seq_size + s, LANES:, :] = small[here, :].astype(BF)


def receivers(results, seq_size, mine=0):
    core = lax.rem(lax.axis_index("dp"), 2)
    for to, side in zip(results, (core, 1 - core)):
        for x in range(to.shape[0] // seq_size):
            for s in range(seq_size):
                yield to, x, s, 2 * lax.bitwise_xor(x, mine) + side


def partials(seq_size, gated, branch, normed, grad_gate, attended, cot, keep, send, out, gate, proj):
    out[...] = dot_tn(gated[...], branch)
    gate[...] = dot_tn(normed[...], grad_gate[...])
    proj[...] = dot_tn(attended, cot[...])
    across = out.shape[1] // LANES
    down = seq_size // across
    mine = lax.axis_index("dp") // 2
    for to, x, s, at in receivers((keep, send), seq_size, mine):
        rows = pl.ds(pl.multiple_of((at * down + s // across) * LANES, LANES), LANES)
        to[x * seq_size + s, :LANES, :] = out[rows, tile(s % across)].astype(BF)
        rows = pl.ds(pl.multiple_of(at * LANES, LANES), LANES)
        to[x * seq_size + s, LANES : 2 * LANES, :] = gate[rows, tile(s)].astype(BF)
        rows = pl.ds(pl.multiple_of((at * down + s // across) * HD, HD), HD)
        to[x * seq_size + s, 2 * LANES :, :] = proj[rows, tile(s % across)].astype(BF)


def tokens_kernel(grad_inner, w_in, grad_gate, tok, halo, n1, grad_after, o_tok, o_halo, o_n1):
    grad_inner, w_in, grad_gate = ready(grad_inner, w_in, grad_gate)
    inner_width = grad_inner.shape[1]
    grad_normed = dot_nt(grad_inner[...], w_in[:, :inner_width])
    own = dot_nt(grad_gate[...], w_in[:, inner_width:])
    grad_normed = jnp.concatenate([grad_normed[:HALO], grad_normed[HALO:] + own], axis=0)
    tok, halo, n1, grad_after = ready(tok, halo, n1, grad_after)
    x = jnp.concatenate([halo[...], tok[...]], axis=0).astype(F32)
    grad_x, grad_gain = rms_back(x, n1[...], grad_normed)
    o_tok[...] = grad_after[...] + grad_x[HALO:]
    o_halo[...] = grad_x[HALO - 8 : HALO]
    grad_gain = jnp.sum(grad_gain, axis=0, keepdims=True)
    tiles = grad_gain.shape[1] // LANES
    rows = [grad_gain[:, tile(j)] for j in range(tiles)] + [jnp.zeros((16 - tiles, LANES), F32)]
    o_n1[...] = jnp.concatenate(rows, axis=0).astype(BF)


def head_products_kernel(normed, back, *rest):
    *outs, pieces = rest
    normed, back = ready(normed, back)
    both = back[...].reshape(back.shape[0] * back.shape[1], 2 * LANES)
    grad = dot_tn(both, normed[...])
    left = lax.broadcasted_iota(jnp.int32, (HD, LANES), 1) < HD
    for g in range(len(outs)):
        pieces[g, : 2 * HD, :] = jnp.transpose(grad[:LANES, tile(g)])
        value = jnp.transpose(grad[LANES:, tile(g)])
        pieces[g, 2 * HD :, :] = jnp.where(left, value[:HD], pltpu.roll(value[HD:], HD, 1))
    for distance, to in enumerate(outs):
        to[...] = pieces[lax.bitwise_xor(lax.axis_index("dp"), distance)].astype(BF)


def early_sum_kernel(parts, *heads):
    *heads, o_sum = heads
    heads, parts = ready(*heads), ready(parts)
    head = heads[0][...].astype(F32)
    for part in heads[1:]:
        head = head + part[...].astype(F32)
    total = parts[0].astype(F32)
    for d in range(1, parts.shape[0]):
        total = total + parts[d].astype(F32)
    rows = total.shape[0]
    o_sum[:rows, :] = total.astype(BF)
    o_sum[rows:, :] = head.astype(BF)


def sum_and_spread_kernel(parts, own, o_all):
    parts, own = ready(parts, own)
    total = parts[0].astype(F32)
    for d in range(1, parts.shape[0]):
        total = total + parts[d].astype(F32)
    total = total.astype(BF)
    rows = total.shape[0]
    for d in range(o_all.shape[0]):
        o_all[d, :rows, :] = total
        o_all[d, rows:, :] = own[...]


def early_assembly_kernel(groups, early, w_in, o_out, o_proj, o_qkv, o_in, pieces, out, proj, qkv, gate, loads, stores):
    seq_size = early.shape[0] // groups
    inner_width, width = gate.shape[1], proj.shape[1]
    across = width // LANES
    left = lax.broadcasted_iota(jnp.int32, (LANES, LANES), 1) < HD
    at = 2 * LANES + HD

    def pairs(a, b):
        a, b = a.astype(F32), b.astype(F32)
        mask = left[: a.shape[0]]
        return jnp.where(mask, a, pltpu.roll(b, HD, 1)), jnp.where(mask, pltpu.roll(a, HD, 1), b)

    own = [slice(g * seq_size, (g + 1) * seq_size) for g in range(groups)]
    arrivals = [pltpu.make_async_copy(early.at[own[g]], pieces.at[own[g]], loads.at[g]) for g in range(groups)]
    for copy in arrivals:
        copy.start()
    copies = []
    for g in range(groups):
        arrivals[g].wait()
        down = seq_size // across
        for s in range(seq_size):
            piece = pieces[g * seq_size + s]
            row = g * down + s // across
            out[tile(row), tile(s % across)] = piece[:LANES].astype(F32)
            gate[tile(g), tile(s)] = piece[LANES : 2 * LANES].astype(F32)
            proj[row * HD : (row + 1) * HD, tile(s % across)] = piece[2 * LANES : at].astype(F32)
        for p in range(seq_size // 2):
            a, b = pieces[g * seq_size + 2 * p], pieces[g * seq_size + 2 * p + 1]
            first, second, third = (slice(i * width + p * LANES, i * width + (p + 1) * LANES) for i in range(3))
            qkv[tile(g), first], qkv[tile(g), second] = pairs(a[at : at + LANES], b[at : at + LANES])
            low, high = pairs(a[at + LANES :], b[at + LANES :])
            qkv[g * LANES : g * LANES + HD, third] = low
            qkv[g * LANES + HD : (g + 1) * LANES, third] = high
        for i, (source, target, rows) in enumerate(
            ((out, o_out, down * LANES), (proj, o_proj, down * HD), (qkv, o_qkv, LANES), (gate, o_in, LANES))
        ):
            here = slice(g * rows, (g + 1) * rows)
            target = target.at[here, inner_width:] if i == 3 else target.at[here]
            copies.append(pltpu.make_async_copy(source.at[here], target, stores.at[4 * g + i]))
            copies[-1].start()
    for copy in copies:
        copy.wait()


def late_assembly_kernel(
    groups, mine, other, o_in, o_n1, o_conv_w, o_conv_b, o_xp, o_dt, o_dtb, o_a, o_skip, o_n2, inner, small, sems
):
    mine, other = ready(mine, other)
    seq_size = mine.shape[0] * 2 // groups
    width, inner_width = inner.shape
    rows = mine.shape[1] - LANES - 16
    copies = []
    for ref, x, s, g in receivers((mine, other), seq_size):
        at = pl.ds(pl.multiple_of(g * LANES, LANES), LANES)
        inner[at, tile(s)] = ref[x * seq_size + s, :LANES, :].astype(F32)
        here = pl.ds(pl.multiple_of((g * seq_size + s) * rows, rows), rows)
        small[here, :] = ref[x * seq_size + s, LANES : LANES + rows, :].astype(F32)
        if s == seq_size - 1:
            copies.append(pltpu.make_async_copy(inner.at[at], o_in.at[at, :inner_width], sems.at[len(copies)]))
            copies[-1].start()
    for j in range(inner_width // LANES):
        value = from_rows(small, j, SMALL)
        for ref, first, last in (
            (o_xp, 0, 64), (o_dt, 64, 96), (o_conv_w, 96, 100), (o_conv_b, 100, 101), (o_dtb, 101, 102),
            (o_skip, 102, 103), (o_a, 104, 120),
        ):
            ref[:, tile(j)] = value[first:last]
        if j >= width // LANES:
            o_n2[:, tile(j - width // LANES)] = value[103:104]
    sent(o_conv_w, o_conv_b, o_xp, o_dt, o_dtb, o_a, o_skip, o_n2)
    gain = jnp.zeros((16, LANES), F32)
    for source in (mine, other):
        for d in range(source.shape[0]):
            gain = gain + source[d, LANES + rows :, :].astype(F32)
    for j in range(width // LANES):
        o_n1[:, tile(j)] = gain[j : j + 1]
    for copy in copies:
        copy.wait()


class Held:
    def __init__(self, buffer, copy):
        self.ref, self.copy, self.shape = buffer, copy, buffer.shape
        self.done = False

    def __getitem__(self, at):
        return self.ref[at]

    def __setitem__(self, at, value):
        self.ref[at] = value


def ready(*held):
    for one in held:
        if not one.done:
            one.copy.wait()
            one.done = True
    refs = tuple(one.ref for one in held)
    return refs[0] if len(refs) == 1 else refs


def sent(*held):
    for one in held:
        if not one.done:
            one.copy.start()
            one.done = True


IN_HBM = pl.BlockSpec(memory_space=pltpu.HBM)


def call(
    kernel, outs, scratch, *args, name=None, us=1, raw=(), raw_out=(), scalars=(), views=None, aliases=None, after=(),
    near=(), vmem=60,
):
    views = views or {}
    count, first_out = len(args), len(args) + len(after)
    first_scratch = first_out + len(outs)
    buffers = []
    for i, arg in enumerate(args):
        shape = jax.eval_shape(lambda v, i=i: v[views[i]], arg).shape if i in views else arg.shape
        kind = pltpu.SMEM if i in scalars else pltpu.VMEM
        buffers.append(None if i in raw else kind(shape, arg.dtype))
    for i, (shape, dtype) in enumerate(outs):
        buffers.append(None if i in raw_out else pltpu.VMEM(shape, dtype))
    used = [b for b in buffers if b is not None]

    def run(*refs):
        given = list(refs[:count]) + list(refs[first_out:first_scratch])
        own = list(refs[first_scratch : first_scratch + len(used)])
        sems = refs[first_scratch + len(used)]
        passed = []
        for i, (ref, buffer) in enumerate(zip(given, buffers)):
            if buffer is None:
                passed.append(ref)
                continue
            buffer = own.pop(0)
            if i < count:
                source = ref.at[views[i]] if i in views else ref
                copy = pltpu.make_async_copy(source, buffer, sems.at[i])
                copy.start()
            else:
                copy = pltpu.make_async_copy(buffer, ref, sems.at[i])
            passed.append(Held(buffer, copy))
        kernel(*passed, *refs[first_scratch + len(used) + 1 :])
        ready(*[p for p in passed[:count] if isinstance(p, Held)])
        results = [p for p in passed[count:] if isinstance(p, Held)]
        sent(*results)
        for result in results:
            result.copy.wait()

    return pl.pallas_call(
        run,
        out_shape=[jax.ShapeDtypeStruct(s, d) for s, d in outs],
        in_specs=[pl.BlockSpec(memory_space=pl.ANY) if i in near else IN_HBM for i in range(first_out)],
        out_specs=[IN_HBM] * len(outs),
        scratch_shapes=used + [pltpu.SemaphoreType.DMA((len(buffers),))] + scratch,
        compiler_params=pltpu.CompilerParams(vmem_limit_bytes=vmem * 1024 * 1024),
        cost_estimate=pl.CostEstimate(flops=us * 10**9 + 1000, bytes_accessed=1000, transcendentals=0),
        input_output_aliases=aliases or {},
        name=name,
    )(*args, *after)


def exchange(value, axes):
    return lax.all_to_all(value, axes, 0, 0, tiled=True)


def own_core(value, groups, seq_size):
    peers = [
        [g * seq_size + s for g in range(core, groups, 2) for s in range(seq_size)] for core in range(2)
    ]
    return lax.all_to_all(value, ("dp", "seq"), 0, 0, tiled=True, axis_index_groups=peers)


def other_core(value, groups):
    return lax.ppermute(value, "dp", [(g, g ^ 1) for g in range(groups)])


def body(
    tokens, seg_start, norm_one, w_in, conv_w, conv_b, w_xproj, w_dt, dt_bias, a_log, d_skip,
    w_out, norm_two, w_qkv, w_proj, cotangent,
):
    count, width = tokens.shape
    inner_width = w_in.shape[1] // 2
    states = a_log.shape[1]
    rank = w_dt.shape[0]
    taps = conv_w.shape[0]
    groups, seq_size = lax.axis_size("dp"), lax.axis_size("seq")
    rows = count * seq_size
    ext_rows = HALO + count
    tiled = inner_width == seq_size * LANES and width == groups * LANES and seq_size == H
    peers = groups // 2 * seq_size
    line = lambda v: v.reshape(1, -1)
    seg = line(seg_start)
    n1, n2, cb, dtb, skip = (line(v) for v in (norm_one, norm_two, conv_b, dt_bias, d_skip))
    vmem, smem = pltpu.VMEM, pltpu.SMEM((count, 2 * states), F32)
    sem = pltpu.SemaphoreType.DMA
    blocks = ((count * 8, LANES), F32)
    ends_at = states * 8
    halo = lax.ppermute(tokens[count - HALO :], "seq", [(i, i + 1) for i in range(seq_size - 1)])
    msg, normed, inner, gate, mixed, bc, low, step_pre, s, dx, a = call(
        functools.partial(forward_kernel, seq_size),
        [
            ((seq_size, states * 8 + 32, LANES), BF), ((ext_rows, width), BF),
            ((ext_rows, inner_width), BF), ((count, inner_width), BF), ((count, inner_width), BF), ((count, 2 * states), F32),
            ((count, rank), BF), ((count, inner_width), F32), blocks, blocks, ((states * 8, LANES), F32),
        ],
        [vmem((ext_rows, inner_width), F32), smem, sem],
        tokens, halo, n1, w_in, conv_w, cb, w_xproj.T, w_dt, dtb, a_log.T, seg,
        name="forward", us=0, near=(1,),
    )
    msg = exchange(msg, "seq")
    qkvg, start, ssm, after, gated, normed_two = call(
        middle_kernel,
        [
            ((seq_size, count, 2 * LANES), BF), ((states * 8, LANES), F32), ((count, inner_width), F32),
            ((count, width), F32), ((count, inner_width), BF), ((count, width), BF),
        ],
        [vmem(*blocks)],
        msg, a, bc, s, dx, mixed, gate, skip, tokens, w_out, n2, w_qkv, cotangent, w_proj,
        name="middle", us=0, scalars=(2,), views={0: np.s_[:, : ends_at + 16, :]}, near=(0,),
    )
    qkvg = exchange(qkvg, "seq")
    every, slope = call(
        functools.partial(states_kernel, seq_size),
        [(((count + 1) * states * 8, LANES), F32), ((count, inner_width), F32)],
        [vmem((ext_rows, inner_width), F32)],
        start, a, bc, s, dx, inner, conv_w, cb, seg, name="states", us=0, scalars=(2,),
    )
    (back,) = call(
        attention_kernel,
        [((seq_size, count, 2 * LANES), BF)],
        [vmem((rows, LANES), BF)] * 4 + [vmem((rows, LANES), F32)] * 2,
        qkvg, msg, name="attention", us=0, views={1: np.s_[:, ends_at + 16 :, :]},  near=(0,),
    )
    back_own = exchange(back, "seq")
    pieces = [((peers, 2 * LANES + HD, LANES), BF)] * 2
    rest = [((count, width), BF), ((count, 3 * width), BF), ((count, width), BF)]
    out, grad_after, grad_n2, grad_gate, g, adj, *more = call(
        functools.partial(backward_kernel, tiled),
        [
            ((count, width), BF), ((count, width), F32), ((1, width), F32), ((count, inner_width), BF), blocks,
            ((seq_size, states * 8, LANES), BF),
        ] + (pieces if tiled else rest),
        [vmem((inner_width, width), F32), vmem((width, inner_width), F32), vmem((width, width), F32)] if tiled else [],
        back_own, after, w_proj, w_qkv, n2, cotangent, w_out, gate, ssm, gated, normed, s, a, bc,
        name="backward", us=0, scalars=(13,), views={10: np.s_[HALO:, :]}, near=(0,),
    )
    adj = exchange(adj, "seq")
    between = ()
    if tiled:
        normed_two_all = lax.all_gather(normed_two, "seq", axis=0, tiled=True)
        keep, send = more
        add = lambda *parts: sum(part.astype(F32) for part in parts).astype(BF)
        received = other_core(send, groups)
        across = add(keep[seq_size:], received[seq_size:])
        across = lax.ppermute(across, "dp", [(g, g ^ 2) for g in range(groups)])
        across, slope = lax.optimization_barrier((across, slope))
        part = add(keep[:seq_size], received[:seq_size], across)
        between = (part,)
        part = exchange(part, "seq")
    gs, ai, grad_bc, grad_a = call(
        functools.partial(adjoint_kernel, seq_size),
        [blocks, blocks, ((count, rank + 2 * states), F32), ((states * 8, LANES), F32)],
        [vmem(((count + 1) * states * 8, LANES), F32), vmem((count * 2 * states, LANES), F32), sem((8,))],
        adj, msg, a, bc, s, dx, g, every, name="adjoint", us=0, raw=(7,), scalars=(3,), near=(0,),
        views={1: np.s_[:, ends_at : ends_at + 16, :]}, after=between,
    )
    small_rows = SMALL * 8 // (groups * seq_size)
    *sums, small, grad_inner = call(
        functools.partial(inner_kernel, seq_size),
        ([((peers, LANES + small_rows, LANES), BF)] * 2 if tiled else [((width, inner_width), F32), ((SMALL * 8, LANES), F32)])
        + [((ext_rows, inner_width), BF)],
        ([vmem((SMALL * 8, LANES), F32)] if tiled else [])
        + [vmem((ext_rows, inner_width), F32), vmem((ext_rows, inner_width), F32), vmem((width, inner_width), F32)],
        gs, ai, g, mixed, step_pre, low, w_dt, grad_bc, grad_a, w_xproj.T, inner, slope, conv_w, skip, seg, normed, grad_n2,
        name="inner", us=0,
    )
    grad_tokens, grad_halo, grad_n1 = call(
        tokens_kernel, [((count, width), F32), ((8, width), F32), ((16, LANES), BF)], [],
        grad_inner, w_in, grad_gate, tokens, halo, n1, grad_after, name="tokens", us=0,
    )
    returned = lax.ppermute(grad_halo, "seq", [(i + 1, i) for i in range(seq_size - 1)])
    grad_tokens = grad_tokens.at[count - 8 :].add(returned)
    flat = lambda v: v.reshape(-1)
    if tiled:
        head, *heads = call(
            head_products_kernel, [((3 * HD, LANES), BF)] * groups, [vmem((groups, 3 * HD, LANES), F32)],
            normed_two_all, back, name="head_products", us=0, after=(grad_inner,),
        )
        heads = [
            lax.ppermute(piece, "dp", [(g, g ^ distance) for g in range(groups)])
            for distance, piece in enumerate(heads, 1)
        ]
        (early,) = call(
            early_sum_kernel, [((part.shape[1] + head.shape[0], LANES), BF)], [], part, head, *heads,
            name="early_sum", us=0, vmem=40, near=(0, 2, 3, 4),
        )
        late = add(sums[0], other_core(small, groups))
        late, early = lax.optimization_barrier((late, early))
        late = own_core(late, groups, seq_size)
        early = lax.all_gather(early, ("dp", "seq"))
        (late,) = call(
            sum_and_spread_kernel, [((peers, late.shape[1] + 16, LANES), BF)], [], late, grad_n1, name="late_sum", us=0, vmem=40,
            near=(0,),
        )
        mine = own_core(late, groups, seq_size)
        mine, grad_tokens = lax.optimization_barrier((mine, grad_tokens))
        row = lambda n: ((n, inner_width), F32)
        half, g_n1, g_conv_w, g_conv_b, g_xp, g_dt, g_dtb, g_a, g_skip, g_n2 = call(
            functools.partial(late_assembly_kernel, groups),
            [
                ((width, 2 * inner_width), F32), ((1, width), F32), row(taps), row(1), row(2 * states + rank), row(rank),
                row(1), row(states), row(1), ((1, width), F32),
            ],
            [vmem((width, inner_width), F32), vmem((SMALL * 8, LANES), F32), sem((4,))],
            mine, other_core(mine, groups), name="late_assembly", us=0, vmem=40, raw_out=(0,), near=(0, 1),
        )
        whole = [((inner_width, width), F32), ((width, width), F32), ((width, 3 * width), F32)]
        grad_w_out, grad_w_proj, grad_w_qkv, grad_w_in = call(
            functools.partial(early_assembly_kernel, groups),
            whole + [((width, 2 * inner_width), F32)],
            [vmem(early.shape, BF)] + [vmem(*v) for v in whole] + [vmem((width, inner_width), F32), sem((4,)), sem((16,))],
            early, half, name="early_assembly", us=0, raw=(0, 1), raw_out=(0, 1, 2, 3), aliases={1: 3},
        )
        g_xp, g_a, g_n1, g_n2 = g_xp.T, g_a.T, flat(g_n1), flat(g_n2)
    else:
        attended, grad_qkv, branch = more
        small = small.reshape(SMALL, inner_width)
        g_n1 = flat(grad_n1[: width // LANES].astype(F32))
        both = jnp.concatenate([sums[0], dot_tn(normed[HALO:], grad_gate)], axis=1)
        grad_w_in, grad_w_out, grad_w_qkv, grad_w_proj, small, g_n1 = lax.psum(
            (both, dot_tn(gated, branch), dot_tn(normed_two, grad_qkv), dot_tn(attended, cotangent), small, g_n1), ("dp", "seq")
        )
        g_xp, g_dt, g_conv_w, g_conv_b, g_dtb = small[:64].T, small[64:96], small[96:100], small[100], small[101]
        g_skip, g_n2, g_a = small[102], small[103, width:], small[104:120].T
    return (out, grad_tokens, g_n1, grad_w_in, g_conv_w, flat(g_conv_b), g_xp, g_dt, flat(g_dtb), g_a, flat(g_skip),
            grad_w_out, g_n2, grad_w_qkv, grad_w_proj)


def solution(mesh):
    split, copied = P(("dp", "seq"), None), P()
    return jax.shard_map(
        body,
        mesh=mesh,
        in_specs=(split, P(("dp", "seq"))) + (copied,) * 13 + (split,),
        out_specs=(split, split) + (copied,) * 13,
        check_vma=False,
    )
```

```python
import functools

import jax
import jax.numpy as jnp
import numpy as np
from jax import lax
from jax.experimental import pallas as pl
from jax.experimental.pallas import tpu as pltpu
from jax.sharding import PartitionSpec as P

H = 8
HD = 64
LANES = 128
HALO = 16
SMALL = 128
RESET = 1e30
EPSILON = 1e-05
LOG2E = 1.4426950408889634
LN2 = 0.6931471805599453
BF = jnp.bfloat16
F32 = jnp.float32


def dot(a, b):
    return jnp.dot(a, b, preferred_element_type=F32)


def dot_nt(a, b):
    return lax.dot_general(a, b, (((1,), (1,)), ((), ())), preferred_element_type=F32)


def dot_tn(a, b):
    return lax.dot_general(a, b, (((0,), (0,)), ((), ())), preferred_element_type=F32)


def tile(j):
    return slice(j * LANES, (j + 1) * LANES)


def softplus(x):
    u = jnp.exp(-jnp.abs(x))
    series = u * (1.0 - u * (0.5 - u * (1.0 / 3.0 - u * 0.25)))
    return jnp.maximum(x, 0.0) + jnp.where(u < 0.015, series, jnp.log(1.0 + u))


def rms_parts(x):
    return lax.rsqrt(jnp.mean(x * x, axis=-1, keepdims=True) + EPSILON)


def rms_back(x, gain, grad):
    r = rms_parts(x)
    scaled = grad * gain
    inner = jnp.mean(x * scaled, axis=-1, keepdims=True)
    return r * scaled - x * (r * r * r * inner), grad * x * r


def to_rows(ref, j, value):
    ref[pl.ds(j, value.shape[0], stride=8), :] = value


def from_rows(ref, j, count):
    return ref[pl.ds(j, count, stride=8), :]


def block(ref, t):
    return ref[pl.ds(pl.multiple_of(t * 8, 8), 8), :]


def offsets_in_sequence(seg_ref, seq_size):
    count = seg_ref.shape[1]
    base = (lax.axis_index("dp") * seq_size + lax.axis_index("seq")) * count
    places = base + lax.broadcasted_iota(jnp.int32, (1, count), 1)
    row = (places - seg_ref[...]).astype(F32)
    return jnp.transpose(jnp.broadcast_to(row, (LANES, count)))


def conv_tile(ext_ref, w_ref, b_ref, offset, j, count):
    taps = w_ref.shape[0]
    pre = jnp.broadcast_to(b_ref[:, tile(j)], (count, LANES))
    for k in range(taps):
        rows = ext_ref[pl.ds(HALO - taps + 1 + k, count), tile(j)]
        pre = pre + jnp.where(offset >= taps - 1 - k, w_ref[k : k + 1, tile(j)] * rows, 0.0)
    return pre


def forward_kernel(
    seq_size, tok, halo, n1, w_in, conv_w, conv_b, w_xp, w_dt, dtb, a_log, seg,
    o_msg, o_normed, o_inner, o_gate, o_mixed, o_bc, o_low, o_pre, o_s, o_dx, o_a,
    ext, smem, sem,
):
    tok, halo, n1, seg = ready(tok, halo, n1, seg)
    count = tok.shape[0]
    states = a_log.shape[0]
    inner_width = conv_w.shape[1]
    tiles = inner_width // LANES
    rank = w_dt.shape[0]
    x = jnp.concatenate([halo[...], tok[...]], axis=0).astype(F32)
    normed = (x * rms_parts(x) * n1[...]).astype(BF)
    o_normed[...] = normed
    sent(o_normed)
    w_in = ready(w_in)
    inner = dot(normed, w_in[:, :inner_width]).astype(BF)
    o_inner[...] = inner
    sent(o_inner)
    ext[...] = inner.astype(F32)
    conv_w, conv_b, w_xp, w_dt, dtb, a_log = ready(conv_w, conv_b, w_xp, w_dt, dtb, a_log)
    offset = offsets_in_sequence(seg, seq_size)
    for j in range(tiles):
        pre = conv_tile(ext, conv_w, conv_b, offset, j, count)
        o_mixed[:, tile(j)] = (pre * jax.nn.sigmoid(pre)).astype(BF)
    sent(o_mixed)
    selector = dot_nt(o_mixed[...], w_xp[...])
    low = selector[:, :rank].astype(BF)
    o_low[...] = low
    o_bc[...] = selector[:, rank:]
    sent(o_low, o_bc)
    copy = pltpu.make_async_copy(o_bc.ref, smem, sem)
    copy.start()
    o_pre[...] = dot(low, w_dt[...]) + dtb[...]
    sent(o_pre)
    o_gate[...] = dot(normed[HALO:], w_in[:, inner_width:]).astype(BF)
    sent(o_gate)
    for j in range(tiles):
        step = softplus(o_pre[:, tile(j)])
        to_rows(o_s, j, jnp.where(offset == 0.0, RESET, step))
        to_rows(o_dx, j, step * o_mixed[:, tile(j)].astype(F32))
        to_rows(o_a, j, -LOG2E * jnp.exp(a_log[:, tile(j)]))
    sent(o_s, o_dx, o_a)
    copy.wait()

    def one(t, carry):
        total, state = carry
        s, dx = block(o_s, t), block(o_dx, t)
        return total + s, tuple(
            jnp.exp2(s * block(o_a, n)) * state[n] + dx * smem[t, n] for n in range(states)
        )

    zero = jnp.zeros((8, LANES), F32)
    total, state = lax.fori_loop(0, count, one, (zero, (zero,) * states), unroll=4)
    high = total.astype(BF).astype(F32)
    seg_local = (seg[...] - lax.axis_index("dp") * (seq_size * count)).astype(F32)
    seg_high = jnp.floor(seg_local * (1.0 / 64.0))
    last = jnp.concatenate([seg_high, seg_local - 64.0 * seg_high, jnp.zeros((14, LANES), F32)], axis=0)
    blocks = [jnp.concatenate([state[n], state[n + 1]], axis=0) for n in range(0, states, 2)]
    blocks += [jnp.concatenate([high, total - high], axis=0), last]
    for i, value in enumerate(blocks):
        value = value.astype(BF)
        for d in range(seq_size):
            o_msg[d, 16 * i : 16 * i + 16, :] = value


def total_step(msg, d, states):
    rows = msg[d, states * 8 : states * 8 + 16, :].astype(F32)
    return rows[:8] + rows[8:]


def state_rows(msg, d, n):
    rows = msg[d, 16 * (n // 2) : 16 * (n // 2) + 16, :].astype(F32)
    return rows[:8] if n % 2 == 0 else rows[8:]


def middle_kernel(
    msg, a_ref, bc, s_ref, dx_ref, mixed, gate, d_skip, tok, w_out, n2, w_qkv, cot, w_proj,
    o_qkvg, o_start, o_ssm, o_after, o_gated, o_normed,
    y_ref,
):
    msg, a_ref = ready(msg, a_ref)
    states = a_ref.shape[0] // 8
    zero = jnp.zeros((8, LANES), F32)

    def join(d, carry):
        total = total_step(msg, d, states)
        return tuple(
            jnp.exp2(block(a_ref, n) * total) * carry[n] + state_rows(msg, d, n)
            for n in range(states)
        )

    start = lax.fori_loop(0, lax.axis_index("seq"), join, (zero,) * states)
    for n in range(states):
        o_start[8 * n : 8 * n + 8, :] = start[n]
    sent(o_start)
    s_ref, dx_ref, smem = ready(s_ref, dx_ref, bc)
    count = smem.shape[0]

    def one(t, state):
        s, dx = block(s_ref, t), block(dx_ref, t)
        state = tuple(
            jnp.exp2(s * block(a_ref, n)) * state[n] + dx * smem[t, n] for n in range(states)
        )
        parts = [state[n] * smem[t, states + n] for n in range(states)]
        while len(parts) > 1:
            parts = [a + b for a, b in zip(parts[::2], parts[1::2])]
        y_ref[pl.ds(pl.multiple_of(t * 8, 8), 8), :] = parts[0]
        return state

    lax.fori_loop(0, count, one, start, unroll=4)
    mixed, gate, d_skip, tok, w_out, n2 = ready(mixed, gate, d_skip, tok, w_out, n2)
    inner_width, width = mixed.shape[1], tok.shape[1]
    tiles = inner_width // LANES
    for j in range(tiles):
        ssm = from_rows(y_ref, j, count) + d_skip[:, tile(j)] * mixed[:, tile(j)].astype(F32)
        o_ssm[:, tile(j)] = ssm
        v = gate[:, tile(j)].astype(F32)
        o_gated[:, tile(j)] = (ssm * (v * jax.nn.sigmoid(v))).astype(BF)
    sent(o_ssm, o_gated)
    after = tok[...].astype(F32) + dot(o_gated[...], w_out[...])
    o_after[...] = after
    sent(o_after)
    normed = (after * rms_parts(after) * n2[...]).astype(BF)
    o_normed[...] = normed
    sent(o_normed)
    w_qkv, cot, w_proj = ready(w_qkv, cot, w_proj)
    qkv = dot(normed, w_qkv[...])
    grad_att = dot_nt(cot[...], w_proj[...])
    copies = o_qkvg.shape[0] // H
    left = lax.broadcasted_iota(jnp.int32, (count, LANES), 1) < HD
    for p in range(H // 2):
        q, k, v = (qkv[:, i * width + p * LANES : i * width + (p + 1) * LANES] for i in range(3))
        g = grad_att[:, tile(p)]
        first = (jnp.where(left, q, pltpu.roll(k, HD, 1)), jnp.where(left, v, pltpu.roll(g, HD, 1)))
        second = (jnp.where(left, pltpu.roll(q, HD, 1), k), jnp.where(left, pltpu.roll(v, HD, 1), g))
        for h, pair in ((2 * p, first), (2 * p + 1, second)):
            for i, value in enumerate(pair):
                value = value.astype(BF)
                for r in range(copies):
                    o_qkvg[h * copies + r, :, tile(i)] = value


def attention_kernel(qkvg, ends, o_back, qz, kr, gz, vr, dk, dv):
    qkvg, ends = ready(qkvg, ends)
    seq_size, count = qkvg.shape[0], qkvg.shape[1]
    rows = seq_size * count
    left = lax.broadcasted_iota(jnp.int32, (count, LANES), 1) < HD
    for d in range(seq_size):
        at = slice(d * count, (d + 1) * count)
        a, b = qkvg[d, :, :LANES].astype(F32), qkvg[d, :, LANES:].astype(F32)
        qz[at, :] = jnp.where(left, a, 0.0).astype(BF)
        kr[at, :] = pltpu.roll(a, HD, 1).astype(BF)
        gz[at, :] = jnp.where(left, 0.0, b).astype(BF)
        vr[at, :] = pltpu.roll(b, HD, 1).astype(BF)
    dk[...] = jnp.zeros_like(dk)
    dv[...] = jnp.zeros_like(dv)
    scale = HD**-0.5

    def queries(b, length, blocks):
        tall = blocks * count
        at = pl.ds(b * count if isinstance(b, int) else pl.multiple_of(b * count, count), tall)
        firsts = []
        for i in range(blocks):
            tail = ends[b + i].astype(F32)
            starts = jnp.broadcast_to(tail[0:1] * 64.0 + tail[1:2], (LANES, LANES))
            firsts.append(jnp.transpose(starts)[:, :1])
        first = jnp.concatenate(firsts, axis=0).astype(jnp.int32)
        column = lax.broadcasted_iota(jnp.int32, (tall, length), 1)
        row = b * count + lax.broadcasted_iota(jnp.int32, (tall, 1), 0)
        visible = (column <= row) & (column >= first)
        scores = jnp.where(visible, dot_nt(qz[at, :], kr[:length, :]) * scale, -1e30)
        weight = jnp.exp(scores - jnp.max(scores, axis=1, keepdims=True))
        probs = weight * (1.0 / jnp.sum(weight, axis=1, keepdims=True))
        low = probs.astype(BF)
        grad_probs = dot_nt(gz[at, :], vr[:length, :])
        delta = jnp.sum(probs * grad_probs, axis=1, keepdims=True)
        grad_scores = (probs * (grad_probs - delta)).astype(BF)
        dk[:length, :] += dot_tn(grad_scores, kr[at, :])
        dv[:length, :] += dot_tn(low, vr[at, :])
        dq = (dot(grad_scores, kr[:length, :]) * scale).astype(BF)
        attended = dot(low, vr[:length, :]).astype(BF)
        for i in range(blocks):
            o_back[b + i, :, :LANES] = dq[i * count : (i + 1) * count]
            o_back[b + i, :, LANES:] = attended[i * count : (i + 1) * count]

    if seq_size <= 8:
        for b in range(0, seq_size, 2):
            queries(b, (b + 2) * count, 2)
    else:
        lax.fori_loop(0, seq_size, lambda b, _: (queries(b, rows, 1), 0)[1], 0)
    for d in range(seq_size):
        at = slice(d * count, (d + 1) * count)
        o_back[d, :, :LANES] = jnp.where(left, o_back[d, :, :LANES].astype(F32), dk[at, :] * scale).astype(BF)
        o_back[d, :, LANES:] = jnp.where(left, dv[at, :], o_back[d, :, LANES:].astype(F32)).astype(BF)


def backward_kernel(
    tiled, back, after, w_proj, w_qkv, n2, cot, w_out, gate, ssm, gated, normed,
    o_out, o_after, o_n2, o_gate, o_g, *o_more
):
    back = ready(back)
    seq_size, count = back.shape[0], back.shape[1]
    copies = seq_size // H
    left = lax.broadcasted_iota(jnp.int32, (count, LANES), 1) < HD
    dq, dk, dv, att = [], [], [], []
    for p in range(H // 2):
        a0, b0 = (back[2 * p * copies, :, tile(i)].astype(F32) for i in range(2))
        a1, b1 = (back[(2 * p + 1) * copies, :, tile(i)].astype(F32) for i in range(2))
        dq.append(jnp.where(left, a0, pltpu.roll(a1, HD, 1)))
        dk.append(jnp.where(left, pltpu.roll(a0, HD, 1), a1))
        dv.append(jnp.where(left, b0, pltpu.roll(b1, HD, 1)))
        att.append(jnp.where(left, pltpu.roll(b0, HD, 1), b1))
    attended = jnp.concatenate(att, axis=1).astype(BF)
    after, w_proj = ready(after, w_proj)
    width = after.shape[1]
    o_out[...] = (after[...] + dot(attended, w_proj[...])).astype(BF)
    sent(o_out)
    w_qkv, n2, cot = ready(w_qkv, n2, cot)
    grad_qkv = jnp.concatenate(dq + dk + dv, axis=1).astype(BF)
    if not tiled:
        o_more[0][...] = attended
        o_more[1][...] = grad_qkv
    grad_x, grad_gain = rms_back(after[...], n2[...], dot_nt(grad_qkv, w_qkv[...]))
    o_n2[...] = jnp.sum(grad_gain, axis=0, keepdims=True)
    grad_after = cot[...].astype(F32) + grad_x
    o_after[...] = grad_after
    branch = grad_after.astype(BF)
    if not tiled:
        o_more[2][...] = branch
    sent(o_n2, o_after)
    w_out, gate, ssm = ready(w_out, gate, ssm)
    inner_width = gate.shape[1]
    tiles = inner_width // LANES
    grad_gated = dot_nt(branch, w_out[...])
    for j in range(tiles):
        v = gate[:, tile(j)].astype(F32)
        sig = jax.nn.sigmoid(v)
        grad = grad_gated[:, tile(j)]
        to_rows(o_g, j, grad * (v * sig))
        grad_gate = grad * ssm[:, tile(j)] * (sig * (1.0 + v * (1.0 - sig)))
        o_gate[:, tile(j)] = grad_gate.astype(BF)
    sent(o_gate, o_g)
    gated, normed = ready(gated, normed)
    if tiled:
        partials(seq_size, gated, branch, normed, o_gate, attended, cot, *o_more)
        sent(*o_more[:2])


def leaving_kernel(g_ref, a_ref, bc, s_ref, o_msg):
    g_ref, a_ref, smem, s_ref = ready(g_ref, a_ref, bc, s_ref)
    count, states = smem.shape[0], a_ref.shape[0] // 8
    seq_size = o_msg.shape[0]

    def one(i, later):
        t = count - 1 - i
        s, g = block(s_ref, t), block(g_ref, t)
        return tuple(
            jnp.exp2(s * block(a_ref, n)) * (g * smem[t, states + n] + later[n])
            for n in range(states)
        )

    leaving = lax.fori_loop(0, count, one, (jnp.zeros((8, LANES), F32),) * states, unroll=4)
    for n in range(0, states, 2):
        value = jnp.concatenate([leaving[n], leaving[n + 1]], axis=0).astype(BF)
        for d in range(seq_size):
            o_msg[d, 8 * n : 8 * n + 16, :] = value


def states_kernel(
    seq_size, start, a_ref, bc, s_ref, dx_ref, inner, conv_w, conv_b, seg, o_every, o_slope, ext
):
    start, a_ref, smem, s_ref, dx_ref = ready(start, a_ref, bc, s_ref, dx_ref)
    count = smem.shape[0]
    states = a_ref.shape[0] // 8
    o_every[: states * 8, :] = start[...]

    def again(t, state):
        s, dx = block(s_ref, t), block(dx_ref, t)
        state = tuple(
            jnp.exp2(s * block(a_ref, n)) * state[n] + dx * smem[t, n] for n in range(states)
        )
        for n in range(states):
            o_every[pl.ds(pl.multiple_of(((t + 1) * states + n) * 8, 8), 8), :] = state[n]
        return state

    lax.fori_loop(0, count, again, tuple(start[8 * n : 8 * n + 8, :] for n in range(states)), unroll=2)
    sent(o_every)
    inner, conv_w, conv_b, seg = ready(inner, conv_w, conv_b, seg)
    ext[...] = inner[...].astype(F32)
    offset = offsets_in_sequence(seg, seq_size)
    for j in range(o_slope.shape[1] // LANES):
        pre = conv_tile(ext, conv_w, conv_b, offset, j, count)
        sig = jax.nn.sigmoid(pre)
        o_slope[:, tile(j)] = sig * (1.0 + pre * (1.0 - sig))


def fold8(values, sub):
    low4, low2, low1 = sub < 4, (sub & 2) == 0, (sub & 1) == 0
    four = []
    for k in range(4):
        a, b = values[k], values[k + 4]
        four.append(jnp.where(low4, a, b) + pltpu.roll(jnp.where(low4, b, a), 4, 0))
    two = []
    for k in range(2):
        a, b = four[k], four[k + 2]
        two.append(jnp.where(low2, a + pltpu.roll(a, 6, 0), b + pltpu.roll(b, 2, 0)))
    a, b = two
    return jnp.where(low1, a + pltpu.roll(a, 7, 0), b + pltpu.roll(b, 1, 0))


def adjoint_kernel(
    seq_size, back, totals, a_ref, bc, s_ref, dx_ref, g_ref, every, gs_ref, ai_ref, o_bc, o_a, held, sums, arrived
):
    back, totals, a_ref = ready(back, totals, a_ref)
    states = a_ref.shape[0] // 8
    count = s_ref.shape[0] // 8
    zero = jnp.zeros((8, LANES), F32)
    chunks = arrived.shape[0]
    span = count // chunks
    loads = []
    for c in range(chunks):
        first, last = c * span * states * 8, ((c + 1) * span + (c == chunks - 1)) * states * 8
        loads.append(pltpu.make_async_copy(every.at[first:last], held.at[first:last], arrived.at[c]))
    for load in reversed(loads):
        load.start()

    def join(i, carry):
        d = seq_size - 1 - i
        total = total_step(totals, d, 0)
        return tuple(
            jnp.exp2(block(a_ref, n) * total) * carry[n] + state_rows(back, d, n)
            for n in range(states)
        )

    leaving = lax.fori_loop(0, seq_size - 1 - lax.axis_index("seq"), join, (zero,) * states)
    smem, s_ref, dx_ref, g_ref = ready(bc, s_ref, dx_ref, g_ref)
    sub = lax.broadcasted_iota(jnp.int32, (8, LANES), 0)

    def one(last, i, carry):
        later, grad_a = carry
        t = last - i
        s, dx, g = block(s_ref, t), block(dx_ref, t), block(g_ref, t)
        new_later, new_grad_a, with_b, with_c = [], [], [], []
        grad_step, adjoint_in = zero, zero
        for n in range(states):
            a = block(a_ref, n)
            adjoint = g * smem[t, states + n] + later[n]
            passed = jnp.exp2(s * a) * adjoint
            before = held[pl.ds(pl.multiple_of((t * states + n) * 8, 8), 8), :]
            now = held[pl.ds(pl.multiple_of(((t + 1) * states + n) * 8, 8), 8), :]
            grad_decay = passed * before
            grad_step = grad_step + grad_decay * a
            adjoint_in = adjoint_in + adjoint * smem[t, n]
            new_later.append(passed)
            new_grad_a.append(grad_a[n] + grad_decay * s)
            with_b.append(adjoint * dx)
            with_c.append(g * now)
        here = pl.ds(pl.multiple_of(t * 8, 8), 8)
        gs_ref[here, :] = grad_step
        ai_ref[here, :] = adjoint_in
        for i, part in enumerate((with_b[:8], with_b[8:], with_c[:8], with_c[8:])):
            sums[pl.ds(pl.multiple_of(t * 32 + 8 * i, 8), 8), :] = fold8(part, sub)
        return tuple(new_later), tuple(new_grad_a)

    carry = (leaving, (zero,) * states)
    for c in reversed(range(chunks)):
        loads[c].wait()
        carry = lax.fori_loop(0, span, functools.partial(one, (c + 1) * span - 1), carry, unroll=4)
    grad_a = carry[1]
    sent(gs_ref, ai_ref)
    for n in range(states):
        o_a[8 * n : 8 * n + 8, :] = grad_a[n] * (LN2 * block(a_ref, n))
    columns = o_bc.shape[1]
    lane = lax.broadcasted_iota(jnp.int32, (LANES, columns), 1)
    grad_bc = jnp.zeros(o_bc.shape, F32)
    for q in range(2 * states):
        rows = sums[pl.ds(q, count, stride=2 * states), :]
        high = rows.astype(BF)
        low = (rows - high.astype(F32)).astype(BF)
        to_column = (lane == columns - 2 * states + q).astype(BF)
        grad_bc = grad_bc + dot(high, to_column) + dot(low, to_column)
    o_bc[...] = grad_bc


def inner_kernel(
    seq_size, gs_ref, ai_ref, g_ref, mixed, step_pre, low, w_dt, grad_bc, grad_a, w_xp, inner, slope, conv_w, d_skip,
    seg, normed, grad_n2,
    *rest,
):
    o_first, o_second, o_inner, *own_small, ext, gext, grad_w = rest
    small = own_small[0] if own_small else o_second.ref
    gs_ref, ai_ref, g_ref = ready(gs_ref, ai_ref, g_ref)
    grad_bc, grad_a = ready(grad_bc, grad_a)
    count = g_ref.shape[0] // 8
    states = grad_a.shape[0] // 8
    mixed, step_pre, low, w_dt, w_xp, inner = ready(mixed, step_pre, low, w_dt, w_xp, inner)
    slope, conv_w, d_skip, seg, normed, grad_n2 = ready(slope, conv_w, d_skip, seg, normed, grad_n2)
    inner_width = mixed.shape[1]
    tiles = inner_width // LANES
    rank = w_dt.shape[0]
    taps = conv_w.shape[0]
    small[...] = jnp.zeros_like(small)
    small[104 * 8 : (104 + states) * 8, :] = grad_a[...]
    offset = offsets_in_sequence(seg, seq_size)
    halves = []
    for j in range(tiles):
        mix = mixed[:, tile(j)].astype(F32)
        pre = step_pre[:, tile(j)]
        grad_step = LN2 * from_rows(gs_ref, j, count) + mix * from_rows(ai_ref, j, count)
        grad_pre = grad_step * jax.nn.sigmoid(pre)
        small[101 * 8 + j : 101 * 8 + j + 1, :] = jnp.sum(grad_pre, axis=0, keepdims=True)
        grad_ssm = from_rows(g_ref, j, count)
        small[102 * 8 + j : 102 * 8 + j + 1, :] = jnp.sum(grad_ssm * mix, axis=0, keepdims=True)
        halves.append(grad_pre.astype(BF))
    half = jnp.concatenate(halves, axis=1)
    grad_w_dt = dot_tn(low[...], half)
    padded_dt = jnp.concatenate([w_dt[...], jnp.zeros((2 * states, inner_width), BF)], axis=0)
    grad_selector = (dot_nt(half, padded_dt) + grad_bc[...]).astype(BF)
    grad_w_xp = dot_tn(grad_selector, mixed[...])
    from_selector = dot(grad_selector, w_xp[...])
    ext[...] = inner[...].astype(F32)
    gext[...] = jnp.zeros_like(gext)
    for j in range(tiles):
        to_rows(small.at[pl.ds(0, 64 * 8)], j, grad_w_xp[:, tile(j)])
        to_rows(small.at[pl.ds(64 * 8, 32 * 8)], j, grad_w_dt[:, tile(j)])
        grad_mixed = (
            softplus(step_pre[:, tile(j)]) * from_rows(ai_ref, j, count)
            + from_rows(g_ref, j, count) * d_skip[:, tile(j)]
            + from_selector[:, tile(j)]
        )
        grad_pre = grad_mixed * slope[:, tile(j)]
        small[100 * 8 + j : 100 * 8 + j + 1, :] = jnp.sum(grad_pre, axis=0, keepdims=True)
        for k in range(taps):
            shifted = pl.ds(HALO - taps + 1 + k, count)
            usable = jnp.where(offset >= taps - 1 - k, grad_pre, 0.0)
            row = (96 + k) * 8 + j
            small[row : row + 1, :] = jnp.sum(usable * ext[shifted, tile(j)], axis=0, keepdims=True)
            gext[shifted, tile(j)] += conv_w[k : k + 1, tile(j)] * usable
    o_inner[...] = gext[...].astype(BF)
    sent(o_inner)
    width = grad_n2.shape[1]
    for j in range(width // LANES):
        small[103 * 8 + 4 + j : 103 * 8 + 5 + j, :] = grad_n2[:, tile(j)]
    if not own_small:
        o_first[...] = dot_tn(normed[...], o_inner[...])
        return
    grad_w[...] = dot_tn(normed[...], o_inner[...])
    for to, x, s, at in receivers((o_first, o_second), seq_size):
        to[x * seq_size + s, :LANES, :] = grad_w[pl.ds(pl.multiple_of(at * LANES, LANES), LANES), tile(s)].astype(BF)
        rows = small.shape[0] // (width // LANES * seq_size)
        here = pl.ds(pl.multiple_of((at * seq_size + s) * rows, rows), rows)
        to[x * seq_size + s, LANES:, :] = small[here, :].astype(BF)


def receivers(results, seq_size, mine=0):
    core = lax.rem(lax.axis_index("dp"), 2)
    for to, side in zip(results, (core, 1 - core)):
        for x in range(to.shape[0] // seq_size):
            for s in range(seq_size):
                yield to, x, s, 2 * lax.bitwise_xor(x, mine) + side


def partials(seq_size, gated, branch, normed, grad_gate, attended, cot, keep, send, out, gate, proj):
    out[...] = dot_tn(gated[...], branch)
    gate[...] = dot_tn(normed[...], grad_gate[...])
    proj[...] = dot_tn(attended, cot[...])
    across = out.shape[1] // LANES
    down = seq_size // across
    mine = lax.axis_index("dp") // 2
    for to, x, s, at in receivers((keep, send), seq_size, mine):
        rows = pl.ds(pl.multiple_of((at * down + s // across) * LANES, LANES), LANES)
        to[x * seq_size + s, :LANES, :] = out[rows, tile(s % across)].astype(BF)
        rows = pl.ds(pl.multiple_of(at * LANES, LANES), LANES)
        to[x * seq_size + s, LANES : 2 * LANES, :] = gate[rows, tile(s)].astype(BF)
        rows = pl.ds(pl.multiple_of((at * down + s // across) * HD, HD), HD)
        to[x * seq_size + s, 2 * LANES :, :] = proj[rows, tile(s % across)].astype(BF)


def tokens_kernel(grad_inner, w_in, grad_gate, tok, halo, n1, grad_after, o_tok, o_halo, o_n1):
    grad_inner, w_in, grad_gate = ready(grad_inner, w_in, grad_gate)
    inner_width = grad_inner.shape[1]
    grad_normed = dot_nt(grad_inner[...], w_in[:, :inner_width])
    own = dot_nt(grad_gate[...], w_in[:, inner_width:])
    grad_normed = jnp.concatenate([grad_normed[:HALO], grad_normed[HALO:] + own], axis=0)
    tok, halo, n1, grad_after = ready(tok, halo, n1, grad_after)
    x = jnp.concatenate([halo[...], tok[...]], axis=0).astype(F32)
    grad_x, grad_gain = rms_back(x, n1[...], grad_normed)
    o_tok[...] = grad_after[...] + grad_x[HALO:]
    o_halo[...] = grad_x[HALO - 8 : HALO]
    grad_gain = jnp.sum(grad_gain, axis=0, keepdims=True)
    tiles = grad_gain.shape[1] // LANES
    rows = [grad_gain[:, tile(j)] for j in range(tiles)] + [jnp.zeros((16 - tiles, LANES), F32)]
    o_n1[...] = jnp.concatenate(rows, axis=0).astype(BF)


def head_products_kernel(normed, back, *rest):
    *outs, pieces = rest
    normed, back = ready(normed, back)
    both = back[...].reshape(back.shape[0] * back.shape[1], 2 * LANES)
    grad = dot_tn(both, normed[...])
    left = lax.broadcasted_iota(jnp.int32, (HD, LANES), 1) < HD
    for g in range(len(outs)):
        pieces[g, : 2 * HD, :] = jnp.transpose(grad[:LANES, tile(g)])
        value = jnp.transpose(grad[LANES:, tile(g)])
        pieces[g, 2 * HD :, :] = jnp.where(left, value[:HD], pltpu.roll(value[HD:], HD, 1))
    for distance, to in enumerate(outs):
        to[...] = pieces[lax.bitwise_xor(lax.axis_index("dp"), distance)].astype(BF)


def early_sum_kernel(parts, *heads):
    *heads, o_sum = heads
    heads, parts = ready(*heads), ready(parts)
    head = heads[0][...].astype(F32)
    for part in heads[1:]:
        head = head + part[...].astype(F32)
    total = parts[0].astype(F32)
    for d in range(1, parts.shape[0]):
        total = total + parts[d].astype(F32)
    rows = total.shape[0]
    o_sum[:rows, :] = total.astype(BF)
    o_sum[rows:, :] = head.astype(BF)


def sum_and_spread_kernel(parts, own, o_all):
    parts, own = ready(parts, own)
    total = parts[0].astype(F32)
    for d in range(1, parts.shape[0]):
        total = total + parts[d].astype(F32)
    total = total.astype(BF)
    rows = total.shape[0]
    for d in range(o_all.shape[0]):
        o_all[d, :rows, :] = total
        o_all[d, rows:, :] = own[...]


def early_assembly_kernel(groups, early, w_in, o_out, o_proj, o_qkv, o_in, pieces, out, proj, qkv, gate, loads, stores):
    seq_size = early.shape[0] // groups
    inner_width, width = gate.shape[1], proj.shape[1]
    across = width // LANES
    left = lax.broadcasted_iota(jnp.int32, (LANES, LANES), 1) < HD
    at = 2 * LANES + HD

    def pairs(a, b):
        a, b = a.astype(F32), b.astype(F32)
        mask = left[: a.shape[0]]
        return jnp.where(mask, a, pltpu.roll(b, HD, 1)), jnp.where(mask, pltpu.roll(a, HD, 1), b)

    own = [slice(g * seq_size, (g + 1) * seq_size) for g in range(groups)]
    arrivals = [pltpu.make_async_copy(early.at[own[g]], pieces.at[own[g]], loads.at[g]) for g in range(groups)]
    for copy in arrivals:
        copy.start()
    copies = []
    for g in range(groups):
        arrivals[g].wait()
        down = seq_size // across
        for s in range(seq_size):
            piece = pieces[g * seq_size + s]
            row = g * down + s // across
            out[tile(row), tile(s % across)] = piece[:LANES].astype(F32)
            gate[tile(g), tile(s)] = piece[LANES : 2 * LANES].astype(F32)
            proj[row * HD : (row + 1) * HD, tile(s % across)] = piece[2 * LANES : at].astype(F32)
        for p in range(seq_size // 2):
            a, b = pieces[g * seq_size + 2 * p], pieces[g * seq_size + 2 * p + 1]
            first, second, third = (slice(i * width + p * LANES, i * width + (p + 1) * LANES) for i in range(3))
            qkv[tile(g), first], qkv[tile(g), second] = pairs(a[at : at + LANES], b[at : at + LANES])
            low, high = pairs(a[at + LANES :], b[at + LANES :])
            qkv[g * LANES : g * LANES + HD, third] = low
            qkv[g * LANES + HD : (g + 1) * LANES, third] = high
        for i, (source, target, rows) in enumerate(
            ((out, o_out, down * LANES), (proj, o_proj, down * HD), (qkv, o_qkv, LANES), (gate, o_in, LANES))
        ):
            here = slice(g * rows, (g + 1) * rows)
            target = target.at[here, inner_width:] if i == 3 else target.at[here]
            copies.append(pltpu.make_async_copy(source.at[here], target, stores.at[4 * g + i]))
            copies[-1].start()
    for copy in copies:
        copy.wait()


def late_assembly_kernel(
    groups, mine, other, o_in, o_n1, o_conv_w, o_conv_b, o_xp, o_dt, o_dtb, o_a, o_skip, o_n2, inner, small, sems
):
    mine, other = ready(mine, other)
    seq_size = mine.shape[0] * 2 // groups
    width, inner_width = inner.shape
    rows = mine.shape[1] - LANES - 16
    copies = []
    for ref, x, s, g in receivers((mine, other), seq_size):
        at = pl.ds(pl.multiple_of(g * LANES, LANES), LANES)
        inner[at, tile(s)] = ref[x * seq_size + s, :LANES, :].astype(F32)
        here = pl.ds(pl.multiple_of((g * seq_size + s) * rows, rows), rows)
        small[here, :] = ref[x * seq_size + s, LANES : LANES + rows, :].astype(F32)
        if s == seq_size - 1:
            copies.append(pltpu.make_async_copy(inner.at[at], o_in.at[at, :inner_width], sems.at[len(copies)]))
            copies[-1].start()
    for j in range(inner_width // LANES):
        value = from_rows(small, j, SMALL)
        for ref, first, last in (
            (o_xp, 0, 64), (o_dt, 64, 96), (o_conv_w, 96, 100), (o_conv_b, 100, 101), (o_dtb, 101, 102),
            (o_skip, 102, 103), (o_a, 104, 120),
        ):
            ref[:, tile(j)] = value[first:last]
        if j >= width // LANES:
            o_n2[:, tile(j - width // LANES)] = value[103:104]
    sent(o_conv_w, o_conv_b, o_xp, o_dt, o_dtb, o_a, o_skip, o_n2)
    gain = jnp.zeros((16, LANES), F32)
    for source in (mine, other):
        for d in range(source.shape[0]):
            gain = gain + source[d, LANES + rows :, :].astype(F32)
    for j in range(width // LANES):
        o_n1[:, tile(j)] = gain[j : j + 1]
    for copy in copies:
        copy.wait()


class Held:
    def __init__(self, buffer, copy):
        self.ref, self.copy, self.shape = buffer, copy, buffer.shape
        self.done = False

    def __getitem__(self, at):
        return self.ref[at]

    def __setitem__(self, at, value):
        self.ref[at] = value


def ready(*held):
    for one in held:
        if not one.done:
            one.copy.wait()
            one.done = True
    refs = tuple(one.ref for one in held)
    return refs[0] if len(refs) == 1 else refs


def sent(*held):
    for one in held:
        if not one.done:
            one.copy.start()
            one.done = True


IN_HBM = pl.BlockSpec(memory_space=pltpu.HBM)


def call(
    kernel, outs, scratch, *args, name=None, us=1, raw=(), raw_out=(), scalars=(), views=None, aliases=None, after=(),
    near=(), vmem=60,
):
    views = views or {}
    count, first_out = len(args), len(args) + len(after)
    first_scratch = first_out + len(outs)
    buffers = []
    for i, arg in enumerate(args):
        shape = jax.eval_shape(lambda v, i=i: v[views[i]], arg).shape if i in views else arg.shape
        kind = pltpu.SMEM if i in scalars else pltpu.VMEM
        buffers.append(None if i in raw else kind(shape, arg.dtype))
    for i, (shape, dtype) in enumerate(outs):
        buffers.append(None if i in raw_out else pltpu.VMEM(shape, dtype))
    used = [b for b in buffers if b is not None]

    def run(*refs):
        given = list(refs[:count]) + list(refs[first_out:first_scratch])
        own = list(refs[first_scratch : first_scratch + len(used)])
        sems = refs[first_scratch + len(used)]
        passed = []
        for i, (ref, buffer) in enumerate(zip(given, buffers)):
            if buffer is None:
                passed.append(ref)
                continue
            buffer = own.pop(0)
            if i < count:
                source = ref.at[views[i]] if i in views else ref
                copy = pltpu.make_async_copy(source, buffer, sems.at[i])
                copy.start()
            else:
                copy = pltpu.make_async_copy(buffer, ref, sems.at[i])
            passed.append(Held(buffer, copy))
        kernel(*passed, *refs[first_scratch + len(used) + 1 :])
        ready(*[p for p in passed[:count] if isinstance(p, Held)])
        results = [p for p in passed[count:] if isinstance(p, Held)]
        sent(*results)
        for result in results:
            result.copy.wait()

    return pl.pallas_call(
        run,
        out_shape=[jax.ShapeDtypeStruct(s, d) for s, d in outs],
        in_specs=[pl.BlockSpec(memory_space=pl.ANY) if i in near else IN_HBM for i in range(first_out)],
        out_specs=[IN_HBM] * len(outs),
        scratch_shapes=used + [pltpu.SemaphoreType.DMA((len(buffers),))] + scratch,
        compiler_params=pltpu.CompilerParams(vmem_limit_bytes=vmem * 1024 * 1024),
        cost_estimate=pl.CostEstimate(flops=us * 10**9 + 1000, bytes_accessed=1000, transcendentals=0),
        input_output_aliases=aliases or {},
        name=name,
    )(*args, *after)


def exchange(value, axes):
    return lax.all_to_all(value, axes, 0, 0, tiled=True)


def own_core(value, groups, seq_size):
    peers = [
        [g * seq_size + s for g in range(core, groups, 2) for s in range(seq_size)] for core in range(2)
    ]
    return lax.all_to_all(value, ("dp", "seq"), 0, 0, tiled=True, axis_index_groups=peers)


def other_core(value, groups):
    return lax.ppermute(value, "dp", [(g, g ^ 1) for g in range(groups)])


def body(
    tokens, seg_start, norm_one, w_in, conv_w, conv_b, w_xproj, w_dt, dt_bias, a_log, d_skip,
    w_out, norm_two, w_qkv, w_proj, cotangent,
):
    count, width = tokens.shape
    inner_width = w_in.shape[1] // 2
    states = a_log.shape[1]
    rank = w_dt.shape[0]
    taps = conv_w.shape[0]
    groups, seq_size = lax.axis_size("dp"), lax.axis_size("seq")
    rows = count * seq_size
    ext_rows = HALO + count
    tiled = inner_width == seq_size * LANES and width == groups * LANES and seq_size == H
    peers = groups // 2 * seq_size
    line = lambda v: v.reshape(1, -1)
    seg = line(seg_start)
    n1, n2, cb, dtb, skip = (line(v) for v in (norm_one, norm_two, conv_b, dt_bias, d_skip))
    vmem, smem = pltpu.VMEM, pltpu.SMEM((count, 2 * states), F32)
    sem = pltpu.SemaphoreType.DMA
    blocks = ((count * 8, LANES), F32)
    ends_at = states * 8
    halo = lax.ppermute(tokens[count - HALO :], "seq", [(i, i + 1) for i in range(seq_size - 1)])
    msg, normed, inner, gate, mixed, bc, low, step_pre, s, dx, a = call(
        functools.partial(forward_kernel, seq_size),
        [
            ((seq_size, states * 8 + 32, LANES), BF), ((ext_rows, width), BF),
            ((ext_rows, inner_width), BF), ((count, inner_width), BF), ((count, inner_width), BF), ((count, 2 * states), F32),
            ((count, rank), BF), ((count, inner_width), F32), blocks, blocks, ((states * 8, LANES), F32),
        ],
        [vmem((ext_rows, inner_width), F32), smem, sem],
        tokens, halo, n1, w_in, conv_w, cb, w_xproj.T, w_dt, dtb, a_log.T, seg,
        name="forward", us=0, near=(1,),
    )
    msg = exchange(msg, "seq")
    qkvg, start, ssm, after, gated, normed_two = call(
        middle_kernel,
        [
            ((seq_size, count, 2 * LANES), BF), ((states * 8, LANES), F32), ((count, inner_width), F32),
            ((count, width), F32), ((count, inner_width), BF), ((count, width), BF),
        ],
        [vmem(*blocks)],
        msg, a, bc, s, dx, mixed, gate, skip, tokens, w_out, n2, w_qkv, cotangent, w_proj,
        name="middle", us=0, scalars=(2,), views={0: np.s_[:, : ends_at + 16, :]}, near=(0,),
    )
    qkvg = exchange(qkvg, "seq")
    every, slope = call(
        functools.partial(states_kernel, seq_size),
        [(((count + 1) * states * 8, LANES), F32), ((count, inner_width), F32)],
        [vmem((ext_rows, inner_width), F32)],
        start, a, bc, s, dx, inner, conv_w, cb, seg, name="states", us=0, scalars=(2,),
    )
    (back,) = call(
        attention_kernel,
        [((seq_size, count, 2 * LANES), BF)],
        [vmem((rows, LANES), BF)] * 4 + [vmem((rows, LANES), F32)] * 2,
        qkvg, msg, name="attention", us=0, views={1: np.s_[:, ends_at + 16 :, :]},  near=(0,),
    )
    back_own = exchange(back, "seq")
    pieces = [((peers, 2 * LANES + HD, LANES), BF)] * 2
    rest = [((count, width), BF), ((count, 3 * width), BF), ((count, width), BF)]
    out, grad_after, grad_n2, grad_gate, g, *more = call(
        functools.partial(backward_kernel, tiled),
        [
            ((count, width), BF), ((count, width), F32), ((1, width), F32), ((count, inner_width), BF), blocks,
        ] + (pieces if tiled else rest),
        [vmem((inner_width, width), F32), vmem((width, inner_width), F32), vmem((width, width), F32)] if tiled else [],
        back_own, after, w_proj, w_qkv, n2, cotangent, w_out, gate, ssm, gated, normed,
        name="backward", us=0, views={10: np.s_[HALO:, :]}, near=(0,),
    )
    (adj,) = call(
        leaving_kernel, [((seq_size, states * 8, LANES), BF)], [], g, a, bc, s, name="leaving", us=0, scalars=(2,)
    )
    adj = exchange(adj, "seq")
    between = ()
    if tiled:
        normed_two_all = lax.all_gather(normed_two, "seq", axis=0, tiled=True)
        keep, send = more
        add = lambda *parts: sum(part.astype(F32) for part in parts).astype(BF)
        received = other_core(send, groups)
        across = add(keep[seq_size:], received[seq_size:])
        across = lax.ppermute(across, "dp", [(g, g ^ 2) for g in range(groups)])
        across, slope = lax.optimization_barrier((across, slope))
        part = add(keep[:seq_size], received[:seq_size], across)
        between = (part,)
        part = exchange(part, "seq")
    gs, ai, grad_bc, grad_a = call(
        functools.partial(adjoint_kernel, seq_size),
        [blocks, blocks, ((count, rank + 2 * states), F32), ((states * 8, LANES), F32)],
        [vmem(((count + 1) * states * 8, LANES), F32), vmem((count * 2 * states, LANES), F32), sem((8,))],
        adj, msg, a, bc, s, dx, g, every, name="adjoint", us=0, raw=(7,), scalars=(3,), near=(0,),
        views={1: np.s_[:, ends_at : ends_at + 16, :]}, after=between,
    )
    small_rows = SMALL * 8 // (groups * seq_size)
    *sums, small, grad_inner = call(
        functools.partial(inner_kernel, seq_size),
        ([((peers, LANES + small_rows, LANES), BF)] * 2 if tiled else [((width, inner_width), F32), ((SMALL * 8, LANES), F32)])
        + [((ext_rows, inner_width), BF)],
        ([vmem((SMALL * 8, LANES), F32)] if tiled else [])
        + [vmem((ext_rows, inner_width), F32), vmem((ext_rows, inner_width), F32), vmem((width, inner_width), F32)],
        gs, ai, g, mixed, step_pre, low, w_dt, grad_bc, grad_a, w_xproj.T, inner, slope, conv_w, skip, seg, normed, grad_n2,
        name="inner", us=0,
    )
    grad_tokens, grad_halo, grad_n1 = call(
        tokens_kernel, [((count, width), F32), ((8, width), F32), ((16, LANES), BF)], [],
        grad_inner, w_in, grad_gate, tokens, halo, n1, grad_after, name="tokens", us=0,
    )
    returned = lax.ppermute(grad_halo, "seq", [(i + 1, i) for i in range(seq_size - 1)])
    grad_tokens = grad_tokens.at[count - 8 :].add(returned)
    flat = lambda v: v.reshape(-1)
    if tiled:
        head, *heads = call(
            head_products_kernel, [((3 * HD, LANES), BF)] * groups, [vmem((groups, 3 * HD, LANES), F32)],
            normed_two_all, back, name="head_products", us=0, after=(grad_inner,),
        )
        heads = [
            lax.ppermute(piece, "dp", [(g, g ^ distance) for g in range(groups)])
            for distance, piece in enumerate(heads, 1)
        ]
        (early,) = call(
            early_sum_kernel, [((part.shape[1] + head.shape[0], LANES), BF)], [], part, head, *heads,
            name="early_sum", us=0, vmem=40, near=(0, 2, 3, 4),
        )
        late = add(sums[0], other_core(small, groups))
        late, early = lax.optimization_barrier((late, early))
        late = own_core(late, groups, seq_size)
        early = lax.all_gather(early, ("dp", "seq"))
        (late,) = call(
            sum_and_spread_kernel, [((peers, late.shape[1] + 16, LANES), BF)], [], late, grad_n1, name="late_sum", us=0, vmem=40,
            near=(0,),
        )
        mine = own_core(late, groups, seq_size)
        mine, grad_tokens = lax.optimization_barrier((mine, grad_tokens))
        row = lambda n: ((n, inner_width), F32)
        half, g_n1, g_conv_w, g_conv_b, g_xp, g_dt, g_dtb, g_a, g_skip, g_n2 = call(
            functools.partial(late_assembly_kernel, groups),
            [
                ((width, 2 * inner_width), F32), ((1, width), F32), row(taps), row(1), row(2 * states + rank), row(rank),
                row(1), row(states), row(1), ((1, width), F32),
            ],
            [vmem((width, inner_width), F32), vmem((SMALL * 8, LANES), F32), sem((4,))],
            mine, other_core(mine, groups), name="late_assembly", us=0, vmem=40, raw_out=(0,), near=(0, 1),
        )
        whole = [((inner_width, width), F32), ((width, width), F32), ((width, 3 * width), F32)]
        grad_w_out, grad_w_proj, grad_w_qkv, grad_w_in = call(
            functools.partial(early_assembly_kernel, groups),
            whole + [((width, 2 * inner_width), F32)],
            [vmem(early.shape, BF)] + [vmem(*v) for v in whole] + [vmem((width, inner_width), F32), sem((4,)), sem((16,))],
            early, half, name="early_assembly", us=0, raw=(0, 1), raw_out=(0, 1, 2, 3), aliases={1: 3},
        )
        g_xp, g_a, g_n1, g_n2 = g_xp.T, g_a.T, flat(g_n1), flat(g_n2)
    else:
        attended, grad_qkv, branch = more
        small = small.reshape(SMALL, inner_width)
        g_n1 = flat(grad_n1[: width // LANES].astype(F32))
        both = jnp.concatenate([sums[0], dot_tn(normed[HALO:], grad_gate)], axis=1)
        grad_w_in, grad_w_out, grad_w_qkv, grad_w_proj, small, g_n1 = lax.psum(
            (both, dot_tn(gated, branch), dot_tn(normed_two, grad_qkv), dot_tn(attended, cotangent), small, g_n1), ("dp", "seq")
        )
        g_xp, g_dt, g_conv_w, g_conv_b, g_dtb = small[:64].T, small[64:96], small[96:100], small[100], small[101]
        g_skip, g_n2, g_a = small[102], small[103, width:], small[104:120].T
    return (out, grad_tokens, g_n1, grad_w_in, g_conv_w, flat(g_conv_b), g_xp, g_dt, flat(g_dtb), g_a, flat(g_skip),
            grad_w_out, g_n2, grad_w_qkv, grad_w_proj)


def solution(mesh):
    split, copied = P(("dp", "seq"), None), P()
    return jax.shard_map(
        body,
        mesh=mesh,
        in_specs=(split, P(("dp", "seq"))) + (copied,) * 13 + (split,),
        out_specs=(split, split) + (copied,) * 13,
        check_vma=False,
    )
```
